32 devices in a mesh: rep: 4 (over z), shard: 8 (over y, x, core).
Axes of the slice: x: 2, y: 2, z: 4, core: 2. Of those that a mesh axis runs over, the one named last changes fastest.
Arguments:
- tokens: bfloat16 [32768, 768], P(('rep', 'shard')), may hold values from -6 to 6
- word_counts: int32 [256], P(('rep', 'shard')), may hold values from 2 to 60
- region_counts: int32 [256], P(('rep', 'shard')), may hold values from 36 to 68
- task_labels: int32 [256], P(('rep', 'shard')), may hold values from 0 to 2
- masked_slots: int32 [256, 128], P(('rep', 'shard')), may hold values 0 or 1
- qkv_weight: bfloat16 [768, 2304], P('shard'), may hold values from -0.3125 to 0.3125
- query_bias: bfloat16 [768], P('shard'), may hold values from -3 to 3
- value_bias: bfloat16 [768], P('shard'), may hold values from -3 to 3
- out_weight: bfloat16 [768, 768], P('shard'), may hold values from -0.875 to 0.875
- out_bias: bfloat16 [768], P('shard'), may hold values from -3 to 3
- attn_gain: bfloat16 [768], P('shard'), may hold values from 0.5 to 1.5
- attn_shift: bfloat16 [768], P('shard'), may hold values from -3 to 3
- inner_weight: bfloat16 [768, 3072], P('shard'), may hold values from -0.21875 to 0.21875
- inner_bias: bfloat16 [3072], P('shard'), may hold values from -3 to 3
- back_weight: bfloat16 [3072, 768], P('shard'), may hold values from -0.109375 to 0.109375
- back_bias: bfloat16 [768], P('shard'), may hold values from -3 to 3
- ffn_gain: bfloat16 [768], P('shard'), may hold values from 0.5 to 1.5
- ffn_shift: bfloat16 [768], P('shard'), may hold values from -3 to 3
- cotangent: bfloat16 [32768, 768], P(('rep', 'shard')), may hold values from -6 to 6
Outputs:
- result: bfloat16 [32768, 768], P(('rep', 'shard'))
- input_grad: float32 [32768, 768], P(('rep', 'shard'))
- grad_qkv: float32 [768, 2304], P('shard')
- grad_query: float32 [768], P('shard')
- grad_value: float32 [768], P('shard')
- grad_proj: float32 [768, 768], P('shard')
- grad_pbias: float32 [768], P('shard')
- grad_again: float32 [768], P('shard')
- grad_ashift: float32 [768], P('shard')
- grad_inner: float32 [768, 3072], P('shard')
- grad_ibias: float32 [3072], P('shard')
- grad_back: float32 [3072, 768], P('shard')
- grad_bbias: float32 [768], P('shard')
- grad_fgain: float32 [768], P('shard')
- grad_fshift: float32 [768], P('shard')
The draws below stay inside these ranges and needn't reach their ends.
All inputs are finite; a program needn't handle non-finite values. No bound on the sum of `masked_slots` on one device may be relied on, other than what follows from the above.
Results may differ from the reference program's by a relative error of at most 0.02.
Values may be sent and summed in bfloat16 or wider, within the bound.
No kernel may reach another device: no remote copies, remote signals or barrier semaphores. Data moves between devices by JAX's collectives and lax.ppermute only.
A program may use at most 192 MiB of HBM per device.

```python
import jax
import jax.numpy as jnp
from jax import lax

D = 768
HEADS = 12
HEAD_DIM = 64
FF = 3072
WORD_SLOTS = 60
REGION_SLOTS = 68
SEQ = 128
PAIRS = 256
TOKENS = 32768


def with_ends(values, own_key, least, top_value):
    longest = values.shape.index(max(values.shape))
    spots = []
    for shift in (0, 1):
        where = [jax.random.randint(jax.random.fold_in(own_key, axis), (), 0, length) for axis, length in enumerate(values.shape)]
        where[longest] = (where[longest] + shift) % values.shape[longest]
        spots.append(tuple(where))
    return values.at[spots[0]].set(least).at[spots[1]].set(top_value)


def block_levels(key, dims, cuts, low, high):
    def one(dim, shards_of):
        steps = jax.random.uniform(jax.random.fold_in(jax.random.fold_in(key, 6), dim), (shards_of,), jnp.float32, low / len(cuts), high / len(cuts))
        return jnp.repeat(jnp.exp(steps), dims[dim] // shards_of).reshape((-1,) + (1,) * (len(dims) - dim - 1))

    level = one(*cuts[0])
    for cut in cuts[1:]:
        level = level * one(*cut)
    return level


def scatter_about(rng, dims, deviation, bound, cuts=(), kind=jnp.bfloat16):
    array = jax.random.normal(rng, dims, jnp.float32) * deviation
    if len(cuts) > 0:
        array = block_levels(rng, dims, cuts, -0.22, 0.18) * array
    return jnp.clip(array, min=-bound, max=bound).astype(kind)


def setup_inputs(seed: int = 0) -> dict:
    splits = jax.random.split(jax.random.key(seed), 20)
    tokens = scatter_about(splits[0], (TOKENS, D), 1.0, 6.0, ((0, 32),))
    word_counts = with_ends(jax.random.randint(splits[1], (PAIRS,), 2, WORD_SLOTS + 1), jax.random.fold_in(splits[1], 1), 2, WORD_SLOTS).astype(jnp.int32)
    region_counts = with_ends(jax.random.randint(splits[2], (PAIRS,), REGION_SLOTS // 2 + 2, REGION_SLOTS + 1), jax.random.fold_in(splits[2], 1), REGION_SLOTS // 2 + 2, REGION_SLOTS).astype(jnp.int32)
    task_labels = with_ends(jax.random.randint(splits[3], (PAIRS,), 0, 3), jax.random.fold_in(splits[3], 1), 0, 2).astype(jnp.int32)
    masked_slots = with_ends((jax.random.randint(splits[4], (PAIRS, SEQ), 0, 20) < 3).astype(jnp.int32), jax.random.fold_in(splits[4], 1), 0, 1)
    qkv_weight = scatter_about(splits[5], (D, 3 * D), (D // 2) ** -0.5, 0.3125, ((0, 8),))
    query_bias = scatter_about(splits[6], (D,), 0.5, 3.0, ((0, 8),))
    value_bias = scatter_about(splits[7], (D,), 0.5, 3.0, ((0, 8),))
    out_weight = scatter_about(splits[8], (D, D), (D // 16) ** -0.5, 0.875, ((0, 8),))
    out_bias = scatter_about(splits[9], (D,), 0.5, 3.0, ((0, 8),))
    attn_gain = jnp.clip(0.5 + 1.0 * jax.random.uniform(splits[10], (D,), jnp.float32) ** block_levels(splits[10], (D,), ((0, 8),), -0.2, 0.2), 0.5, 1.5).astype(jnp.bfloat16)
    attn_shift = scatter_about(splits[11], (D,), 0.5, 3.0, ((0, 8),))
    inner_weight = scatter_about(splits[12], (D, FF), D ** -0.5, 0.21875, ((0, 8),))
    inner_bias = scatter_about(splits[13], (FF,), 0.5, 3.0, ((0, 8),))
    back_weight = scatter_about(splits[14], (FF, D), FF ** -0.5, 0.109375, ((0, 8),))
    back_bias = scatter_about(splits[15], (D,), 0.5, 3.0, ((0, 8),))
    ffn_gain = jnp.clip(0.5 + 1.0 * jax.random.uniform(splits[16], (D,), jnp.float32) ** block_levels(splits[16], (D,), ((0, 8),), -0.2, 0.2), 0.5, 1.5).astype(jnp.bfloat16)
    ffn_shift = scatter_about(splits[17], (D,), 0.5, 3.0, ((0, 8),))
    cotangent = scatter_about(splits[18], (TOKENS, D), 1.0, 6.0, ((0, 32),))
    return dict(tokens=tokens, word_counts=word_counts, region_counts=region_counts, task_labels=task_labels, masked_slots=masked_slots, qkv_weight=qkv_weight, query_bias=query_bias, value_bias=value_bias, out_weight=out_weight, out_bias=out_bias, attn_gain=attn_gain, attn_shift=attn_shift, inner_weight=inner_weight, inner_bias=inner_bias, back_weight=back_weight, back_bias=back_bias, ffn_gain=ffn_gain, ffn_shift=ffn_shift, cotangent=cotangent)


@jax.custom_vjp
def low(v):
    return lax.optimization_barrier(v.astype(jnp.bfloat16)).astype(jnp.float32)

@jax.custom_vjp
def low_back(v):
    return v

def low_keep(v):
    return (low(v), None)

def low_pass(kept, grad):
    return (grad,)

def back_keep(v):
    return (v, None)

def back_low(kept, grad):
    return (low(grad),)
low.defvjp(low_keep, low_pass)
low_back.defvjp(back_keep, back_low)

def matmul(left, right):
    return jnp.dot(left, right, precision=lax.Precision.HIGHEST, preferred_element_type=jnp.float32)

def layer_norm(value, gain, shift):
    mean = lax.optimization_barrier(jnp.mean(value, -1, keepdims=True))
    centred = value - mean
    var = lax.optimization_barrier(jnp.mean(centred * centred, -1, keepdims=True))
    return centred * lax.rsqrt(var + 1e-05) * gain + shift

def forward(xs, params, valid):
    qkv_weight, query_bias, value_bias, out_weight, out_bias, attn_gain, attn_shift, inner_weight, inner_bias, back_weight, back_bias, ffn_gain, ffn_shift = params
    group = xs.shape[0]
    rows = xs.reshape(-1, D)
    bias = jnp.concatenate([query_bias, jnp.zeros_like(query_bias), value_bias])
    qkv = low(low_back(matmul(rows, qkv_weight) + bias))
    queries = qkv[:, :D].reshape(group, SEQ, HEADS, HEAD_DIM)
    keys = qkv[:, D:2 * D].reshape(group, SEQ, HEADS, HEAD_DIM)
    values = qkv[:, 2 * D:].reshape(group, SEQ, HEADS, HEAD_DIM)
    scores = jnp.einsum('pqhe,pkhe->phqk', queries, keys, precision=lax.Precision.HIGHEST) * HEAD_DIM ** (-0.5)
    scores = low_back(jnp.where(valid[:, None, None, :], scores, -1000000000.0))
    probs = jax.nn.softmax(scores, axis=-1)
    mixed = jnp.einsum('phqk,pkhe->pqhe', low(probs), values, precision=lax.Precision.HIGHEST).reshape(-1, D)
    mixed = low(low_back(mixed))
    branch = low_back(matmul(mixed, out_weight) + out_bias)
    hidden1 = layer_norm(rows + branch, attn_gain, attn_shift)
    inner = low_back(matmul(low(hidden1), inner_weight) + inner_bias)
    act = low(jax.nn.gelu(inner, approximate=False))
    second = low_back(matmul(act, back_weight) + back_bias)
    return layer_norm(hidden1 + second, ffn_gain, ffn_shift)

def reference(tokens, word_counts, region_counts, task_labels, masked_slots, qkv_weight, query_bias, value_bias, out_weight, out_bias, attn_gain, attn_shift, inner_weight, inner_bias, back_weight, back_bias, ffn_gain, ffn_shift, cotangent):
    slots = jnp.arange(SEQ, dtype=jnp.int32)[None, :]
    words = word_counts[:, None]
    in_regions = (slots >= WORD_SLOTS) & (slots < WORD_SLOTS + region_counts[:, None])
    valid = (slots < words) | in_regions
    picked = masked_slots == 1
    labels = task_labels[:, None]
    live = (labels == 0) & picked & (slots >= 1) & (slots < words) | (labels == 1) & picked & in_regions | (labels == 2) & (slots == 0)
    row_weight = live.astype(jnp.float32).reshape(-1, 1)
    params = tuple((w.astype(jnp.float32) for w in (qkv_weight, query_bias, value_bias, out_weight, out_bias, attn_gain, attn_shift, inner_weight, inner_bias, back_weight, back_bias, ffn_gain, ffn_shift)))
    group_pairs = 32
    rounds = PAIRS // group_pairs
    xs_all = tokens.astype(jnp.float32).reshape(rounds, group_pairs, SEQ, D)
    ct_all = (cotangent.astype(jnp.float32) * row_weight).reshape(rounds, group_pairs * SEQ, D)
    valid_all = valid.reshape(rounds, group_pairs, SEQ)

    def step(totals, items):
        xs, valid_now, ct_now = items

        def local(xin, *weights):
            return forward(xin, weights, valid_now)
        output, pull = jax.vjp(local, xs, *params)
        grads = pull(ct_now)
        totals = tuple((a + g for a, g in zip(totals, grads[1:])))
        return (totals, (output.astype(jnp.bfloat16), grads[0].reshape(-1, D)))
    start = tuple((jnp.zeros_like(p) for p in params))
    totals, (outputs, dinput) = lax.scan(step, start, (xs_all, valid_all, ct_all))
    return (outputs.reshape(TOKENS, D), dinput.reshape(TOKENS, D), totals[0], totals[1], totals[2], totals[3], totals[4], totals[5], totals[6], totals[7], totals[8], totals[9], totals[10], totals[11], totals[12])
```

```python
import jax
import jax.numpy as jnp
from jax import lax
from jax.sharding import PartitionSpec as P

HEADS = 12
HEAD_DIM = 64
WORD_SLOTS = 60
CORE, XBIT, YBIT = 1, 2, 4


def swap(value, bit):
    return lax.ppermute(value, "shard", [(i, i ^ bit) for i in range(8)])


def pick(value, index, axis):
    return lax.dynamic_index_in_dim(value, index, axis, keepdims=False)


def gather_pieces(first, second):
    out = []
    mine = (first, second)
    by_x = [swap(v, XBIT) for v in mine]
    by_y = [swap(v, YBIT) for v in mine]
    diagonal = [swap(by_y[0], XBIT), swap(by_x[1], YBIT)]
    for k in range(2):
        own = {0: mine[k], XBIT: by_x[k], YBIT: by_y[k], XBIT | YBIT: diagonal[k]}
        pieces = dict(own)
        for key, piece in own.items():
            pieces[key | CORE] = swap(piece, CORE)
        out.append(pieces)
    return out


def assemble(pieces, me):
    rows = pieces[0].shape[0]
    full = jnp.zeros((8 * rows,) + pieces[0].shape[1:], pieces[0].dtype)
    for key in range(8):
        full = lax.dynamic_update_slice_in_dim(full, pieces[key], (me ^ key) * rows, 0)
    return full


def scatter_sum(grad, me):
    bf, fl = jnp.bfloat16, jnp.float32
    core, x, y = me & 1, (me >> 1) & 1, me >> 2
    blocks = grad.reshape((2, 2, 2) + grad.shape[1:])
    got = swap(pick(blocks, 1 - core, 2).astype(bf), CORE)
    chip = pick(blocks, core, 2).astype(fl) + got.astype(fl)
    half = grad.shape[2] // 2
    a, b = chip[..., :half], chip[..., half:]
    got_a = swap(pick(a, 1 - x, 1).astype(bf), XBIT)
    got_b = swap(pick(b, 1 - y, 0).astype(bf), YBIT)
    a = pick(a, x, 1) + got_a.astype(fl)
    b = pick(b, y, 0) + got_b.astype(fl)
    got_a = swap(pick(a, 1 - y, 0).astype(bf), YBIT)
    got_b = swap(pick(b, 1 - x, 0).astype(bf), XBIT)
    a = pick(a, y, 0) + got_a.astype(fl)
    b = pick(b, x, 0) + got_b.astype(fl)
    return jnp.stack([a, b])


def rep_sum(parts):
    bf, fl = jnp.bfloat16, jnp.float32
    z = lax.axis_index("rep")
    mine = jnp.where((z == 0) | (z == 3), 0, 1)
    pairs = [(0, 1), (1, 0), (2, 3), (3, 2)]
    across = [(0, 3), (3, 0), (1, 2), (2, 1)]
    got = lax.ppermute(pick(parts, 1 - mine, 0).astype(bf), "rep", pairs)
    total = pick(parts, mine, 0) + got.astype(fl)
    got = lax.ppermute(total.astype(bf), "rep", across)
    total = total + got.astype(fl)
    low = total.astype(bf)
    other = lax.ppermute(low, "rep", pairs)
    low, other = low.astype(fl), other.astype(fl)
    first = jnp.where(mine == 0, low, other)
    second = jnp.where(mine == 0, other, low)
    return jnp.concatenate([first, second], -1)


def norm_rows(value, gain, shift):
    mean = jnp.mean(value, -1, keepdims=True)
    centred = value - mean
    scale = lax.rsqrt(jnp.mean(centred * centred, -1, keepdims=True) + 1e-05)
    normed = centred * scale
    return (normed * gain + shift, normed, scale)


def norm_back(grad, normed, scale, gain):
    dgain = jnp.sum(grad * normed, 0)
    dshift = jnp.sum(grad, 0)
    dnorm = grad * gain
    dvalue = scale * (
        dnorm
        - jnp.mean(dnorm, -1, keepdims=True)
        - normed * jnp.mean(dnorm * normed, -1, keepdims=True)
    )
    return (dvalue, dgain, dshift)


def outer(left, right):
    return lax.dot_general(
        left, right, (((0,), (0,)), ((), ())), preferred_element_type=jnp.float32
    )


def times_trans(left, right):
    return lax.dot_general(
        left, right, (((1,), (1,)), ((), ())), preferred_element_type=jnp.float32
    )


def gelu_slope(inner):
    cumul = 0.5 * (1.0 + lax.erf(inner * 0.7071067811865476))
    density = jnp.exp(-0.5 * inner * inner) * 0.3989422804014327
    return cumul + inner * density


def split_heads(block, pairs):
    return block.reshape(pairs, -1, HEADS, HEAD_DIM)


def masked_scores(queries, keys, valid):
    scores = jnp.einsum(
        "pqhe,pkhe->phqk", queries, keys, preferred_element_type=jnp.float32
    ) * HEAD_DIM ** (-0.5)
    return jnp.where(valid[:, None, None, :], scores, -1000000000.0)


def local(
    tokens,
    word_counts,
    region_counts,
    task_labels,
    masked_slots,
    qkv_weight,
    query_bias,
    value_bias,
    out_weight,
    out_bias,
    attn_gain,
    attn_shift,
    inner_weight,
    inner_bias,
    back_weight,
    back_bias,
    ffn_gain,
    ffn_shift,
    cotangent,
    *,
    shards,
    reps,
):
    fl = jnp.float32
    bf = jnp.bfloat16
    pairs = word_counts.shape[0]
    width = tokens.shape[1]
    hidden = back_weight.shape[0] * shards
    seq = tokens.shape[0] // pairs
    cube = shards == 8 and reps == 4
    me = lax.axis_index("shard")
    slots = jnp.arange(seq, dtype=jnp.int32)[None, :]
    words = word_counts[:, None]
    in_regions = (slots >= WORD_SLOTS) & (slots < WORD_SLOTS + region_counts[:, None])
    valid = (slots < words) | in_regions
    picked = masked_slots == 1
    labels = task_labels[:, None]
    live = (
        (labels == 0) & picked & (slots >= 1) & (slots < words)
        | (labels == 1) & picked & in_regions
        | (labels == 2) & (slots == 0)
    )
    row_weight = live.astype(fl).reshape(-1, 1)

    rows = width // shards
    vectors = jnp.stack(
        [query_bias, value_bias, out_bias, attn_gain, attn_shift, back_bias, ffn_gain, ffn_shift]
        + [inner_bias[k * rows : (k + 1) * rows] for k in range(hidden // width)],
        1,
    )
    vectors = jnp.pad(vectors, ((0, 0), (0, 128 - vectors.shape[1])))
    attn_shard = jnp.concatenate([qkv_weight, out_weight, vectors], 1)
    if cube:
        half = attn_shard.shape[0] // 2
        top, bottom = gather_pieces(attn_shard[:half], attn_shard[half:])
        attn_pieces = {k: jnp.concatenate([top[k], bottom[k]]) for k in top}
        attn_full = assemble(attn_pieces, me)
        inner_pieces, back_pieces = gather_pieces(inner_weight, back_weight)
        inner_full, back_full = assemble(inner_pieces, me), assemble(back_pieces, me)
    else:
        attn_full, inner_full, back_full = (
            lax.all_gather(v, "shard", axis=0, tiled=True)
            for v in (attn_shard, inner_weight, back_weight)
        )
    qkv_full = attn_full[:, : 3 * width]
    proj_full = attn_full[:, 3 * width : 4 * width]
    vectors = attn_full[:, 4 * width :].astype(fl).T
    qbias, vbias, pbias, again, ashift, bbias, fgain, fshift = vectors[:8]
    ibias = vectors[8 : 8 + hidden // width].reshape(-1, shards, rows).transpose(1, 0, 2).reshape(-1)

    bias = jnp.concatenate([qbias, jnp.zeros_like(qbias), vbias])
    qkv = (jnp.dot(tokens, qkv_full, preferred_element_type=fl) + bias).astype(bf)
    queries = split_heads(qkv[:, :width], pairs)
    keys = split_heads(qkv[:, width : 2 * width], pairs)
    values = split_heads(qkv[:, 2 * width :], pairs)
    scores = masked_scores(queries, keys, valid)
    peak = jnp.max(scores, -1, keepdims=True)
    expo = jnp.exp(scores - peak)
    total = jnp.sum(expo, -1, keepdims=True)
    lse = peak + jnp.log(total)
    probs_low = (expo / total).astype(bf)
    mixed = (
        jnp.einsum("phqk,pkhe->pqhe", probs_low, values, preferred_element_type=fl)
        .reshape(-1, width)
        .astype(bf)
    )
    branch = jnp.dot(mixed, proj_full, preferred_element_type=fl) + pbias
    hidden1, normed1, scale1 = norm_rows(tokens.astype(fl) + branch, again, ashift)
    hidden1_low = hidden1.astype(bf)
    inner = jnp.dot(hidden1_low, inner_full, preferred_element_type=fl) + ibias
    act = jax.nn.gelu(inner, approximate=False).astype(bf)
    second = jnp.dot(act, back_full, preferred_element_type=fl) + bbias
    result, normed2, scale2 = norm_rows(hidden1 + second, fgain, fshift)
    d_out = cotangent.astype(fl) * row_weight
    d_r2, grad_fgain, grad_fshift = norm_back(d_out, normed2, scale2, fgain)
    d_second = d_r2.astype(bf)
    grad_back = outer(act, d_second)
    grad_bbias = jnp.sum(d_second.astype(fl), 0)
    d_act = times_trans(d_second, back_full)
    d_inner = (d_act * gelu_slope(inner)).astype(bf)
    grad_inner = outer(hidden1_low, d_inner)
    grad_ibias = jnp.sum(d_inner.astype(fl), 0)
    d_hidden1 = d_r2 + times_trans(d_inner, inner_full)
    d_r1, grad_again, grad_ashift = norm_back(d_hidden1, normed1, scale1, again)
    d_branch = d_r1.astype(bf)
    grad_proj = outer(mixed, d_branch)
    grad_pbias = jnp.sum(d_branch.astype(fl), 0)
    d_mixed = split_heads(times_trans(d_branch, proj_full).astype(bf), pairs)
    probs = jnp.exp(masked_scores(queries, keys, valid) - lse)
    d_probs = jnp.einsum("pqhe,pkhe->phqk", d_mixed, values, preferred_element_type=fl)
    d_values = jnp.einsum("phqk,pqhe->pkhe", probs_low, d_mixed, preferred_element_type=fl)
    d_scores = (probs * (d_probs - jnp.sum(d_probs * probs, -1, keepdims=True))).astype(bf)
    d_queries = jnp.einsum(
        "phqk,pkhe->pqhe", d_scores, keys, preferred_element_type=fl
    ) * HEAD_DIM ** (-0.5)
    d_keys = jnp.einsum(
        "phqk,pqhe->pkhe", d_scores, queries, preferred_element_type=fl
    ) * HEAD_DIM ** (-0.5)
    d_qkv = jnp.concatenate(
        [d_queries.reshape(-1, width), d_keys.reshape(-1, width), d_values.reshape(-1, width)], 1
    ).astype(bf)
    grad_qkv = outer(tokens, d_qkv)
    grad_query = jnp.sum(d_qkv[:, :width].astype(fl), 0)
    grad_value = jnp.sum(d_qkv[:, 2 * width :].astype(fl), 0)
    input_grad = d_r1 + times_trans(d_qkv, qkv_full)

    grad_vectors = jnp.stack(
        [
            grad_query,
            grad_value,
            grad_pbias,
            grad_again,
            grad_ashift,
            grad_bbias,
            grad_fgain,
            grad_fshift,
        ]
    )
    grad_ibias = grad_ibias.reshape(shards, -1, rows).transpose(1, 0, 2).reshape(-1, width)
    grad_vectors = jnp.concatenate([grad_vectors, grad_ibias])
    grad_vectors = jnp.pad(grad_vectors, ((0, 256 - grad_vectors.shape[0]), (0, 0))).T
    grad_attn = jnp.concatenate([grad_qkv, grad_proj, grad_vectors], 1)
    if cube:
        back_sum, inner_sum, attn_sum = (
            rep_sum(scatter_sum(g.reshape(8, -1, g.shape[1]).astype(bf), me))
            for g in (grad_back, grad_inner, grad_attn)
        )
    else:
        back_sum, inner_sum, attn_sum = (
            lax.psum(
                lax.psum_scatter(g.astype(bf), "shard", scatter_dimension=0, tiled=True), "rep"
            ).astype(fl)
            for g in (grad_back, grad_inner, grad_attn)
        )
    sums = attn_sum[:, 4 * width :].T
    return (
        result.astype(bf),
        input_grad,
        attn_sum[:, : 3 * width],
        sums[0],
        sums[1],
        attn_sum[:, 3 * width : 4 * width],
        sums[2],
        sums[3],
        sums[4],
        inner_sum,
        sums[8 : 8 + hidden // width].reshape(-1),
        back_sum,
        sums[5],
        sums[6],
        sums[7],
    )


def solution(mesh):
    rows, both, one = P(("rep", "shard"), None), P(("rep", "shard")), P("shard")
    matrix = P("shard", None)
    in_specs = (rows, both, both, both, rows, matrix, one, one, matrix, one, one, one)
    in_specs += (matrix, one, matrix, one, one, one, rows)
    out_specs = (rows, rows, matrix, one, one, matrix, one, one, one, matrix, one, matrix)
    out_specs += (one, one, one)
    sizes = dict(mesh.shape)

    def run(*args):
        return local(*args, shards=sizes["shard"], reps=sizes["rep"])

    return jax.shard_map(
        run, mesh=mesh, in_specs=in_specs, out_specs=out_specs, check_vma=False
    )
```

```python
import functools

import jax
import jax.numpy as jnp
from jax import lax
from jax.experimental import pallas as pl
from jax.experimental.pallas import tpu as pltpu
from jax.sharding import PartitionSpec as P

HEADS = 12
HEAD_DIM = 64
WORD_SLOTS = 60
CORE, XBIT, YBIT = 1, 2, 4
BLOCKS = 8
STEP = 256
LIVE = 128
WINDOW = 96
VMEM = 60 * 2**20
F32 = jnp.float32
BF16 = jnp.bfloat16


def mm(left, right):
    return jnp.dot(left, right, preferred_element_type=F32)


def mm_nt(left, right):
    return lax.dot_general(left, right, (((1,), (1,)), ((), ())), preferred_element_type=F32)


def mm_tn(left, right):
    return lax.dot_general(left, right, (((0,), (0,)), ((), ())), preferred_element_type=F32)


def norm_parts(value):
    mean = jnp.mean(value, -1, keepdims=True)
    centred = value - mean
    scale = lax.rsqrt(jnp.mean(centred * centred, -1, keepdims=True) + 1e-05)
    return centred * scale, scale


def norm_grad(grad, normed, scale):
    return scale * (
        grad
        - jnp.mean(grad, -1, keepdims=True)
        - normed * jnp.mean(grad * normed, -1, keepdims=True)
    )


def column_sum(value):
    return jnp.sum(value, 0, keepdims=True)


def start_pieces(pieces, offsets, scratch, sems):
    copies = []
    for j, piece in enumerate(pieces):
        start = pl.multiple_of(offsets[j], 16)
        target = scratch.at[pl.ds(start, piece.shape[0]), :]
        copies.append(pltpu.make_async_copy(piece, target, sems.at[j]))
        copies[-1].start()
    return copies


def stacked(block):
    lane = lax.broadcasted_iota(jnp.int32, block.shape, 1)
    zero = jnp.zeros_like(block)
    return jnp.concatenate(
        [jnp.where(lane < HEAD_DIM, block, zero), jnp.where(lane >= HEAD_DIM, block, zero)], 0
    )


def unstacked(block):
    rows = block.shape[0] // 2
    lane = lax.broadcasted_iota(jnp.int32, (rows, block.shape[1]), 1)
    return jnp.where(lane < HEAD_DIM, block[:rows], block[rows:])


def probabilities(queries, keys, valid):
    scores = jnp.where(valid, mm_nt(queries, keys), -1000000000.0)
    peak = jnp.max(scores, -1, keepdims=True)
    expo = jnp.exp(scores - peak)
    return expo * (1.0 / jnp.sum(expo, -1, keepdims=True))


def valid_slots(words, regions, seq):
    slot = lax.broadcasted_iota(jnp.int32, (1, seq), 1)
    return (slot < words) | ((slot >= WORD_SLOTS) & (slot < WORD_SLOTS + regions))


def selector(pos, start, seq):
    row = lax.broadcasted_iota(jnp.int32, (WINDOW, seq), 0) + start
    return jnp.where(row == pos, 1.0, 0.0).astype(BF16)


def window_start(base):
    return pl.multiple_of(base // 16 * 16, 16)


def attend_kernel(count, seq, *refs):
    offsets, base, words, regions = refs[:4]
    pieces = refs[4 : 4 + count]
    tokens, cotangent, pos, weights_out, qkv, hidden, compact, vectors = refs[4 + count : 12 + count]
    weights, mixed, sems, out_sem = refs[12 + count :]
    width = tokens.shape[1]
    step = pl.program_id(0)
    export = pltpu.make_async_copy(weights, weights_out, out_sem)

    @pl.when(step == 0)
    def _():
        for copy in start_pieces(pieces, offsets, weights, sems):
            copy.wait()
        export.start()
        vectors[...] = weights[:, 4 * width :].astype(F32).T[: vectors.shape[0]]
        compact[...] = jnp.zeros_like(compact)

    x = tokens[...]
    for part, row in ((0, 0), (1, None), (2, 1)):
        columns = slice(part * width, (part + 1) * width)
        value = mm(x, weights[:, columns])
        if row is not None:
            value = value + vectors[row : row + 1, :]
        qkv[:, columns] = value.astype(BF16)
    for k in range(STEP // seq):
        rows = slice(k * seq, (k + 1) * seq)
        pair = step * (STEP // seq) + k
        valid = valid_slots(words[pair], regions[pair], seq)
        for h in range(HEADS // 2):
            lanes = slice(h * 128, (h + 1) * 128)
            queries = stacked(qkv[rows, lanes] * HEAD_DIM ** (-0.5))
            keys = qkv[rows, width + h * 128 : width + (h + 1) * 128]
            values = qkv[rows, 2 * width + h * 128 : 2 * width + (h + 1) * 128]
            probs = probabilities(queries, keys, valid).astype(BF16)
            mixed[rows, lanes] = unstacked(mm(probs, values)).astype(BF16)
    branch = mm(mixed[...], weights[:, 3 * width : 4 * width]) + vectors[2:3, :]
    normed, scale = norm_parts(x.astype(F32) + branch)
    value = normed * vectors[3:4, :] + vectors[4:5, :]
    hidden[...] = value
    high = scale.astype(BF16)
    rest = scale - high.astype(F32)
    middle = rest.astype(BF16)
    low = (rest - middle.astype(F32)).astype(BF16)
    lane = lax.broadcasted_iota(jnp.int32, (STEP, 128), 1)
    zero = jnp.zeros((STEP, 128), BF16)
    scales = jnp.where(lane == 0, high, jnp.where(lane == 1, middle, jnp.where(lane == 2, low, zero)))
    parts = (value.astype(BF16), normed.astype(BF16), mixed[...], cotangent[...], scales)
    for k in range(STEP // seq):
        pair = step * (STEP // seq) + k
        start = window_start(base[pair])
        chosen = selector(pos[pair], start, seq)
        at = 0
        for part in parts:
            columns = slice(at, at + part.shape[1])
            at += part.shape[1]
            got = mm(chosen, part[k * seq : (k + 1) * seq]).astype(BF16)
            compact[pl.ds(start, WINDOW), columns] += got

    @pl.when(step == pl.num_programs(0) - 1)
    def _():
        export.wait()


def gelu_parts(inner):
    cumul = 0.5 + 0.5 * lax.erf(inner * 0.7071067811865476)
    return inner * cumul, cumul


def inner_kernel(count, *refs):
    offsets, blocks = refs[:2]
    pieces = refs[2 : 2 + count]
    hidden, compact, bias, weights_out, act, live_act, live_slope = refs[2 + count : 9 + count]
    weights, sems, out_sem = refs[9 + count :]
    width = hidden.shape[1]
    size = weights.shape[1] // BLOCKS
    step = pl.program_id(0)
    export = pltpu.make_async_copy(weights, weights_out, out_sem)

    @pl.when(step == 0)
    def _():
        for copy in start_pieces(pieces, offsets, weights, sems):
            copy.wait()
        export.start()

        @pl.loop(0, blocks[0])
        def _(b):
            rows = pl.ds(pl.multiple_of(b * LIVE, LIVE), LIVE)
            x = compact[rows, :]
            for c in range(BLOCKS):
                columns = slice(c * size, (c + 1) * size)
                inner = mm(x, weights[:, columns]) + bias[:, columns]
                value, cumul = gelu_parts(inner)
                density = jnp.exp(-0.5 * inner * inner) * 0.3989422804014327
                live_act[rows, columns] = value.astype(BF16)
                live_slope[rows, columns] = (cumul + inner * density).astype(BF16)

    x = hidden[...].astype(BF16)
    for c in range(BLOCKS):
        columns = slice(c * size, (c + 1) * size)
        inner = mm(x, weights[:, columns]) + bias[:, columns]
        act[:, columns] = gelu_parts(inner)[0].astype(BF16)

    @pl.when(step == pl.num_programs(0) - 1)
    def _():
        export.wait()


def ffn_back_kernel(count, *refs):
    offsets, order, blocks = refs[:3]
    pieces = refs[3 : 3 + count]
    inner_hbm, compact, act, slope, vectors = refs[3 + count : 8 + count]
    back_out, keep_out, send_out, d_hidden, sums, inner_sum = refs[8 + count : 14 + count]
    back, inner, d_second, d_inner, total, out, sems, more = refs[14 + count :]
    width = inner.shape[0]
    size = inner.shape[1] // BLOCKS
    quarters = inner.shape[1] // width
    rows = width // BLOCKS
    first = slice(0, LIVE)
    count_live = blocks[0]
    copies = start_pieces(pieces, offsets, back, sems)
    inner_copy = pltpu.make_async_copy(inner_hbm, inner, more.at[0])
    inner_copy.start()
    export = pltpu.make_async_copy(back, back_out, more.at[1])
    sums[...] = jnp.zeros_like(sums)
    inner_sum[...] = jnp.zeros_like(inner_sum)
    for copy in copies:
        copy.wait()
    export.start()

    def rows_of(b):
        return pl.ds(pl.multiple_of(b * LIVE, LIVE), LIVE)

    @pl.loop(0, count_live)
    def _(b):
        here = rows_of(b)
        second = mm(act[here, :], back[...]) + vectors[5:6, :]
        normed, scale = norm_parts(compact[here, :width].astype(F32) + second)
        d_out = compact[here, 3 * width : 4 * width].astype(F32)
        sums[0:1, :] += column_sum(d_out * normed)
        sums[1:2, :] += column_sum(d_out)
        d_r2 = norm_grad(d_out * vectors[6:7, :], normed, scale)
        low = d_r2.astype(BF16)
        d_second[here, :] = low
        sums[2:3, :] += column_sum(low.astype(F32))
        d_hidden[here, :] = d_r2

    inner_copy.wait()

    @pl.loop(0, count_live)
    def _(b):
        here = rows_of(b)
        grad = d_second[here, :]
        for c in range(quarters):
            columns = slice(c * width, (c + 1) * width)
            d_act = mm_nt(grad, back[columns, :])
            low = (d_act * slope[here, columns].astype(F32)).astype(BF16)
            d_inner[here, columns] = low
            inner_sum[:, columns] += column_sum(low.astype(F32))
            d_hidden[here, :] += mm_nt(low, inner[:, columns])

    outs = []
    for i in range(BLOCKS):
        chunk = pl.ds(pl.multiple_of(order[i] * size, 128), size)
        total[:size, :] = mm_tn(act[first, chunk], d_second[first, :])

        @pl.loop(1, count_live)
        def _(b):
            here = rows_of(b)
            total[:size, :] += mm_tn(act[here, chunk], d_second[here, :])

        out[i, :size, :] = total[:size, :].astype(BF16)
    for c in range(quarters):
        columns = slice(c * width, (c + 1) * width)
        total[...] = mm_tn(compact[first, :width], d_inner[first, columns])

        @pl.loop(1, count_live)
        def _(b):
            here = rows_of(b)
            total[...] += mm_tn(compact[here, :width], d_inner[here, columns])

        for i in range(BLOCKS):
            start = pl.multiple_of(order[i] * rows, 8)
            target = slice(size + c * rows, size + (c + 1) * rows)
            out[i, target, :] = total[pl.ds(start, rows), :].astype(BF16)
    half = BLOCKS // 2
    outs = [
        pltpu.make_async_copy(out.at[pl.ds(half, half)], send_out, more.at[2]),
        pltpu.make_async_copy(out.at[pl.ds(0, half)], keep_out, more.at[3]),
    ]
    for copy in outs:
        copy.start()
    for copy in outs + [export]:
        copy.wait()


def result_kernel(act, hidden, back, vectors, result):
    second = mm(act[...], back[...]) + vectors[5:6, :]
    normed, _ = norm_parts(hidden[...] + second)
    result[...] = (normed * vectors[6:7, :] + vectors[7:8, :]).astype(BF16)


def attend_back_kernel(
    seq,
    order,
    base,
    words,
    regions,
    blocks,
    compact,
    d_hidden,
    proj,
    vectors,
    grads,
    qkv,
    tokens,
    pos,
    d_qkv_out,
    d_r1,
    keep_out,
    send_out,
    d_mixed,
    d_qkv,
    total,
    out,
    sums,
    sems,
):
    width = tokens.shape[1]
    rows = width // BLOCKS
    step = pl.program_id(0)
    count_live = blocks[0]
    d_branch = d_qkv

    def spread(columns):
        for i in range(BLOCKS):
            start = pl.multiple_of(order[i] * rows, 8)
            out[i, :, columns] = total[pl.ds(start, rows), : columns.stop - columns.start].astype(BF16)

    @pl.when(step == 0)
    def _():
        sums[...] = grads[...]
        d_mixed[...] = jnp.zeros_like(d_mixed)
        d_r1[...] = jnp.zeros_like(d_r1)

        @pl.loop(0, count_live)
        def _(b):
            here = pl.ds(pl.multiple_of(b * LIVE, LIVE), LIVE)
            grad = d_hidden[here, :]
            normed = compact[here, width : 2 * width].astype(F32)
            scale = jnp.sum(compact[here, 4 * width :].astype(F32), -1, keepdims=True)
            sums[3:4, :] += column_sum(grad * normed)
            sums[4:5, :] += column_sum(grad)
            value = norm_grad(grad * vectors[3:4, :], normed, scale)
            d_r1[here, :] = value
            low = value.astype(BF16)
            sums[2:3, :] += column_sum(low.astype(F32))
            d_branch[here, :width] = low
            d_mixed[here, :] = mm_nt(low, proj[...]).astype(BF16)

        total[...] = mm_tn(compact[:LIVE, 2 * width : 3 * width], d_branch[:LIVE, :width])

        @pl.loop(1, count_live)
        def _(b):
            here = pl.ds(pl.multiple_of(b * LIVE, LIVE), LIVE)
            total[...] += mm_tn(compact[here, 2 * width : 3 * width], d_branch[here, :width])

        spread(slice(3 * width, 4 * width))

    for k in range(STEP // seq):
        mine = slice(k * seq, (k + 1) * seq)
        pair = step * (STEP // seq) + k
        here = pl.ds(pl.multiple_of(pair * seq, seq), seq)
        valid = valid_slots(words[pair], regions[pair], seq)
        start = window_start(base[pair])
        chosen = selector(pos[pair], start, seq)
        d_mix = mm_tn(chosen, d_mixed[pl.ds(start, WINDOW), :]).astype(BF16)
        for h in range(HEADS // 2):
            lanes = slice(h * 128, (h + 1) * 128)
            queries = stacked(qkv[mine, lanes] * HEAD_DIM ** (-0.5))
            keys = qkv[mine, width + h * 128 : width + (h + 1) * 128]
            values = qkv[mine, 2 * width + h * 128 : 2 * width + (h + 1) * 128]
            probs = probabilities(queries, keys, valid)
            grad = stacked(d_mix[:, lanes])
            d_probs = mm_nt(grad, values)
            inside = jnp.sum(d_probs * probs, -1, keepdims=True)
            d_scores = (probs * (d_probs - inside)).astype(BF16)
            d_queries = unstacked(mm(d_scores, keys)) * HEAD_DIM ** (-0.5)
            d_keys = mm_tn(d_scores, queries)
            d_values = mm_tn(probs.astype(BF16), grad)
            for part, value in enumerate((d_queries, d_keys, d_values)):
                columns = slice(part * width + h * 128, part * width + (h + 1) * 128)
                low = value.astype(BF16)
                d_qkv[here, columns] = low
                if part != 1:
                    row = 0 if part == 0 else 1
                    sums[row : row + 1, lanes] += column_sum(low.astype(F32))
    block = pl.ds(pl.multiple_of(step * STEP, STEP), STEP)
    d_qkv_out[...] = d_qkv[block, :]

    @pl.when(step == pl.num_programs(0) - 1)
    def _():
        for part in range(3):
            columns = slice(part * width, (part + 1) * width)
            total[...] = mm_tn(tokens[...], d_qkv[:, columns])
            spread(columns)
        total[:, :128] = jnp.concatenate(
            [sums[...], jnp.zeros((128 - sums.shape[0], width), F32)], 0
        ).T
        spread(slice(4 * width, 4 * width + 128))
        half = BLOCKS // 2
        outs = [
            pltpu.make_async_copy(out.at[pl.ds(half, half)], send_out, sems.at[0]),
            pltpu.make_async_copy(out.at[pl.ds(0, half)], keep_out, sems.at[1]),
        ]
        for copy in outs:
            copy.start()
        for copy in outs:
            copy.wait()


def input_grad_kernel(seq, base, d_qkv, weights, d_r1, pos, out):
    step = pl.program_id(0)
    out[...] = mm_nt(d_qkv[...], weights[...])
    for k in range(STEP // seq):
        pair = step * (STEP // seq) + k
        start = window_start(base[pair])
        chosen = selector(pos[pair], start, seq)
        part = d_r1[pl.ds(start, WINDOW), :]
        high = part.astype(BF16)
        low = (part - high.astype(F32)).astype(BF16)
        out[k * seq : (k + 1) * seq, :] += mm_tn(chosen, high) + mm_tn(chosen, low)


def swap(value, bit):
    return lax.ppermute(value, "shard", [(i, i ^ bit) for i in range(8)])


def gather_pieces(mine):
    half = mine.shape[0] // 2
    by_x, by_y = swap(mine, XBIT), swap(mine, YBIT)
    far = XBIT | YBIT
    own = [(mine, 0, 0), (by_x, XBIT, 0), (by_y, YBIT, 0)]
    own += [(swap(by_y[:half], XBIT), far, 0), (swap(by_x[half:], YBIT), far, half)]
    return own + [(swap(v, CORE), key | CORE, row) for v, key, row in own]


def scatter_sum(keep, send, half):
    chip = keep.astype(F32) + swap(send, CORE).astype(F32)
    low = chip.astype(BF16)
    a, b = low[:, :half], low[:, half:]
    got_a = swap(a[1::2], XBIT)
    got_b = swap(b[2:], YBIT)
    a = (a[0::2].astype(F32) + got_a.astype(F32)).astype(BF16)
    b = (b[:2].astype(F32) + got_b.astype(F32)).astype(BF16)
    got_a = swap(a[1], YBIT)
    got_b = swap(b[1], XBIT)
    return a[0].astype(F32) + got_a.astype(F32), b[0].astype(F32) + got_b.astype(F32)


def rep_sum(a, b):
    z = lax.axis_index("rep")
    ends = (z == 0) | (z == 3)
    pairs = [(0, 1), (1, 0), (2, 3), (3, 2)]
    across = [(0, 3), (3, 0), (1, 2), (2, 1)]
    got = lax.ppermute(jnp.where(ends, b, a).astype(BF16), "rep", pairs)
    total = jnp.where(ends, a, b) + got.astype(F32)
    got = lax.ppermute(total.astype(BF16), "rep", across)
    low = (total + got.astype(F32)).astype(BF16)
    other = lax.ppermute(low, "rep", pairs)
    return jnp.where(ends, low, other).astype(F32), jnp.where(ends, other, low).astype(F32)


def whole(shape, dtype=None):
    del dtype
    return pl.BlockSpec(shape, lambda *_: (0,) * len(shape))


def steps(width):
    return pl.BlockSpec((STEP, width), lambda i: (i, 0))


SCALARS = pl.BlockSpec(memory_space=pltpu.SMEM)
ANYWHERE = pl.BlockSpec(memory_space=pl.ANY)


def shape_of(*dims, dtype=BF16):
    return jax.ShapeDtypeStruct(dims, dtype)


def params():
    return pltpu.CompilerParams(vmem_limit_bytes=VMEM)


def cost(flops, moved):
    return pl.CostEstimate(flops=int(flops), bytes_accessed=int(moved), transcendentals=0)


def local(
    tokens,
    word_counts,
    region_counts,
    task_labels,
    masked_slots,
    qkv_weight,
    query_bias,
    value_bias,
    out_weight,
    out_bias,
    attn_gain,
    attn_shift,
    inner_weight,
    inner_bias,
    back_weight,
    back_bias,
    ffn_gain,
    ffn_shift,
    cotangent,
    *,
    shards,
    reps,
):
    pairs = word_counts.shape[0]
    count, width = tokens.shape
    hidden = back_weight.shape[0] * shards
    seq = count // pairs
    grid = (count // STEP,)
    region_slots = seq - WORD_SLOTS
    cap = -(-(pairs * region_slots // 16 * 16 + WINDOW) // LIVE) * LIVE
    cube = shards == 8 and reps == 4
    rows = width // shards
    me = lax.axis_index("shard")

    vectors = jnp.stack(
        [query_bias, value_bias, out_bias, attn_gain, attn_shift, back_bias, ffn_gain, ffn_shift]
        + [inner_bias[k * rows : (k + 1) * rows] for k in range(hidden // width)],
        1,
    )
    vectors = jnp.pad(vectors, ((0, 0), (0, 128 - vectors.shape[1])))
    attn_shard = jnp.concatenate([qkv_weight, out_weight, vectors], 1)
    if cube:
        attn, inner, back = (gather_pieces(v) for v in (attn_shard, inner_weight, back_weight))
        order = jnp.array([0, 2, 4, 6, 1, 3, 5, 7], jnp.int32) ^ me
    else:
        attn, inner, back = (
            [(lax.all_gather(v, "shard", axis=0, tiled=True), 0, 0)]
            for v in (attn_shard, inner_weight, back_weight)
        )
        order = jnp.arange(BLOCKS, dtype=jnp.int32)

    def offsets(pieces, size):
        if not cube:
            return jnp.zeros((1,), jnp.int32)
        keys = jnp.array([key for _, key, _ in pieces], jnp.int32)
        return (keys ^ me) * size + jnp.array([row for _, _, row in pieces], jnp.int32)

    slots = jnp.arange(seq, dtype=jnp.int32)[None, :]
    words = word_counts[:, None]
    in_regions = (slots >= WORD_SLOTS) & (slots < WORD_SLOTS + region_counts[:, None])
    picked = masked_slots == 1
    labels = task_labels[:, None]
    live = (
        (labels == 0) & picked & (slots >= 1) & (slots < words)
        | (labels == 1) & picked & in_regions
        | (labels == 2) & (slots == 0)
    )
    live_count = jnp.sum(live.astype(jnp.int32), 1)
    base = jnp.cumsum(live_count) - live_count
    rank = jnp.cumsum(live.astype(jnp.int32), 1) - 1 + base[:, None]
    pos = jnp.where(live, rank, -1).reshape(pairs, 1, seq)
    blocks = jnp.maximum(1, (jnp.sum(live_count) + LIVE - 1) // LIVE).reshape(1)

    columns = 4 * width + 128
    attn_count = len(attn)
    attn_weights, qkv, hidden1, compact, vector_rows = pl.pallas_call(
        functools.partial(attend_kernel, attn_count, seq),
        grid=grid,
        in_specs=[SCALARS] * 4
        + [ANYWHERE] * attn_count
        + [steps(width), steps(width), whole((pairs, 1, seq))],
        out_specs=[
            ANYWHERE,
            steps(3 * width),
            steps(width),
            whole((cap, columns)),
            whole((16, width)),
        ],
        out_shape=[
            shape_of(width, columns),
            shape_of(count, 3 * width),
            shape_of(count, width, dtype=F32),
            shape_of(cap, columns),
            shape_of(16, width, dtype=F32),
        ],
        scratch_shapes=[
            pltpu.VMEM((width, columns), BF16),
            pltpu.VMEM((STEP, width), BF16),
            pltpu.SemaphoreType.DMA((attn_count,)),
            pltpu.SemaphoreType.DMA,
        ],
        compiler_params=params(),
        cost_estimate=cost(8 * count * width * width + 4 * count * seq * width, 30e6),
        name="attend",
    )(
        offsets(attn, rows),
        base,
        word_counts,
        region_counts,
        *(v for v, _, _ in attn),
        tokens,
        cotangent,
        pos,
    )

    inner_bias_full = (
        vector_rows[8 : 8 + hidden // width]
        .reshape(-1, shards, rows)
        .transpose(1, 0, 2)
        .reshape(1, hidden)
    )
    inner_count = len(inner)
    inner_weights, act, live_act, live_slope = pl.pallas_call(
        functools.partial(inner_kernel, inner_count),
        grid=grid,
        in_specs=[SCALARS] * 2
        + [ANYWHERE] * inner_count
        + [steps(width), whole((cap, width)), whole((1, hidden))],
        out_specs=[ANYWHERE, steps(hidden), whole((cap, hidden)), whole((cap, hidden))],
        out_shape=[
            shape_of(width, hidden),
            shape_of(count, hidden),
            shape_of(cap, hidden),
            shape_of(cap, hidden),
        ],
        scratch_shapes=[
            pltpu.VMEM((width, hidden), BF16),
            pltpu.SemaphoreType.DMA((inner_count,)),
            pltpu.SemaphoreType.DMA,
        ],
        compiler_params=params(),
        cost_estimate=cost(2 * count * width * hidden, 30e6),
        name="ffn_inner",
    )(offsets(inner, rows), blocks, *(v for v, _, _ in inner), hidden1, compact, inner_bias_full)

    back_count = len(back)
    half = BLOCKS // 2
    size = hidden // BLOCKS
    both = size + hidden // width * (width // BLOCKS)
    back_weights, keep_ffn, send_ffn, d_hidden1, sums, inner_sum = pl.pallas_call(
        functools.partial(ffn_back_kernel, back_count),
        in_specs=[SCALARS] * 3
        + [ANYWHERE] * (back_count + 1)
        + [pl.BlockSpec(memory_space=pltpu.VMEM)] * 4,
        out_specs=[ANYWHERE] * 3 + [pl.BlockSpec(memory_space=pltpu.VMEM)] * 3,
        out_shape=[
            shape_of(hidden, width),
            shape_of(half, both, width),
            shape_of(half, both, width),
            shape_of(cap, width, dtype=F32),
            shape_of(8, width, dtype=F32),
            shape_of(1, hidden, dtype=F32),
        ],
        scratch_shapes=[
            pltpu.VMEM((hidden, width), BF16),
            pltpu.VMEM((width, hidden), BF16),
            pltpu.VMEM((cap, width), BF16),
            pltpu.VMEM((cap, hidden), BF16),
            pltpu.VMEM((width, width), F32),
            pltpu.VMEM((BLOCKS, both, width), BF16),
            pltpu.SemaphoreType.DMA((back_count,)),
            pltpu.SemaphoreType.DMA((4,)),
        ],
        compiler_params=params(),
        cost_estimate=cost(12 * LIVE * width * hidden, 30e6),
        name="ffn_back",
    )(
        offsets(back, back_weight.shape[0]),
        order,
        blocks,
        *(v for v, _, _ in back),
        inner_weights,
        compact,
        live_act,
        live_slope,
        vector_rows,
    )

    result = pl.pallas_call(
        result_kernel,
        grid=grid,
        in_specs=[steps(hidden), steps(width), whole((hidden, width)), whole((16, width))],
        out_specs=steps(width),
        out_shape=shape_of(count, width),
        compiler_params=params(),
        cost_estimate=cost(2 * count * width * hidden, 16e6),
        name="result",
    )(act, hidden1, back_weights, vector_rows)

    grads = jnp.concatenate(
        [
            jnp.zeros((5, width), F32),
            sums[2:3],
            sums[0:2],
            inner_sum.reshape(shards, -1, rows).transpose(1, 0, 2).reshape(-1, width),
            jnp.zeros((8 - hidden // width, width), F32),
        ]
    )
    d_qkv, d_r1, keep_attn, send_attn = pl.pallas_call(
        functools.partial(attend_back_kernel, seq),
        grid=grid,
        in_specs=[SCALARS] * 5
        + [
            whole((cap, columns)),
            whole((cap, width)),
            pl.BlockSpec((width, width), lambda i: (0, 3)),
            whole((16, width)),
            whole((16, width)),
            steps(3 * width),
            whole((count, width)),
            whole((pairs, 1, seq)),
        ],
        out_specs=[steps(3 * width), whole((cap, width)), ANYWHERE, ANYWHERE],
        out_shape=[
            shape_of(count, 3 * width),
            shape_of(cap, width, dtype=F32),
            shape_of(half, width // BLOCKS, columns),
            shape_of(half, width // BLOCKS, columns),
        ],
        scratch_shapes=[
            pltpu.VMEM((cap, width), BF16),
            pltpu.VMEM((count, 3 * width), BF16),
            pltpu.VMEM((width, width), F32),
            pltpu.VMEM((BLOCKS, width // BLOCKS, columns), BF16),
            pltpu.VMEM((16, width), F32),
            pltpu.SemaphoreType.DMA((2,)),
        ],
        compiler_params=params(),
        cost_estimate=cost(6 * count * width * width + 14 * count * seq * width, 30e6),
        name="attend_back",
    )(
        order,
        base,
        word_counts,
        region_counts,
        blocks,
        compact,
        d_hidden1,
        attn_weights,
        vector_rows,
        grads,
        qkv,
        tokens,
        pos,
    )

    input_grad = pl.pallas_call(
        functools.partial(input_grad_kernel, seq),
        grid=grid,
        in_specs=[
            SCALARS,
            steps(3 * width),
            pl.BlockSpec((width, 3 * width), lambda i: (0, 0)),
            whole((cap, width)),
            whole((pairs, 1, seq)),
        ],
        out_specs=steps(width),
        out_shape=shape_of(count, width, dtype=F32),
        compiler_params=params(),
        cost_estimate=cost(6 * count * width * width, 16e6),
        name="input_grad",
    )(base, d_qkv, attn_weights, d_r1, pos)

    quarters = hidden // width
    block = width // BLOCKS
    if cube:
        back_sum, inner_sum = rep_sum(*scatter_sum(keep_ffn, send_ffn, size))
        inner_sum = inner_sum.reshape(quarters, block, width)
        inner_sum = jnp.concatenate([inner_sum[c] for c in range(quarters)], 1)
        attn_sum = jnp.concatenate(rep_sum(*scatter_sum(keep_attn, send_attn, block // 2)), 0)
    else:
        ffn = jnp.concatenate([keep_ffn, send_ffn])
        inner_grad = ffn[:, size:].reshape(BLOCKS, quarters, block, width)
        inner_grad = inner_grad.transpose(0, 2, 1, 3).reshape(width, hidden)
        attn_grad = jnp.concatenate([keep_attn, send_attn]).reshape(width, columns)
        back_sum, inner_sum, attn_sum = (
            lax.psum(lax.psum_scatter(g, "shard", scatter_dimension=0, tiled=True), "rep").astype(F32)
            for g in (ffn[:, :size].reshape(hidden, width), inner_grad, attn_grad)
        )
    sums = attn_sum[:, 4 * width :].T
    return (
        result,
        input_grad,
        attn_sum[:, : 3 * width],
        sums[0],
        sums[1],
        attn_sum[:, 3 * width : 4 * width],
        sums[2],
        sums[3],
        sums[4],
        inner_sum,
        sums[8 : 8 + quarters].reshape(-1),
        back_sum,
        sums[5],
        sums[6],
        sums[7],
    )


def solution(mesh):
    rows, both, one = P(("rep", "shard"), None), P(("rep", "shard")), P("shard")
    matrix = P("shard", None)
    in_specs = (rows, both, both, both, rows, matrix, one, one, matrix, one, one, one)
    in_specs += (matrix, one, matrix, one, one, one, rows)
    out_specs = (rows, rows, matrix, one, one, matrix, one, one, one, matrix, one, matrix)
    out_specs += (one, one, one)
    sizes = dict(mesh.shape)

    def run(*args):
        return local(*args, shards=sizes["shard"], reps=sizes["rep"])

    return jax.shard_map(
        run, mesh=mesh, in_specs=in_specs, out_specs=out_specs, check_vma=False
    )
```

```python
import functools

import jax
import jax.numpy as jnp
from jax import lax
from jax.experimental import pallas as pl
from jax.experimental.pallas import tpu as pltpu
from jax.sharding import PartitionSpec as P

HEADS = 12
HEAD_DIM = 64
WORD_SLOTS = 60
CORE, XBIT, YBIT = 1, 2, 4
BLOCKS = 8
STEP = 256
LIVE = 192
WINDOW = 80
PART = 16
VMEM = 60 * 2**20
F32 = jnp.float32
BF16 = jnp.bfloat16


def mm(left, right):
    return jnp.dot(left, right, preferred_element_type=F32)


def mm_nt(left, right):
    return lax.dot_general(left, right, (((1,), (1,)), ((), ())), preferred_element_type=F32)


def mm_tn(left, right):
    return lax.dot_general(left, right, (((0,), (0,)), ((), ())), preferred_element_type=F32)


def norm_parts(value):
    mean = jnp.mean(value, -1, keepdims=True)
    centred = value - mean
    scale = lax.rsqrt(jnp.mean(centred * centred, -1, keepdims=True) + 1e-05)
    return centred * scale, scale


def norm_grad(grad, normed, scale):
    return scale * (
        grad
        - jnp.mean(grad, -1, keepdims=True)
        - normed * jnp.mean(grad * normed, -1, keepdims=True)
    )


def column_sum(value):
    return jnp.sum(value, 0, keepdims=True)


def start_pieces(pieces, offsets, scratch, sems, first=0, started=False):
    copies = []
    for j, piece in enumerate(pieces):
        start = pl.multiple_of(offsets[j], 16)
        source = piece.at[:, pl.ds(first, scratch.shape[1])]
        target = scratch.at[pl.ds(start, piece.shape[0]), :]
        copies.append(pltpu.make_async_copy(source, target, sems.at[j]))
        if not started:
            copies[-1].start()
    return copies


def stacked(block):
    lane = lax.broadcasted_iota(jnp.int32, block.shape, 1)
    zero = jnp.zeros_like(block)
    return jnp.concatenate(
        [jnp.where(lane < HEAD_DIM, block, zero), jnp.where(lane >= HEAD_DIM, block, zero)], 0
    )


def unstacked(block):
    rows = block.shape[0] // 2
    lane = lax.broadcasted_iota(jnp.int32, (rows, block.shape[1]), 1)
    return jnp.where(lane < HEAD_DIM, block[:rows], block[rows:])


def probabilities(queries, keys, valid):
    scores = jnp.where(valid, mm_nt(queries, keys), -1000000000.0)
    peak = jnp.max(scores, -1, keepdims=True)
    expo = jnp.exp(scores - peak)
    return expo * (1.0 / jnp.sum(expo, -1, keepdims=True))


def valid_slots(words, regions, seq):
    slot = lax.broadcasted_iota(jnp.int32, (1, seq), 1)
    return (slot < words) | ((slot >= WORD_SLOTS) & (slot < WORD_SLOTS + regions))


def selector(pos, start, seq):
    row = lax.broadcasted_iota(jnp.int32, (WINDOW, seq), 0) + start
    return jnp.where(row == pos, 1.0, 0.0).astype(BF16)


def window_start(base):
    return pl.multiple_of(base, PART)


def project_kernel(count, *refs):
    offsets = refs[0]
    pieces = refs[1 : 1 + count]
    tokens, qkv, vectors, weights, sems = refs[1 + count :]
    width = tokens.shape[1]

    @pl.when(pl.program_id(0) == 0)
    def _():
        for copy in start_pieces(pieces, offsets, weights, sems):
            copy.wait()
        vectors[...] = weights[:, 4 * width :].astype(F32).T[: vectors.shape[0]]

    x = tokens[...]
    for part, row in ((0, 0), (1, None), (2, 1)):
        columns = slice(part * width, (part + 1) * width)
        value = mm(x, weights[:, columns])
        if row is not None:
            value = value + vectors[row : row + 1, :]
        qkv[:, columns] = value.astype(BF16)


def attend_kernel(count, seq, *refs):
    offsets, base, words, regions = refs[:4]
    pieces = refs[4 : 4 + count]
    tokens, cotangent, qkv, pos, vectors, hidden, compact, proj, mixed, sems = refs[4 + count :]
    width = tokens.shape[1]
    step = pl.program_id(0)

    @pl.when(step == 0)
    def _():
        copies = start_pieces(pieces, offsets, proj, sems, 3 * width)
        compact[...] = jnp.zeros_like(compact)
        for copy in copies:
            copy.wait()

    for k in range(STEP // seq):
        rows = slice(k * seq, (k + 1) * seq)
        pair = step * (STEP // seq) + k
        valid = valid_slots(words[pair], regions[pair], seq)
        for h in range(HEADS // 2):
            lanes = slice(h * 128, (h + 1) * 128)
            queries = stacked(qkv[rows, lanes] * HEAD_DIM ** (-0.5))
            keys = qkv[rows, width + h * 128 : width + (h + 1) * 128]
            values = qkv[rows, 2 * width + h * 128 : 2 * width + (h + 1) * 128]
            scores = jnp.where(valid, mm_nt(queries, keys), -1000000000.0)
            expo = jnp.exp(scores - jnp.max(scores, -1, keepdims=True)).astype(BF16)
            both = mm(expo, jnp.concatenate([values, jnp.ones_like(values)], 1))
            mixed[rows, lanes] = (unstacked(both[:, :128]) / unstacked(both[:, 128:])).astype(BF16)
    branch = mm(mixed[...], proj[...]) + vectors[2:3, :]
    normed, scale = norm_parts(tokens[...].astype(F32) + branch)
    value = normed * vectors[3:4, :] + vectors[4:5, :]
    hidden[...] = value
    high = scale.astype(BF16)
    rest = scale - high.astype(F32)
    middle = rest.astype(BF16)
    low = (rest - middle.astype(F32)).astype(BF16)
    lane = lax.broadcasted_iota(jnp.int32, (STEP, 128), 1)
    zero = jnp.zeros((STEP, 128), BF16)
    scales = jnp.where(lane == 0, high, jnp.where(lane == 1, middle, jnp.where(lane == 2, low, zero)))
    parts = (value.astype(BF16), normed.astype(BF16), mixed[...], cotangent[...], scales)
    for k in range(STEP // seq):
        pair = step * (STEP // seq) + k
        start = window_start(base[pair])
        chosen = selector(pos[pair], start, seq)
        at = 0
        for part in parts:
            columns = slice(at, at + part.shape[1])
            at += part.shape[1]
            got = mm(chosen, part[k * seq : (k + 1) * seq]).astype(BF16)
            compact[pl.ds(start, WINDOW), columns] = got


def gelu_parts(inner):
    cumul = 0.5 + 0.5 * lax.erf(inner * 0.7071067811865476)
    return inner * cumul, cumul


def live_inner_kernel(count, *refs):
    offsets, blocks = refs[:2]
    pieces = refs[2 : 2 + count]
    compact, bias, act_out, slope_out = refs[2 + count : 6 + count]
    weights, hidden, act, slope, sems, more = refs[6 + count :]
    width = hidden.shape[1]
    copies = start_pieces(pieces, offsets, weights, sems)
    count_live = blocks[0]

    def rows_of(b):
        return pl.ds(pl.multiple_of(b * LIVE, LIVE), LIVE)

    def load(b):
        return pltpu.make_async_copy(compact.at[rows_of(b), pl.ds(0, width)], hidden, more.at[0])

    load(0).start()
    for copy in copies:
        copy.wait()

    @pl.loop(0, count_live)
    def _(b):
        load(b).wait()
        x = hidden[...]
        for c in range(weights.shape[1] // width):
            columns = slice(c * width, (c + 1) * width)
            inner = mm(x, weights[:, columns]) + bias[:, columns]
            value, cumul = gelu_parts(inner)
            density = jnp.exp(-0.5 * inner * inner) * 0.3989422804014327
            act[:, columns] = value.astype(BF16)
            slope[:, columns] = (cumul + inner * density).astype(BF16)
        outs = [
            pltpu.make_async_copy(act, act_out.at[rows_of(b)], more.at[1]),
            pltpu.make_async_copy(slope, slope_out.at[rows_of(b)], more.at[2]),
        ]
        for copy in outs:
            copy.start()

        @pl.when(b + 1 < count_live)
        def _():
            load(b + 1).start()

        for copy in outs:
            copy.wait()


def ffn_kernel(counts, *refs):
    inner_offsets, back_offsets = refs[:2]
    inner_pieces = refs[2 : 2 + counts[0]]
    back_pieces = refs[2 + counts[0] : 2 + counts[0] + counts[1]]
    hidden, bias, vectors = refs[2 + sum(counts) : 5 + sum(counts)]
    result, inner, back, act, inner_sems, back_sems = refs[-6:]
    width = hidden.shape[1]
    step = pl.program_id(0)

    @pl.when(step == 0)
    def _():
        copies = start_pieces(inner_pieces, inner_offsets, inner, inner_sems)
        start_pieces(back_pieces, back_offsets, back, back_sems)
        for copy in copies:
            copy.wait()

    x = hidden[...]
    low = x.astype(BF16)
    for c in range(inner.shape[1] // width):
        columns = slice(c * width, (c + 1) * width)
        value = mm(low, inner[:, columns]) + bias[:, columns]
        act[:, columns] = gelu_parts(value)[0].astype(BF16)

    @pl.when(step == 0)
    def _():
        for copy in start_pieces(back_pieces, back_offsets, back, back_sems, started=True):
            copy.wait()

    second = mm(act[...], back[...]) + vectors[5:6, :]
    normed, _ = norm_parts(x + second)
    result[...] = (normed * vectors[6:7, :] + vectors[7:8, :]).astype(BF16)


def ffn_back_kernel(counts, *refs):
    inner_offsets, back_offsets, order, blocks = refs[:4]
    inner_pieces = refs[4 : 4 + counts[0]]
    back_pieces = refs[4 + counts[0] : 4 + sum(counts)]
    refs = refs[4 + sum(counts) :]
    compact_hbm, act_hbm, slope_hbm, vectors = refs[:4]
    keep_back, send_back, keep_inner, send_inner, d_hidden_out, sums, inner_sum = refs[4:11]
    back, inner, hidden, cotangent, act, slope, d_second, d_inner, d_hidden = refs[11:20]
    total, out_back, out_inner, turned, ordered, inner_sems, back_sems, more = refs[20:]
    width = inner.shape[0]
    size = inner.shape[1] // BLOCKS
    quarters = inner.shape[1] // width
    rows = width // BLOCKS
    half = BLOCKS // 2
    first = slice(0, LIVE)
    count_live = blocks[0]

    def rows_of(b):
        return pl.ds(pl.multiple_of(b * LIVE, LIVE), LIVE)

    def live_copies(b):
        here = rows_of(b)
        return [
            pltpu.make_async_copy(compact_hbm.at[here, pl.ds(0, width)], hidden.at[here], more.at[0]),
            pltpu.make_async_copy(
                compact_hbm.at[here, pl.ds(3 * width, width)], cotangent.at[here], more.at[1]
            ),
            pltpu.make_async_copy(act_hbm.at[here], act.at[here], more.at[2]),
            pltpu.make_async_copy(slope_hbm.at[here], slope.at[here], more.at[3]),
        ]

    now = live_copies(0)
    for copy in now:
        copy.start()
    back_copies = start_pieces(back_pieces, back_offsets, back, back_sems)
    inner_copies = start_pieces(inner_pieces, inner_offsets, inner, inner_sems)
    sums[...] = jnp.zeros_like(sums)
    inner_sum[...] = jnp.zeros_like(inner_sum)
    for copy in now:
        copy.wait()

    @pl.loop(1, count_live)
    def _(b):
        later = live_copies(b)
        for copy in later:
            copy.start()
        for copy in later:
            copy.wait()

    for copy in back_copies:
        copy.wait()

    @pl.loop(0, count_live)
    def _(b):
        here = rows_of(b)
        second = mm(act[here, :], back[...]) + vectors[5:6, :]
        normed, scale = norm_parts(hidden[here, :].astype(F32) + second)
        d_out = cotangent[here, :].astype(F32)
        sums[6:7, :] += column_sum(d_out * normed)
        sums[7:8, :] += column_sum(d_out)
        d_r2 = norm_grad(d_out * vectors[6:7, :], normed, scale)
        low = d_r2.astype(BF16)
        d_second[here, :] = low
        sums[5:6, :] += column_sum(low.astype(F32))
        d_hidden[here, :] = d_r2

    single = count_live == 1
    outs = []
    for i in range(BLOCKS):
        chunk = pl.ds(pl.multiple_of(order[i] * size, 128), size)

        @pl.when(single)
        def _():
            out_back[i] = mm_tn(act[first, chunk], d_second[first, :]).astype(BF16)

        @pl.when(jnp.logical_not(single))
        def _():
            total[:size, :] = mm_tn(act[first, chunk], d_second[first, :])

            @pl.loop(1, count_live)
            def _(b):
                here = rows_of(b)
                total[:size, :] += mm_tn(act[here, chunk], d_second[here, :])

            out_back[i] = total[:size, :].astype(BF16)

        target = keep_back.at[i] if i < half else send_back.at[i - half]
        outs.append(pltpu.make_async_copy(out_back.at[i], target, more.at[4 + i]))
        outs[-1].start()
    for copy in inner_copies:
        copy.wait()

    @pl.loop(0, count_live)
    def _(b):
        here = rows_of(b)
        grad = d_second[here, :]
        for c in range(quarters):
            columns = slice(c * width, (c + 1) * width)
            d_act = mm_nt(grad, back[columns, :])
            low = (d_act * slope[here, columns].astype(F32)).astype(BF16)
            d_inner[here, columns] = low
            inner_sum[:, columns] += column_sum(low.astype(F32))
            d_hidden[here, :] += mm_nt(low, inner[:, columns])

    def hidden_copy(b):
        return pltpu.make_async_copy(
            d_hidden.at[rows_of(b)], d_hidden_out.at[rows_of(b)], more.at[0]
        )

    hidden_copy(0).start()

    @pl.loop(0, count_live)
    def _(b):
        here = rows_of(b)
        turned[...] = hidden[here, :].T
        for i in range(BLOCKS):
            start = pl.multiple_of(order[i] * rows, 16)
            ordered[b, i * rows : (i + 1) * rows, :] = turned[pl.ds(start, rows), :]

    for c in range(quarters):
        columns = slice(c * width, (c + 1) * width)
        target = slice(c * rows, (c + 1) * rows)

        @pl.when(single)
        def _():
            value = mm(ordered[0], d_inner[first, columns]).astype(BF16)
            for i in range(BLOCKS):
                out_inner[i, target, :] = value[i * rows : (i + 1) * rows, :]

        @pl.when(jnp.logical_not(single))
        def _():
            total[...] = mm(ordered[0], d_inner[first, columns])

            @pl.loop(1, count_live)
            def _(b):
                total[...] += mm(ordered[b], d_inner[rows_of(b), columns])

            for i in range(BLOCKS):
                out_inner[i, target, :] = total[i * rows : (i + 1) * rows, :].astype(BF16)

        for j, out in enumerate((keep_inner, send_inner)):
            blocks_out = pl.ds(j * half, half)
            part = pl.ds(c * rows, rows)
            source = out_inner.at[blocks_out, part]
            outs.append(pltpu.make_async_copy(source, out.at[:, part], more.at[12 + 2 * c + j]))
            outs[-1].start()
    hidden_copy(0).wait()

    @pl.loop(1, count_live)
    def _(b):
        hidden_copy(b).start()
        hidden_copy(b).wait()

    for copy in outs:
        copy.wait()


def by_head(block):
    lane = lax.broadcasted_iota(jnp.int32, block.shape, 1) // HEAD_DIM
    zero = jnp.zeros_like(block)
    return jnp.concatenate([jnp.where(lane == h, block, zero) for h in range(HEADS)], 0)


def from_heads(block):
    rows = block.shape[0] // HEADS
    lane = lax.broadcasted_iota(jnp.int32, (rows, 128), 1)
    parts = []
    for h in range(HEADS // 2):
        lanes = slice(h * 128, (h + 1) * 128)
        left = block[2 * h * rows : (2 * h + 1) * rows, lanes]
        right = block[(2 * h + 1) * rows : (2 * h + 2) * rows, lanes]
        parts.append(jnp.where(lane < HEAD_DIM, left, right))
    return jnp.concatenate(parts, 1)


def attend_back_kernel(count, seq, shard_rows, *refs):
    offsets, order, base, words, regions, blocks = refs[:6]
    pieces = refs[6 : 6 + count]
    refs = refs[6 + count :]
    compact, d_hidden_hbm, qkv_hbm, tokens_hbm, vectors, ffn_sums, inner_sum, pos = refs[:8]
    d_qkv_out, d_r1_out, keep_out, send_out = refs[8:12]
    proj, normed_in, mixed, scales, d_hidden, qkv, tokens, d_r1, d_mixed = refs[12:21]
    d_query, d_keys, d_values, d_qkv, total, out, sums = refs[21:28]
    turned, mixed_turned, tokens_turned, sems, more = refs[28:]
    width = proj.shape[0]
    rows = width // BLOCKS
    half = BLOCKS // 2
    pairs = pos.shape[0]
    count_live = blocks[0]

    def rows_of(b):
        return pl.ds(pl.multiple_of(b * LIVE, LIVE), LIVE)

    def live_copies(b):
        here = rows_of(b)
        sources = [
            (compact.at[here, pl.ds(width, width)], normed_in),
            (compact.at[here, pl.ds(2 * width, width)], mixed),
            (compact.at[here, pl.ds(4 * width, 128)], scales),
            (d_hidden_hbm.at[here], d_hidden),
        ]
        return [
            pltpu.make_async_copy(source, target.at[here], more.at[j])
            for j, (source, target) in enumerate(sources)
        ]

    now = live_copies(0)
    for copy in now:
        copy.start()
    proj_copies = start_pieces(pieces, offsets, proj, sems, 3 * width)
    qkv_copy = pltpu.make_async_copy(qkv_hbm, qkv, more.at[4])
    tokens_copy = pltpu.make_async_copy(tokens_hbm, tokens, more.at[5])
    qkv_copy.start()
    tokens_copy.start()
    d_r1[...] = jnp.zeros_like(d_r1)
    sums[...] = ffn_sums[...]
    for copy in now:
        copy.wait()

    @pl.loop(1, count_live)
    def _(b):
        later = live_copies(b)
        for copy in later:
            copy.start()
        for copy in later:
            copy.wait()

    for copy in proj_copies:
        copy.wait()

    @pl.loop(0, count_live)
    def _(b):
        here = rows_of(b)
        grad = d_hidden[here, :]
        normed = normed_in[here, :].astype(F32)
        scale = jnp.sum(scales[here, :].astype(F32), -1, keepdims=True)
        sums[3:4, :] += column_sum(grad * normed)
        sums[4:5, :] += column_sum(grad)
        low = norm_grad(grad * vectors[3:4, :], normed, scale).astype(BF16)
        sums[2:3, :] += column_sum(low.astype(F32))
        d_r1[here, :] = low
        d_mixed[here, :] = mm_nt(low, proj[...]).astype(BF16)

    d_r1_copy = pltpu.make_async_copy(d_r1, d_r1_out, more.at[0])
    d_r1_copy.start()

    def in_order(source, target):
        turned[:, : source.shape[0]] = source.T
        for i in range(BLOCKS):
            start = pl.multiple_of(order[i] * rows, 16)
            target[i * rows : (i + 1) * rows, :] = turned[pl.ds(start, rows), : source.shape[0]]

    outs = []

    def spread(value, first, size):
        low = value.astype(BF16)
        for i in range(BLOCKS):
            out[i, :, first : first + size] = low[i * rows : (i + 1) * rows, :size]
        columns = pl.ds(first, size)
        for j, target in enumerate((keep_out, send_out)):
            source = out.at[pl.ds(j * half, half), :, columns]
            sem = more.at[6 + len(outs)]
            outs.append(pltpu.make_async_copy(source, target.at[:, :, columns], sem))
            outs[-1].start()

    in_order(mixed[:LIVE, :], mixed_turned)

    @pl.when(count_live == 1)
    def _():
        total[...] = mm(mixed_turned[...], d_r1[:LIVE, :])

    @pl.when(count_live > 1)
    def _():
        total[...] = mm(mixed_turned[...], d_r1[:LIVE, :])

        @pl.loop(1, count_live)
        def _(b):
            here = rows_of(b)
            in_order(mixed[here, :], mixed_turned)
            total[...] += mm(mixed_turned[...], d_r1[here, :])

    spread(total[...], 3 * width, width)
    tokens_copy.wait()
    in_order(tokens[...], tokens_turned)
    qkv_copy.wait()

    def pair_part(pair, b):
        mine = slice(pair * seq, (pair + 1) * seq)
        valid = valid_slots(words[pair], regions[pair], seq)
        first = pl.multiple_of(base[pair] + b * PART, PART)
        row = lax.broadcasted_iota(jnp.int32, (PART, seq), 0) + first
        chosen = jnp.where(row == pos[pair], 1.0, 0.0).astype(BF16)
        live_query = mm(chosen, qkv[mine, :width]).astype(BF16) * HEAD_DIM ** (-0.5)
        queries = by_head(live_query)
        grad = d_mixed[pl.ds(first, PART), :]
        row = lax.broadcasted_iota(jnp.int32, grad.shape, 0) + first
        grad = by_head(jnp.where(row < base[pair + 1], grad, jnp.zeros_like(grad)))
        keys = qkv[mine, width : 2 * width]
        probs = probabilities(queries, keys, valid)
        d_probs = mm_nt(grad, qkv[mine, 2 * width :])
        inside = jnp.sum(d_probs * probs, -1, keepdims=True)
        d_scores = (probs * (d_probs - inside)).astype(BF16)
        part = (from_heads(mm(d_scores, keys)) * HEAD_DIM ** (-0.5)).astype(BF16)
        return mm_tn(chosen, part), mm_tn(d_scores, queries), mm_tn(probs.astype(BF16), grad)

    trips = (base[1] - base[0]) // PART
    for pair in range(1, pairs):
        trips = jnp.maximum(trips, (base[pair + 1] - base[pair]) // PART)
    for pair in range(pairs):
        mine = slice(pair * seq, (pair + 1) * seq)
        for ref, value in zip((d_query, d_keys, d_values), pair_part(pair, 0)):
            ref[mine, :] = value

    @pl.loop(1, trips)
    def _(b):
        for pair in range(pairs):
            mine = slice(pair * seq, (pair + 1) * seq)
            for ref, value in zip((d_query, d_keys, d_values), pair_part(pair, b)):
                ref[mine, :] += value

    for part, ref in enumerate((d_query, d_keys, d_values)):
        low = ref[...].astype(BF16)
        d_qkv[:, part * width : (part + 1) * width] = low
        if part != 1:
            row = 0 if part == 0 else 1
            sums[row : row + 1, :] = column_sum(low.astype(F32))
    d_qkv_copy = pltpu.make_async_copy(d_qkv, d_qkv_out, more.at[1])
    d_qkv_copy.start()
    column_form = jnp.broadcast_to(inner_sum[...], (8, inner_sum.shape[1])).T
    quarters = inner_sum.shape[1] // width
    block = jnp.concatenate([sums[...], jnp.zeros((128 - sums.shape[0], width), F32)], 0).T
    lane = lax.broadcasted_iota(jnp.int32, block.shape, 1)
    for k in range(quarters):
        starts = [(s * quarters + k) * shard_rows for s in range(width // shard_rows)]
        column = jnp.concatenate([column_form[s : s + shard_rows, :1] for s in starts], 0)
        block = jnp.where(lane == 8 + k, column, block)
    total[:, :128] = block
    spread(
        jnp.concatenate(
            [total[pl.ds(pl.multiple_of(order[i] * rows, 8), rows), :128] for i in range(BLOCKS)], 0
        ),
        4 * width,
        128,
    )
    for part in range(3):
        columns = slice(part * width, (part + 1) * width)
        spread(mm(tokens_turned[...], d_qkv[:, columns]), part * width, width)
    for copy in outs + [d_qkv_copy, d_r1_copy]:
        copy.wait()


def input_grad_kernel(count, seq, *refs):
    offsets, base = refs[:2]
    pieces = refs[2 : 2 + count]
    d_qkv, d_r1, pos, out, weights, sems = refs[2 + count :]
    step = pl.program_id(0)

    @pl.when(step == 0)
    def _():
        for copy in start_pieces(pieces, offsets, weights, sems):
            copy.wait()

    value = mm_nt(d_qkv[...], weights[...])
    for k in range(STEP // seq):
        pair = step * (STEP // seq) + k
        start = window_start(base[pair])
        chosen = selector(pos[pair], start, seq)
        rows = slice(k * seq, (k + 1) * seq)
        out[rows, :] = value[rows] + mm_tn(chosen, d_r1[pl.ds(start, WINDOW), :])


def swap(value, bit):
    return lax.ppermute(value, "shard", [(i, i ^ bit) for i in range(8)])


def after(value, *others):
    return lax.optimization_barrier((value,) + others)[0]


def with_core(pieces):
    return pieces + [(swap(v, CORE), key | CORE, row) for v, key, row in pieces]


class Sum:
    def __init__(self, keep, send, early=False):
        self.keep, self.early = keep, early
        self.got = swap(send, CORE)
        self.extra = None
        z = lax.axis_index("rep")
        self.ends = (z == 0) | (z == 3)

    def wait(self, names, others):
        values = tuple(getattr(self, name) for name in names)
        got = lax.optimization_barrier(values + tuple(others))
        for name, value in zip(names, got):
            setattr(self, name, value)

    def chip(self, block, bottom):
        if self.early:
            half = self.mine.shape[1] // 2
            rows = slice(half, None) if bottom else slice(0, half)
            return self.mine[block, rows].astype(F32) + self.extra[block, rows].astype(F32)
        half = self.keep.shape[1] // 2
        rows = slice(half, None) if bottom else slice(0, half)
        return self.keep[block, rows].astype(F32) + self.got[block, rows].astype(F32)

    def rep_early(self, *others):
        self.wait(("keep", "got"), others)
        half = self.keep.shape[1] // 2
        a = self.keep[:, :half].astype(F32) + self.got[:, :half].astype(F32)
        b = self.keep[:, half:].astype(F32) + self.got[:, half:].astype(F32)
        sent = jnp.where(self.ends, b, a).astype(BF16)
        self.mine = jnp.where(self.ends, a, b).astype(BF16)
        self.extra = lax.ppermute(sent, "rep", PAIRS)
        return (sent,)

    def near(self, *others):
        self.wait(("mine", "extra") if self.early else ("keep", "got"), others)
        sent = self.chip(slice(1, 3), False).astype(BF16), self.chip(slice(2, 4), True).astype(BF16)
        self.got_a, self.got_b = swap(sent[0], XBIT), swap(sent[1], YBIT)
        return sent

    def far(self, *others):
        self.wait(("got_a", "got_b"), others)
        send_a = (self.chip(3, False) + self.got_a[1].astype(F32)).astype(BF16)
        send_b = (self.chip(1, True) + self.got_b[0].astype(F32)).astype(BF16)
        self.far_a, self.far_b = swap(send_a, YBIT), swap(send_b, XBIT)
        return send_a, send_b

    def halves(self):
        a = self.chip(0, False) + self.got_a[0].astype(F32) + self.far_a.astype(F32)
        b = self.chip(0, True) + self.got_b[1].astype(F32) + self.far_b.astype(F32)
        return a, b

    def rep_first(self, *others):
        self.wait(("far_a", "far_b"), others)
        a, b = self.halves()
        sent = jnp.where(self.ends, b, a).astype(BF16)
        self.total = jnp.where(self.ends, a, b)
        self.across = lax.ppermute(sent, "rep", PAIRS)
        return (sent,)

    def rep_second(self, *others):
        if self.early:
            self.wait(("far_a", "far_b"), others)
            self.total = jnp.concatenate(self.halves(), 0)
        else:
            self.wait(("across",), others)
            self.total = self.total + self.across.astype(F32)
        sent = self.total.astype(BF16)
        self.across = lax.ppermute(sent, "rep", ACROSS)
        return (sent,)

    def rep_third(self, *others):
        self.wait(("across",), others)
        self.low = (self.total + self.across.astype(F32)).astype(BF16)
        self.other = lax.ppermute(self.low, "rep", PAIRS)
        return (self.low,)

    def done(self):
        top = jnp.where(self.ends, self.low, self.other)
        bottom = jnp.where(self.ends, self.other, self.low)
        return jnp.concatenate([top, bottom], 0).astype(F32)


PAIRS = [(0, 1), (1, 0), (2, 3), (3, 2)]
ACROSS = [(0, 3), (3, 0), (1, 2), (2, 1)]


def whole(shape, dtype=None):
    del dtype
    return pl.BlockSpec(shape, lambda *_: (0,) * len(shape))


def steps(width):
    return pl.BlockSpec((STEP, width), lambda i: (i, 0))


SCALARS = pl.BlockSpec(memory_space=pltpu.SMEM)
ANYWHERE = pl.BlockSpec(memory_space=pl.ANY)


def shape_of(*dims, dtype=BF16):
    return jax.ShapeDtypeStruct(dims, dtype)


def params():
    return pltpu.CompilerParams(vmem_limit_bytes=VMEM)


def cost(time):
    return pl.CostEstimate(flops=int(time * 1.15e+09), bytes_accessed=0, transcendentals=0)


def local(
    tokens,
    word_counts,
    region_counts,
    task_labels,
    masked_slots,
    qkv_weight,
    query_bias,
    value_bias,
    out_weight,
    out_bias,
    attn_gain,
    attn_shift,
    inner_weight,
    inner_bias,
    back_weight,
    back_bias,
    ffn_gain,
    ffn_shift,
    cotangent,
    *,
    shards,
    reps,
):
    pairs = word_counts.shape[0]
    count, width = tokens.shape
    hidden = back_weight.shape[0] * shards
    seq = count // pairs
    grid = (count // STEP,)
    cap = -(-pairs * WINDOW // LIVE) * LIVE
    cube = shards == 8 and reps == 4
    rows = width // shards
    me = lax.axis_index("shard")

    vectors = jnp.stack(
        [query_bias, value_bias, out_bias, attn_gain, attn_shift, back_bias, ffn_gain, ffn_shift]
        + [inner_bias[k * rows : (k + 1) * rows] for k in range(hidden // width)],
        1,
    )
    vectors = jnp.pad(vectors, ((0, 0), (0, 128 - vectors.shape[1])))
    attn_shard = jnp.concatenate([qkv_weight, out_weight, vectors], 1)
    if cube:
        far = XBIT | YBIT
        inner_x, inner_y = swap(inner_weight, XBIT), swap(inner_weight, YBIT)
        attn_x, attn_y = swap(attn_shard, XBIT), swap(attn_shard, YBIT)
        near = lax.optimization_barrier((inner_x, inner_y, attn_x, attn_y, back_weight))
        inner_x, inner_y, attn_x, attn_y, back_weight = near
        half = attn_shard.shape[0] // 2
        attn_far = swap(attn_y[:half], XBIT), swap(attn_x[half:], YBIT)
        back_x, back_y = swap(back_weight, XBIT), swap(back_weight, YBIT)
        attn = with_core(
            [(attn_shard, 0, 0), (attn_x, XBIT, 0), (attn_y, YBIT, 0)]
            + [(attn_far[0], far, 0), (attn_far[1], far, half)]
        )
        order = jnp.array([0, 2, 6, 4, 1, 3, 7, 5], jnp.int32) ^ me
    else:
        attn, inner, back = (
            [(lax.all_gather(v, "shard", axis=0, tiled=True), 0, 0)]
            for v in (attn_shard, inner_weight, back_weight)
        )
        order = jnp.arange(BLOCKS, dtype=jnp.int32)

    def offsets(pieces, size):
        if not cube:
            return jnp.zeros((1,), jnp.int32)
        keys = jnp.array([key for _, key, _ in pieces], jnp.int32)
        return (keys ^ me) * size + jnp.stack([jnp.int32(row) for _, _, row in pieces])

    slots = jnp.arange(seq, dtype=jnp.int32)[None, :]
    words = word_counts[:, None]
    in_regions = (slots >= WORD_SLOTS) & (slots < WORD_SLOTS + region_counts[:, None])
    picked = masked_slots == 1
    labels = task_labels[:, None]
    live = (
        (labels == 0) & picked & (slots >= 1) & (slots < words)
        | (labels == 1) & picked & in_regions
        | (labels == 2) & (slots == 0)
    )
    live_count = jnp.sum(live.astype(jnp.int32), 1)
    taken = (live_count + PART - 1) // PART * PART
    base = jnp.concatenate([jnp.zeros((1,), jnp.int32), jnp.cumsum(taken)])
    rank = jnp.cumsum(live.astype(jnp.int32), 1) - 1 + base[:-1, None]
    pos = jnp.where(live, rank, -1).reshape(pairs, 1, seq)
    blocks = jnp.maximum(1, (base[-1:] + LIVE - 1) // LIVE)

    columns = 4 * width + 128
    attn_count = len(attn)
    attn_offsets, attn_pieces = offsets(attn, rows), [v for v, _, _ in attn]
    qkv, vector_rows = pl.pallas_call(
        functools.partial(project_kernel, attn_count),
        grid=grid,
        in_specs=[SCALARS] + [ANYWHERE] * attn_count + [steps(width)],
        out_specs=[steps(3 * width), whole((16, width))],
        out_shape=[shape_of(count, 3 * width), shape_of(16, width, dtype=F32)],
        scratch_shapes=[
            pltpu.VMEM((width, columns), BF16),
            pltpu.SemaphoreType.DMA((attn_count,)),
        ],
        compiler_params=params(),
        cost_estimate=cost(9),
        name="project",
    )(attn_offsets, *attn_pieces, tokens)
    if cube:
        back_x, back_y, inner_x, inner_y, qkv = lax.optimization_barrier(
            (back_x, back_y, inner_x, inner_y, qkv)
        )
        inner_far, back_far = swap(inner_y, XBIT), swap(back_x, YBIT)
    hidden1, compact = pl.pallas_call(
        functools.partial(attend_kernel, attn_count, seq),
        grid=grid,
        in_specs=[SCALARS] * 4
        + [ANYWHERE] * attn_count
        + [steps(width), steps(width), steps(3 * width), whole((pairs, 1, seq)), whole((16, width))],
        out_specs=[steps(width), whole((cap, columns))],
        out_shape=[shape_of(count, width, dtype=F32), shape_of(cap, columns)],
        scratch_shapes=[
            pltpu.VMEM((width, width), BF16),
            pltpu.VMEM((STEP, width), BF16),
            pltpu.SemaphoreType.DMA((attn_count,)),
        ],
        compiler_params=params(),
        cost_estimate=cost(14),
        name="attend",
    )(
        attn_offsets,
        base,
        word_counts,
        region_counts,
        *attn_pieces,
        tokens,
        cotangent,
        qkv,
        pos,
        vector_rows,
    )

    if cube:
        inner_far, back_far = lax.optimization_barrier((inner_far, back_far, hidden1))[:2]
        inner = with_core(
            [(inner_weight, 0, 0), (inner_x, XBIT, 0), (inner_y, YBIT, 0), (inner_far, far, 0)]
        )
        back = with_core(
            [(back_weight, 0, 0), (back_x, XBIT, 0), (back_y, YBIT, 0), (back_far, far, 0)]
        )
    inner_bias_full = (
        vector_rows[8 : 8 + hidden // width]
        .reshape(-1, shards, rows)
        .transpose(1, 0, 2)
        .reshape(1, hidden)
    )
    inner_count, back_count = len(inner), len(back)
    inner_offsets, inner_pieces = offsets(inner, rows), [v for v, _, _ in inner]
    back_offsets, back_pieces = offsets(back, back_weight.shape[0]), [v for v, _, _ in back]
    in_vmem = pl.BlockSpec(memory_space=pltpu.VMEM)
    live_act, live_slope = pl.pallas_call(
        functools.partial(live_inner_kernel, inner_count),
        in_specs=[SCALARS] * 2 + [ANYWHERE] * (inner_count + 1) + [in_vmem],
        out_specs=[ANYWHERE] * 2,
        out_shape=[shape_of(cap, hidden)] * 2,
        scratch_shapes=[
            pltpu.VMEM((width, hidden), BF16),
            pltpu.VMEM((LIVE, width), BF16),
            pltpu.VMEM((LIVE, hidden), BF16),
            pltpu.VMEM((LIVE, hidden), BF16),
            pltpu.SemaphoreType.DMA((inner_count,)),
            pltpu.SemaphoreType.DMA((3,)),
        ],
        compiler_params=params(),
        cost_estimate=cost(6),
        name="live_inner",
    )(inner_offsets, blocks, *inner_pieces, compact, inner_bias_full)

    half = BLOCKS // 2
    size = hidden // BLOCKS
    block = width // BLOCKS
    keep_back, send_back, keep_inner, send_inner, d_hidden1, sums, inner_sum = pl.pallas_call(
        functools.partial(ffn_back_kernel, (inner_count, back_count)),
        in_specs=[SCALARS] * 4 + [ANYWHERE] * (inner_count + back_count + 3) + [in_vmem],
        out_specs=[ANYWHERE] * 5 + [in_vmem] * 2,
        out_shape=[
            shape_of(half, size, width),
            shape_of(half, size, width),
            shape_of(half, size, width),
            shape_of(half, size, width),
            shape_of(cap, width, dtype=F32),
            shape_of(16, width, dtype=F32),
            shape_of(1, hidden, dtype=F32),
        ],
        scratch_shapes=[
            pltpu.VMEM((hidden, width), BF16),
            pltpu.VMEM((width, hidden), BF16),
            pltpu.VMEM((cap, width), BF16),
            pltpu.VMEM((cap, width), BF16),
            pltpu.VMEM((cap, hidden), BF16),
            pltpu.VMEM((cap, hidden), BF16),
            pltpu.VMEM((cap, width), BF16),
            pltpu.VMEM((cap, hidden), BF16),
            pltpu.VMEM((cap, width), F32),
            pltpu.VMEM((width, width), F32),
            pltpu.VMEM((BLOCKS, size, width), BF16),
            pltpu.VMEM((BLOCKS, size, width), BF16),
            pltpu.VMEM((width, LIVE), BF16),
            pltpu.VMEM((cap // LIVE, width, LIVE), BF16),
            pltpu.SemaphoreType.DMA((inner_count,)),
            pltpu.SemaphoreType.DMA((back_count,)),
            pltpu.SemaphoreType.DMA((12 + 2 * hidden // width,)),
        ],
        compiler_params=params(),
        cost_estimate=cost(13),
        name="ffn_back",
    )(
        inner_offsets,
        back_offsets,
        order,
        blocks,
        *inner_pieces,
        *back_pieces,
        compact,
        live_act,
        live_slope,
        vector_rows,
    )

    if cube:
        back_total = Sum(keep_back, send_back)
        inner_total = Sum(keep_inner, send_inner, early=True)

    d_qkv, d_r1, keep_attn, send_attn = pl.pallas_call(
        functools.partial(attend_back_kernel, attn_count, seq, rows),
        in_specs=[SCALARS] * 6 + [ANYWHERE] * (attn_count + 4) + [in_vmem] * 4,
        out_specs=[ANYWHERE] * 4,
        out_shape=[
            shape_of(count, 3 * width),
            shape_of(cap, width),
            shape_of(half, block, columns),
            shape_of(half, block, columns),
        ],
        scratch_shapes=[
            pltpu.VMEM((width, width), BF16),
            pltpu.VMEM((cap, width), BF16),
            pltpu.VMEM((cap, width), BF16),
            pltpu.VMEM((cap, 128), BF16),
            pltpu.VMEM((cap, width), F32),
            pltpu.VMEM((count, 3 * width), BF16),
            pltpu.VMEM((count, width), BF16),
            pltpu.VMEM((cap, width), BF16),
            pltpu.VMEM((cap, width), BF16),
            pltpu.VMEM((count, width), F32),
            pltpu.VMEM((count, width), F32),
            pltpu.VMEM((count, width), F32),
            pltpu.VMEM((count, 3 * width), BF16),
            pltpu.VMEM((width, width), F32),
            pltpu.VMEM((BLOCKS, block, columns), BF16),
            pltpu.VMEM((16, width), F32),
            pltpu.VMEM((width, count), BF16),
            pltpu.VMEM((width, LIVE), BF16),
            pltpu.VMEM((width, count), BF16),
            pltpu.SemaphoreType.DMA((attn_count,)),
            pltpu.SemaphoreType.DMA((16,)),
        ],
        compiler_params=params(),
        cost_estimate=cost(16),
        name="attend_back",
    )(
        attn_offsets,
        order,
        base,
        word_counts,
        region_counts,
        blocks,
        *attn_pieces,
        compact,
        d_hidden1,
        qkv,
        tokens,
        vector_rows,
        sums,
        inner_sum,
        pos,
    )

    def later(shift):
        return lambda i: (i + shift, 0)

    def ffn(first, x, *done):
        return pl.pallas_call(
            functools.partial(ffn_kernel, (inner_count, back_count)),
            grid=(grid[0] // 2,),
            in_specs=[SCALARS] * 2
            + [ANYWHERE] * (inner_count + back_count)
            + [pl.BlockSpec((STEP, width), later(first)), whole((1, hidden)), whole((16, width))]
            + [ANYWHERE] * len(done),
            out_specs=pl.BlockSpec((STEP, width), later(first)),
            out_shape=shape_of(count, width),
            input_output_aliases={5 + inner_count + back_count: 0} if done else {},
            scratch_shapes=[
                pltpu.VMEM((width, hidden), BF16),
                pltpu.VMEM((hidden, width), BF16),
                pltpu.VMEM((STEP, hidden), BF16),
                pltpu.SemaphoreType.DMA((inner_count,)),
                pltpu.SemaphoreType.DMA((back_count,)),
            ],
            compiler_params=params(),
            cost_estimate=cost(11),
            name="ffn",
        )(
            inner_offsets,
            back_offsets,
            *inner_pieces,
            *back_pieces,
            x,
            inner_bias_full,
            vector_rows,
            *done,
        )

    x = hidden1
    if cube:
        sent = back_total.near(d_r1)
        sent += inner_total.rep_early(*sent)
        attn_total = Sum(keep_attn, send_attn)
        sent += attn_total.near(*sent)
        x = after(hidden1, *sent)
    result = ffn(0, x)
    if cube:
        sent = back_total.far(result)
        x = after(hidden1, *sent)
    result = ffn(grid[0] // 2, x, result)
    if cube:
        sent = attn_total.far(result)
        sent += back_total.rep_first(*sent)
        sent += inner_total.near(*sent)
        sent += attn_total.rep_first(*sent)
        sent += back_total.rep_second(*sent)
        d_qkv = after(d_qkv, *sent)

    input_grad = pl.pallas_call(
        functools.partial(input_grad_kernel, attn_count, seq),
        grid=grid,
        in_specs=[SCALARS] * 2
        + [ANYWHERE] * attn_count
        + [steps(3 * width), whole((cap, width)), whole((pairs, 1, seq))],
        out_specs=steps(width),
        out_shape=shape_of(count, width, dtype=F32),
        scratch_shapes=[
            pltpu.VMEM((width, 3 * width), BF16),
            pltpu.SemaphoreType.DMA((attn_count,)),
        ],
        compiler_params=params(),
        cost_estimate=cost(9),
        name="input_grad",
    )(attn_offsets, base, *attn_pieces, d_qkv, d_r1, pos)

    quarters = hidden // width
    if cube:
        inner_total.far(input_grad)
        attn_total.rep_second(input_grad)
        back_total.rep_third(input_grad)
        inner_total.rep_second()
        attn_total.rep_third()
        inner_total.rep_third()
        back_sum, inner_sum, attn_sum = (v.done() for v in (back_total, inner_total, attn_total))
        inner_sum = jnp.concatenate([inner_sum[c * block : (c + 1) * block] for c in range(quarters)], 1)
    else:
        back_grad = jnp.concatenate([keep_back, send_back]).reshape(hidden, width)
        inner_grad = jnp.concatenate([keep_inner, send_inner]).reshape(BLOCKS, quarters, block, width)
        inner_grad = inner_grad.transpose(0, 2, 1, 3).reshape(width, hidden)
        attn_grad = jnp.concatenate([keep_attn, send_attn]).reshape(width, columns)
        back_sum, inner_sum, attn_sum = (
            lax.psum(lax.psum_scatter(g, "shard", scatter_dimension=0, tiled=True), "rep").astype(F32)
            for g in (back_grad, inner_grad, attn_grad)
        )
    sums = attn_sum[:, 4 * width :].T
    return (
        result,
        input_grad,
        attn_sum[:, : 3 * width],
        sums[0],
        sums[1],
        attn_sum[:, 3 * width : 4 * width],
        sums[2],
        sums[3],
        sums[4],
        inner_sum,
        sums[8 : 8 + quarters].reshape(-1),
        back_sum,
        sums[5],
        sums[6],
        sums[7],
    )


def solution(mesh):
    rows, both, one = P(("rep", "shard"), None), P(("rep", "shard")), P("shard")
    matrix = P("shard", None)
    in_specs = (rows, both, both, both, rows, matrix, one, one, matrix, one, one, one)
    in_specs += (matrix, one, matrix, one, one, one, rows)
    out_specs = (rows, rows, matrix, one, one, matrix, one, one, one, matrix, one, matrix)
    out_specs += (one, one, one)
    sizes = dict(mesh.shape)

    def run(*args):
        return local(*args, shards=sizes["shard"], reps=sizes["rep"])

    return jax.shard_map(
        run, mesh=mesh, in_specs=in_specs, out_specs=out_specs, check_vma=False
    )
```

```python
import functools

import jax
import jax.numpy as jnp
from jax import lax
from jax.experimental import pallas as pl
from jax.experimental.pallas import tpu as pltpu
from jax.sharding import PartitionSpec as P

HEADS = 12
HEAD_DIM = 64
WORD_SLOTS = 60
CORE, XBIT, YBIT = 1, 2, 4
BLOCKS = 8
STEP = 256
LIVE = 192
WINDOW = 80
PART = 16
TOGETHER = 2
VMEM = 60 * 2**20
F32 = jnp.float32
BF16 = jnp.bfloat16


def mm(left, right):
    return jnp.dot(left, right, preferred_element_type=F32)


def mm_nt(left, right):
    return lax.dot_general(left, right, (((1,), (1,)), ((), ())), preferred_element_type=F32)


def mm_tn(left, right):
    return lax.dot_general(left, right, (((0,), (0,)), ((), ())), preferred_element_type=F32)


def norm_parts(value):
    mean = jnp.mean(value, -1, keepdims=True)
    centred = value - mean
    scale = lax.rsqrt(jnp.mean(centred * centred, -1, keepdims=True) + 1e-05)
    return centred * scale, scale


def norm_grad(grad, normed, scale):
    return scale * (
        grad
        - jnp.mean(grad, -1, keepdims=True)
        - normed * jnp.mean(grad * normed, -1, keepdims=True)
    )


def column_sum(value):
    return jnp.sum(value, 0, keepdims=True)


def start_pieces(pieces, offsets, scratch, sems, first=0, started=False):
    copies = []
    for j, piece in enumerate(pieces):
        start = pl.multiple_of(offsets[j], 16)
        source = piece.at[:, pl.ds(first, scratch.shape[1])]
        target = scratch.at[pl.ds(start, piece.shape[0]), :]
        copies.append(pltpu.make_async_copy(source, target, sems.at[j]))
        if not started:
            copies[-1].start()
    return copies


def stacked(block):
    lane = lax.broadcasted_iota(jnp.int32, block.shape, 1)
    zero = jnp.zeros_like(block)
    return jnp.concatenate(
        [jnp.where(lane < HEAD_DIM, block, zero), jnp.where(lane >= HEAD_DIM, block, zero)], 0
    )


def unstacked(block):
    rows = block.shape[0] // 2
    lane = lax.broadcasted_iota(jnp.int32, (rows, block.shape[1]), 1)
    return jnp.where(lane < HEAD_DIM, block[:rows], block[rows:])


def probabilities(queries, keys, valid):
    scores = jnp.where(valid, mm_nt(queries, keys), -1000000000.0)
    peak = jnp.max(scores, -1, keepdims=True)
    expo = jnp.exp(scores - peak)
    return expo * (1.0 / jnp.sum(expo, -1, keepdims=True))


def valid_slots(words, regions, seq):
    slot = lax.broadcasted_iota(jnp.int32, (1, seq), 1)
    return (slot < words) | ((slot >= WORD_SLOTS) & (slot < WORD_SLOTS + regions))


def selector(pos, start, seq):
    row = lax.broadcasted_iota(jnp.int32, (WINDOW, seq), 0) + start
    return jnp.where(row == pos, 1.0, 0.0).astype(BF16)


def window_start(base):
    return pl.multiple_of(base, PART)


def project_kernel(count, shard_rows, *refs):
    offsets = refs[0]
    pieces = refs[1 : 1 + count]
    tokens, qkv, vectors, bias, weights, sems = refs[1 + count :]
    width = tokens.shape[1]
    quarters = bias.shape[1] // width

    @pl.when(pl.program_id(0) == 0)
    def _():
        for copy in start_pieces(pieces, offsets, weights, sems):
            copy.wait()
        share = weights[:, 4 * width :].astype(F32)
        vectors[...] = share.T[: vectors.shape[0]]
        parts = []
        for s in range(width // shard_rows):
            for k in range(quarters):
                part = share[s * shard_rows : (s + 1) * shard_rows, 8 + k : 9 + k]
                parts.append(jnp.broadcast_to(part, (shard_rows, 8)))
        bias[...] = jnp.concatenate(parts, 0).T[:1]

    x = tokens[...]
    for part, row in ((0, 0), (1, None), (2, 1)):
        columns = slice(part * width, (part + 1) * width)
        value = mm(x, weights[:, columns])
        if row is not None:
            value = value + vectors[row : row + 1, :]
        qkv[:, columns] = value.astype(BF16)


def attend_kernel(count, seq, *refs):
    offsets, base, words, regions = refs[:4]
    pieces = refs[4 : 4 + count]
    tokens, cotangent, qkv, pos, vectors, hidden, compact, proj, mixed, sems = refs[4 + count :]
    width = tokens.shape[1]
    step = pl.program_id(0)

    @pl.when(step == 0)
    def _():
        copies = start_pieces(pieces, offsets, proj, sems, 3 * width)
        compact[...] = jnp.zeros_like(compact)
        for copy in copies:
            copy.wait()

    for k in range(STEP // seq):
        rows = slice(k * seq, (k + 1) * seq)
        pair = step * (STEP // seq) + k
        valid = valid_slots(words[pair], regions[pair], seq)
        for h in range(HEADS // 2):
            lanes = slice(h * 128, (h + 1) * 128)
            queries = stacked(qkv[rows, lanes] * HEAD_DIM ** (-0.5))
            keys = qkv[rows, width + h * 128 : width + (h + 1) * 128]
            values = qkv[rows, 2 * width + h * 128 : 2 * width + (h + 1) * 128]
            scores = jnp.where(valid, mm_nt(queries, keys), -1000000000.0)
            expo = jnp.exp(scores - jnp.max(scores, -1, keepdims=True)).astype(BF16)
            both = mm(expo, jnp.concatenate([values, jnp.ones_like(values)], 1))
            mixed[rows, lanes] = (unstacked(both[:, :128]) / unstacked(both[:, 128:])).astype(BF16)
    branch = mm(mixed[...], proj[...]) + vectors[2:3, :]
    normed, scale = norm_parts(tokens[...].astype(F32) + branch)
    value = normed * vectors[3:4, :] + vectors[4:5, :]
    hidden[...] = value
    high = scale.astype(BF16)
    rest = scale - high.astype(F32)
    middle = rest.astype(BF16)
    low = (rest - middle.astype(F32)).astype(BF16)
    lane = lax.broadcasted_iota(jnp.int32, (STEP, 128), 1)
    zero = jnp.zeros((STEP, 128), BF16)
    scales = jnp.where(lane == 0, high, jnp.where(lane == 1, middle, jnp.where(lane == 2, low, zero)))
    parts = (value.astype(BF16), normed.astype(BF16), mixed[...], cotangent[...], scales)
    for k in range(STEP // seq):
        pair = step * (STEP // seq) + k
        start = window_start(base[pair])
        chosen = selector(pos[pair], start, seq)
        at = 0
        for part in parts:
            columns = slice(at, at + part.shape[1])
            at += part.shape[1]
            got = mm(chosen, part[k * seq : (k + 1) * seq]).astype(BF16)
            compact[pl.ds(start, WINDOW), columns] = got


def gelu_parts(inner):
    cumul = 0.5 + 0.5 * lax.erf(inner * 0.7071067811865476)
    return inner * cumul, cumul


def live_inner_kernel(count, *refs):
    offsets, blocks = refs[:2]
    pieces = refs[2 : 2 + count]
    compact, bias, act_out, slope_out = refs[2 + count : 6 + count]
    weights, hidden, act, slope, sems, more = refs[6 + count :]
    width = hidden.shape[1]
    copies = start_pieces(pieces, offsets, weights, sems)
    count_live = blocks[0]

    def rows_of(b):
        return pl.ds(pl.multiple_of(b * LIVE, LIVE), LIVE)

    def load(b):
        return pltpu.make_async_copy(compact.at[rows_of(b), pl.ds(0, width)], hidden, more.at[0])

    load(0).start()
    for copy in copies:
        copy.wait()

    @pl.loop(0, count_live)
    def _(b):
        load(b).wait()
        x = hidden[...]
        for c in range(weights.shape[1] // width):
            columns = slice(c * width, (c + 1) * width)
            inner = mm(x, weights[:, columns]) + bias[:, columns]
            value, cumul = gelu_parts(inner)
            density = jnp.exp(-0.5 * inner * inner) * 0.3989422804014327
            act[:, columns] = value.astype(BF16)
            slope[:, columns] = (cumul + inner * density).astype(BF16)
        outs = [
            pltpu.make_async_copy(act, act_out.at[rows_of(b)], more.at[1]),
            pltpu.make_async_copy(slope, slope_out.at[rows_of(b)], more.at[2]),
        ]
        for copy in outs:
            copy.start()

        @pl.when(b + 1 < count_live)
        def _():
            load(b + 1).start()

        for copy in outs:
            copy.wait()


def ffn_kernel(counts, *refs):
    inner_offsets, back_offsets = refs[:2]
    inner_pieces = refs[2 : 2 + counts[0]]
    back_pieces = refs[2 + counts[0] : 2 + counts[0] + counts[1]]
    hidden, bias, vectors = refs[2 + sum(counts) : 5 + sum(counts)]
    result, inner, back, act, inner_sems, back_sems = refs[-6:]
    width = hidden.shape[1]
    step = pl.program_id(0)

    @pl.when(step == 0)
    def _():
        copies = start_pieces(inner_pieces, inner_offsets, inner, inner_sems)
        start_pieces(back_pieces, back_offsets, back, back_sems)
        for copy in copies:
            copy.wait()

    x = hidden[...]
    low = x.astype(BF16)
    for c in range(inner.shape[1] // width):
        columns = slice(c * width, (c + 1) * width)
        value = mm(low, inner[:, columns]) + bias[:, columns]
        act[:, columns] = gelu_parts(value)[0].astype(BF16)

    @pl.when(step == 0)
    def _():
        for copy in start_pieces(back_pieces, back_offsets, back, back_sems, started=True):
            copy.wait()

    second = mm(act[...], back[...]) + vectors[5:6, :]
    normed, _ = norm_parts(x + second)
    result[...] = (normed * vectors[6:7, :] + vectors[7:8, :]).astype(BF16)


def rows_of(b):
    return pl.ds(pl.multiple_of(b * LIVE, LIVE), LIVE)


def load_live(count_live, pairs, sems):
    def copies(b):
        here = rows_of(b)
        return [
            pltpu.make_async_copy(source(here), target.at[here], sems.at[j])
            for j, (source, target) in enumerate(pairs)
        ]

    for copy in copies(0):
        copy.start()

    def finish():
        for copy in copies(0):
            copy.wait()

        @pl.loop(1, count_live)
        def _(b):
            later = copies(b)
            for copy in later:
                copy.start()
            for copy in later:
                copy.wait()

    return finish


def store_live(count_live, pairs, sems):
    def copies(b):
        here = rows_of(b)
        return [
            pltpu.make_async_copy(source.at[here], target.at[here], sems.at[j])
            for j, (source, target) in enumerate(pairs)
        ]

    for copy in copies(0):
        copy.start()

    def finish():
        for copy in copies(0):
            copy.wait()

        @pl.loop(1, count_live)
        def _(b):
            later = copies(b)
            for copy in later:
                copy.start()
            for copy in later:
                copy.wait()

    return finish


def ffn_back_kernel(counts, *refs):
    inner_offsets, back_offsets, order, blocks = refs[:4]
    inner_pieces = refs[4 : 4 + counts[0]]
    back_pieces = refs[4 + counts[0] : 4 + sum(counts)]
    refs = refs[4 + sum(counts) :]
    compact_hbm, act_hbm, slope_hbm, vectors = refs[:4]
    keep_back, send_back, keep_inner, send_inner, d_hidden_out, sums, inner_sum = refs[4:11]
    back, inner, hidden, cotangent, act, slope, d_second, d_inner, d_hidden = refs[11:20]
    total, out_back, out_inner, turned, ordered, inner_sems, back_sems, more = refs[20:]
    width = inner.shape[0]
    size = inner.shape[1] // BLOCKS
    quarters = inner.shape[1] // width
    rows = width // BLOCKS
    half = BLOCKS // 2
    first = slice(0, LIVE)
    count_live = blocks[0]

    def live_copies(b):
        here = rows_of(b)
        return [
            pltpu.make_async_copy(compact_hbm.at[here, pl.ds(0, width)], hidden.at[here], more.at[0]),
            pltpu.make_async_copy(
                compact_hbm.at[here, pl.ds(3 * width, width)], cotangent.at[here], more.at[1]
            ),
            pltpu.make_async_copy(act_hbm.at[here], act.at[here], more.at[2]),
            pltpu.make_async_copy(slope_hbm.at[here], slope.at[here], more.at[3]),
        ]

    now = live_copies(0)
    for copy in now:
        copy.start()
    back_copies = start_pieces(back_pieces, back_offsets, back, back_sems)
    inner_copies = start_pieces(inner_pieces, inner_offsets, inner, inner_sems)
    sums[...] = jnp.zeros_like(sums)
    inner_sum[...] = jnp.zeros_like(inner_sum)
    for copy in now:
        copy.wait()

    @pl.loop(1, count_live)
    def _(b):
        later = live_copies(b)
        for copy in later:
            copy.start()
        for copy in later:
            copy.wait()

    for copy in back_copies:
        copy.wait()

    @pl.loop(0, count_live)
    def _(b):
        here = rows_of(b)
        second = mm(act[here, :], back[...]) + vectors[5:6, :]
        normed, scale = norm_parts(hidden[here, :].astype(F32) + second)
        d_out = cotangent[here, :].astype(F32)
        sums[6:7, :] += column_sum(d_out * normed)
        sums[7:8, :] += column_sum(d_out)
        d_r2 = norm_grad(d_out * vectors[6:7, :], normed, scale)
        low = d_r2.astype(BF16)
        d_second[here, :] = low
        sums[5:6, :] += column_sum(low.astype(F32))
        d_hidden[here, :] = d_r2

    single = count_live == 1
    outs = []
    for i in range(BLOCKS):
        chunk = pl.ds(pl.multiple_of(order[i] * size, 128), size)

        @pl.when(single)
        def _():
            out_back[i] = mm_tn(act[first, chunk], d_second[first, :]).astype(BF16)

        @pl.when(jnp.logical_not(single))
        def _():
            total[:size, :] = mm_tn(act[first, chunk], d_second[first, :])

            @pl.loop(1, count_live)
            def _(b):
                here = rows_of(b)
                total[:size, :] += mm_tn(act[here, chunk], d_second[here, :])

            out_back[i] = total[:size, :].astype(BF16)

        target = keep_back.at[i] if i < half else send_back.at[i - half]
        outs.append(pltpu.make_async_copy(out_back.at[i], target, more.at[4 + i]))
        outs[-1].start()
    for copy in inner_copies:
        copy.wait()

    @pl.loop(0, count_live)
    def _(b):
        here = rows_of(b)
        grad = d_second[here, :]
        for c in range(quarters):
            columns = slice(c * width, (c + 1) * width)
            d_act = mm_nt(grad, back[columns, :])
            low = (d_act * slope[here, columns].astype(F32)).astype(BF16)
            d_inner[here, columns] = low
            inner_sum[:, columns] += column_sum(low.astype(F32))
            d_hidden[here, :] += mm_nt(low, inner[:, columns])

    def hidden_copy(b):
        return pltpu.make_async_copy(
            d_hidden.at[rows_of(b)], d_hidden_out.at[rows_of(b)], more.at[0]
        )

    hidden_copy(0).start()

    @pl.loop(0, count_live)
    def _(b):
        here = rows_of(b)
        turned[...] = hidden[here, :].T
        for i in range(BLOCKS):
            start = pl.multiple_of(order[i] * rows, 16)
            ordered[b, i * rows : (i + 1) * rows, :] = turned[pl.ds(start, rows), :]

    for c in range(quarters):
        columns = slice(c * width, (c + 1) * width)
        target = slice(c * rows, (c + 1) * rows)

        @pl.when(single)
        def _():
            value = mm(ordered[0], d_inner[first, columns]).astype(BF16)
            for i in range(BLOCKS):
                out_inner[i, target, :] = value[i * rows : (i + 1) * rows, :]

        @pl.when(jnp.logical_not(single))
        def _():
            total[...] = mm(ordered[0], d_inner[first, columns])

            @pl.loop(1, count_live)
            def _(b):
                total[...] += mm(ordered[b], d_inner[rows_of(b), columns])

            for i in range(BLOCKS):
                out_inner[i, target, :] = total[i * rows : (i + 1) * rows, :].astype(BF16)

        for j, out in enumerate((keep_inner, send_inner)):
            blocks_out = pl.ds(j * half, half)
            part = pl.ds(c * rows, rows)
            source = out_inner.at[blocks_out, part]
            outs.append(pltpu.make_async_copy(source, out.at[:, part], more.at[12 + 2 * c + j]))
            outs[-1].start()
    hidden_copy(0).wait()

    @pl.loop(1, count_live)
    def _(b):
        hidden_copy(b).start()
        hidden_copy(b).wait()

    for copy in outs:
        copy.wait()


def by_head(block):
    lane = lax.broadcasted_iota(jnp.int32, block.shape, 1) // HEAD_DIM
    zero = jnp.zeros_like(block)
    return jnp.concatenate([jnp.where(lane == h, block, zero) for h in range(HEADS)], 0)


def from_heads(block):
    rows = block.shape[0] // HEADS
    lane = lax.broadcasted_iota(jnp.int32, (rows, 128), 1)
    parts = []
    for h in range(HEADS // 2):
        lanes = slice(h * 128, (h + 1) * 128)
        left = block[2 * h * rows : (2 * h + 1) * rows, lanes]
        right = block[(2 * h + 1) * rows : (2 * h + 2) * rows, lanes]
        parts.append(jnp.where(lane < HEAD_DIM, left, right))
    return jnp.concatenate(parts, 1)


def attend_back_kernel(count, seq, shard_rows, *refs):
    offsets, order, base, words, regions, blocks = refs[:6]
    pieces = refs[6 : 6 + count]
    refs = refs[6 + count :]
    compact, d_hidden_hbm, qkv_hbm, tokens_hbm, vectors, ffn_sums, inner_sum, pos = refs[:8]
    d_qkv_out, d_r1_out, keep_out, send_out = refs[8:12]
    weights, normed_in, mixed, scales, d_hidden, qkv, tokens, d_r1, d_mixed = refs[12:21]
    d_query, d_keys, d_values, d_qkv, total, out, sums = refs[21:28]
    turned, mixed_turned, tokens_turned, sems, more = refs[28:]
    width = weights.shape[0]
    rows = width // BLOCKS
    half = BLOCKS // 2
    pairs = pos.shape[0]
    count_live = blocks[0]

    loads = [
        (lambda here: compact.at[here, pl.ds(width, width)], normed_in),
        (lambda here: compact.at[here, pl.ds(2 * width, width)], mixed),
        (lambda here: compact.at[here, pl.ds(4 * width, 128)], scales),
        (lambda here: d_hidden_hbm.at[here], d_hidden),
    ]
    loaded = load_live(count_live, loads, more)
    weight_copies = start_pieces(pieces, offsets, weights, sems, 3 * width)
    qkv_copy = pltpu.make_async_copy(qkv_hbm, qkv, more.at[4])
    tokens_copy = pltpu.make_async_copy(tokens_hbm, tokens, more.at[5])
    qkv_copy.start()
    tokens_copy.start()
    d_r1[...] = jnp.zeros_like(d_r1)
    sums[...] = ffn_sums[...]
    loaded()
    for copy in weight_copies:
        copy.wait()

    @pl.loop(0, count_live)
    def _(b):
        here = rows_of(b)
        grad = d_hidden[here, :]
        normed = normed_in[here, :].astype(F32)
        scale = jnp.sum(scales[here, :].astype(F32), -1, keepdims=True)
        sums[3:4, :] += column_sum(grad * normed)
        sums[4:5, :] += column_sum(grad)
        low = norm_grad(grad * vectors[3:4, :], normed, scale).astype(BF16)
        sums[2:3, :] += column_sum(low.astype(F32))
        d_r1[here, :] = low
        d_mixed[here, :] = mm_nt(low, weights[...]).astype(BF16)

    def in_order(source, target):
        turned[:, : source.shape[0]] = source.T
        for i in range(BLOCKS):
            start = pl.multiple_of(order[i] * rows, 16)
            target[i * rows : (i + 1) * rows, :] = turned[pl.ds(start, rows), : source.shape[0]]

    outs = []

    def spread(value, first, size):
        low = value.astype(BF16)
        for i in range(BLOCKS):
            out[i, :, first : first + size] = low[i * rows : (i + 1) * rows, :size]
        columns = pl.ds(first, size)
        for j, target in enumerate((keep_out, send_out)):
            source = out.at[pl.ds(j * half, half), :, columns]
            sem = more.at[6 + len(outs)]
            outs.append(pltpu.make_async_copy(source, target.at[:, :, columns], sem))
            outs[-1].start()

    in_order(mixed[:LIVE, :], mixed_turned)

    @pl.when(count_live == 1)
    def _():
        total[...] = mm(mixed_turned[...], d_r1[:LIVE, :])

    @pl.when(count_live > 1)
    def _():
        total[...] = mm(mixed_turned[...], d_r1[:LIVE, :])

        @pl.loop(1, count_live)
        def _(b):
            here = rows_of(b)
            in_order(mixed[here, :], mixed_turned)
            total[...] += mm(mixed_turned[...], d_r1[here, :])

    spread(total[...], 3 * width, width)
    tokens_copy.wait()
    in_order(tokens[...], tokens_turned)
    qkv_copy.wait()

    def pair_part(pair, b):
        mine = pl.ds(pl.multiple_of(pair * seq, seq), seq)
        valid = valid_slots(words[pair], regions[pair], seq)
        first = pl.multiple_of(base[pair] + b * PART, PART)
        row = lax.broadcasted_iota(jnp.int32, (PART, seq), 0) + first
        chosen = jnp.where(row == pos[pair], 1.0, 0.0).astype(BF16)
        live_query = mm(chosen, qkv[mine, :width]).astype(BF16) * HEAD_DIM ** (-0.5)
        queries = by_head(live_query)
        grad = d_mixed[pl.ds(first, PART), :]
        row = lax.broadcasted_iota(jnp.int32, grad.shape, 0) + first
        grad = by_head(jnp.where(row < base[pair + 1], grad, jnp.zeros_like(grad)))
        keys = qkv[mine, width : 2 * width]
        probs = probabilities(queries, keys, valid)
        d_probs = mm_nt(grad, qkv[mine, 2 * width :])
        inside = jnp.sum(d_probs * probs, -1, keepdims=True)
        d_scores = (probs * (d_probs - inside)).astype(BF16)
        part = (from_heads(mm(d_scores, keys)) * HEAD_DIM ** (-0.5)).astype(BF16)
        return mm_tn(chosen, part), mm_tn(d_scores, queries), mm_tn(probs.astype(BF16), grad)

    @pl.loop(0, pairs // TOGETHER)
    def _(step):
        group = [step * TOGETHER + k for k in range(TOGETHER)]
        trips = (base[group[0] + 1] - base[group[0]]) // PART
        for pair in group[1:]:
            trips = jnp.maximum(trips, (base[pair + 1] - base[pair]) // PART)
        for k, pair in enumerate(group):
            for ref, value in zip((d_query, d_keys, d_values), pair_part(pair, 0)):
                ref[k] = value

        @pl.loop(1, trips)
        def _(b):
            for k, pair in enumerate(group):
                for ref, value in zip((d_query, d_keys, d_values), pair_part(pair, b)):
                    ref[k] += value

        for k, pair in enumerate(group):
            mine = pl.ds(pl.multiple_of(pair * seq, seq), seq)
            for part, ref in enumerate((d_query, d_keys, d_values)):
                low = ref[k].astype(BF16)
                d_qkv[mine, part * width : (part + 1) * width] = low
                if part != 1:
                    row = 0 if part == 0 else 1
                    sums[row : row + 1, :] += column_sum(low.astype(F32))

    column_form = jnp.broadcast_to(inner_sum[...], (8, inner_sum.shape[1])).T
    quarters = inner_sum.shape[1] // width
    block = jnp.concatenate([sums[...], jnp.zeros((128 - sums.shape[0], width), F32)], 0).T
    lane = lax.broadcasted_iota(jnp.int32, block.shape, 1)
    for k in range(quarters):
        starts = [(s * quarters + k) * shard_rows for s in range(width // shard_rows)]
        column = jnp.concatenate([column_form[s : s + shard_rows, :1] for s in starts], 0)
        block = jnp.where(lane == 8 + k, column, block)
    total[:, :128] = block
    spread(
        jnp.concatenate(
            [total[pl.ds(pl.multiple_of(order[i] * rows, 8), rows), :128] for i in range(BLOCKS)], 0
        ),
        4 * width,
        128,
    )
    for part in range(3):
        columns = slice(part * width, (part + 1) * width)
        spread(mm(tokens_turned[...], d_qkv[:, columns]), part * width, width)

    outs += [
        pltpu.make_async_copy(d_qkv, d_qkv_out, more.at[6 + len(outs)]),
        pltpu.make_async_copy(d_r1, d_r1_out, more.at[7 + len(outs)]),
    ]
    outs[-2].start()
    outs[-1].start()
    for copy in outs:
        copy.wait()


def input_grad_kernel(count, seq, *refs):
    offsets, base = refs[:2]
    pieces = refs[2 : 2 + count]
    d_qkv, d_r1, pos, out, weights, sems = refs[2 + count :]
    step = pl.program_id(0)

    @pl.when(step == 0)
    def _():
        for copy in start_pieces(pieces, offsets, weights, sems):
            copy.wait()

    value = mm_nt(d_qkv[...], weights[...])
    for k in range(STEP // seq):
        pair = step * (STEP // seq) + k
        start = window_start(base[pair])
        chosen = selector(pos[pair], start, seq)
        rows = slice(k * seq, (k + 1) * seq)
        out[rows, :] = value[rows] + mm_tn(chosen, d_r1[pl.ds(start, WINDOW), :])


def swap(value, bit):
    return lax.ppermute(value, "shard", [(i, i ^ bit) for i in range(8)])


def after(value, *others):
    return lax.optimization_barrier((value,) + others)[0]


def far_swap(by_x, by_y):
    half = by_x.shape[0] // 2
    return swap(by_y[:half], XBIT), swap(by_x[half:], YBIT)


def near_and_far(mine, by_x, by_y, by_both):
    far = XBIT | YBIT
    half = mine.shape[0] // 2
    near = [(mine, 0, 0), (by_x, XBIT, 0), (by_y, YBIT, 0)]
    return near + [(by_both[0], far, 0), (by_both[1], far, half)]


def with_core(pieces, others):
    return pieces + [(v, key | CORE, row) for v, (_, key, row) in zip(others, pieces)]


class Sum:
    def __init__(self, keep, send, early=False):
        self.keep, self.early = keep, early
        self.got = swap(send, CORE)
        self.extra = None
        z = lax.axis_index("rep")
        self.ends = (z == 0) | (z == 3)

    def wait(self, names, others):
        values = tuple(getattr(self, name) for name in names)
        got = lax.optimization_barrier(values + tuple(others))
        for name, value in zip(names, got):
            setattr(self, name, value)

    def chip(self, block, bottom):
        if self.early:
            half = self.mine.shape[1] // 2
            rows = slice(half, None) if bottom else slice(0, half)
            return self.mine[block, rows].astype(F32) + self.extra[block, rows].astype(F32)
        half = self.keep.shape[1] // 2
        rows = slice(half, None) if bottom else slice(0, half)
        return self.keep[block, rows].astype(F32) + self.got[block, rows].astype(F32)

    def rep_early(self, *others):
        self.wait(("keep", "got"), others)
        half = self.keep.shape[1] // 2
        a = self.keep[:, :half].astype(F32) + self.got[:, :half].astype(F32)
        b = self.keep[:, half:].astype(F32) + self.got[:, half:].astype(F32)
        sent = jnp.where(self.ends, b, a).astype(BF16)
        self.mine = jnp.where(self.ends, a, b).astype(BF16)
        self.extra = lax.ppermute(sent, "rep", PAIRS)
        return (sent,)

    def near(self, *others):
        self.wait(("mine", "extra") if self.early else ("keep", "got"), others)
        sent = self.chip(slice(1, 3), False).astype(BF16), self.chip(slice(2, 4), True).astype(BF16)
        self.got_a, self.got_b = swap(sent[0], XBIT), swap(sent[1], YBIT)
        return sent

    def far(self, *others):
        self.wait(("got_a", "got_b"), others)
        send_a = (self.chip(3, False) + self.got_a[1].astype(F32)).astype(BF16)
        send_b = (self.chip(1, True) + self.got_b[0].astype(F32)).astype(BF16)
        self.far_a, self.far_b = swap(send_a, YBIT), swap(send_b, XBIT)
        return send_a, send_b

    def halves(self):
        a = self.chip(0, False) + self.got_a[0].astype(F32) + self.far_a.astype(F32)
        b = self.chip(0, True) + self.got_b[1].astype(F32) + self.far_b.astype(F32)
        return a, b

    def rep_first(self, *others):
        self.wait(("far_a", "far_b"), others)
        a, b = self.halves()
        sent = jnp.where(self.ends, b, a).astype(BF16)
        self.total = jnp.where(self.ends, a, b).astype(BF16)
        self.across = lax.ppermute(sent, "rep", PAIRS)
        return (sent,)

    def rep_second(self, *others):
        if self.early:
            self.wait(("far_a", "far_b"), others)
            self.total = jnp.concatenate(self.halves(), 0).astype(BF16)
        else:
            self.wait(("across",), others)
            self.total = (self.total.astype(F32) + self.across.astype(F32)).astype(BF16)
        self.across = lax.ppermute(self.total, "rep", ACROSS)
        return (self.total,)

    def rep_third(self, *others):
        self.wait(("across",), others)
        self.low = (self.total.astype(F32) + self.across.astype(F32)).astype(BF16)
        self.other = lax.ppermute(self.low, "rep", PAIRS)
        return (self.low,)

    def done(self):
        top = jnp.where(self.ends, self.low, self.other)
        bottom = jnp.where(self.ends, self.other, self.low)
        return jnp.concatenate([top, bottom], 0).astype(F32)


PAIRS = [(0, 1), (1, 0), (2, 3), (3, 2)]
ACROSS = [(0, 3), (3, 0), (1, 2), (2, 1)]


def whole(shape, dtype=None):
    del dtype
    return pl.BlockSpec(shape, lambda *_: (0,) * len(shape))


def steps(width):
    return pl.BlockSpec((STEP, width), lambda i: (i, 0))


SCALARS = pl.BlockSpec(memory_space=pltpu.SMEM)
ANYWHERE = pl.BlockSpec(memory_space=pl.ANY)


def shape_of(*dims, dtype=BF16):
    return jax.ShapeDtypeStruct(dims, dtype)


def params():
    return pltpu.CompilerParams(vmem_limit_bytes=VMEM)


def cost(time):
    return pl.CostEstimate(flops=int(time * 1e8), bytes_accessed=0, transcendentals=0)


def local(
    tokens,
    word_counts,
    region_counts,
    task_labels,
    masked_slots,
    qkv_weight,
    query_bias,
    value_bias,
    out_weight,
    out_bias,
    attn_gain,
    attn_shift,
    inner_weight,
    inner_bias,
    back_weight,
    back_bias,
    ffn_gain,
    ffn_shift,
    cotangent,
    *,
    shards,
    reps,
):
    pairs = word_counts.shape[0]
    count, width = tokens.shape
    hidden = back_weight.shape[0] * shards
    seq = count // pairs
    grid = (count // STEP,)
    cap = -(-pairs * WINDOW // LIVE) * LIVE
    cube = shards == 8 and reps == 4
    rows = width // shards
    me = lax.axis_index("shard")

    slots = jnp.arange(seq, dtype=jnp.int32)[None, :]
    words = word_counts[:, None]
    in_regions = (slots >= WORD_SLOTS) & (slots < WORD_SLOTS + region_counts[:, None])
    picked = masked_slots == 1
    labels = task_labels[:, None]
    live = (
        (labels == 0) & picked & (slots >= 1) & (slots < words)
        | (labels == 1) & picked & in_regions
        | (labels == 2) & (slots == 0)
    )
    live_count = jnp.sum(live.astype(jnp.int32), 1)
    taken = (live_count + PART - 1) // PART * PART
    base = jnp.concatenate([jnp.zeros((1,), jnp.int32), jnp.cumsum(taken)])
    rank = jnp.cumsum(live.astype(jnp.int32), 1) - 1 + base[:-1, None]
    pos = jnp.where(live, rank, -1).reshape(pairs, 1, seq)
    blocks = jnp.maximum(1, (base[-1:] + LIVE - 1) // LIVE)

    vectors = jnp.stack(
        [query_bias, value_bias, out_bias, attn_gain, attn_shift, back_bias, ffn_gain, ffn_shift]
        + [inner_bias[k * rows : (k + 1) * rows] for k in range(hidden // width)],
        1,
    )
    vectors = jnp.pad(vectors, ((0, 0), (0, 128 - vectors.shape[1])))
    attn_shard = jnp.concatenate([qkv_weight, out_weight, vectors], 1)
    def offsets(size):
        if not cube:
            return jnp.zeros((1,), jnp.int32)
        keys = jnp.array([0, XBIT, YBIT, XBIT | YBIT, XBIT | YBIT], jnp.int32)
        starts = jnp.array([0, 0, 0, 0, size // 2], jnp.int32)
        return jnp.concatenate([(keys ^ me) * size + starts, (keys ^ me ^ CORE) * size + starts])

    small_offsets, back_offsets = offsets(rows), offsets(back_weight.shape[0])
    order = jnp.arange(BLOCKS, dtype=jnp.int32)
    if cube:
        order = jnp.array([0, 2, 6, 4, 1, 3, 7, 5], jnp.int32) ^ me
    indices = (base, pos, blocks, small_offsets, back_offsets, order)
    if cube:
        attn_x, attn_y = swap(attn_shard, XBIT), swap(attn_shard, YBIT)
        own = [swap(v, CORE) for v in (attn_shard, inner_weight, back_weight)]
        near = lax.optimization_barrier((attn_x, attn_y, inner_weight, indices, *own))
        attn_x, attn_y, inner_weight, indices, *own = near
        attn_far = far_swap(attn_x, attn_y)
        inner_x, inner_y = swap(inner_weight, XBIT), swap(inner_weight, YBIT)
        attn_core = swap(attn_x, CORE), swap(attn_y, CORE)
        attn_far, attn_core, back_weight = lax.optimization_barrier((attn_far, attn_core, back_weight))
        back_x, back_y = swap(back_weight, XBIT), swap(back_weight, YBIT)
        attn = near_and_far(attn_shard, attn_x, attn_y, attn_far)
        attn_core = (own[0],) + attn_core + tuple(swap(v, CORE) for v in attn_far)
        attn = with_core(attn, attn_core)
    else:
        attn, inner, back = (
            [(lax.all_gather(v, "shard", axis=0, tiled=True), 0, 0)]
            for v in (attn_shard, inner_weight, back_weight)
        )
    base, pos, blocks, small_offsets, back_offsets, order = indices

    columns = 4 * width + 128
    attn_count = len(attn)
    attn_offsets, attn_pieces = small_offsets, [v for v, _, _ in attn]
    qkv, vector_rows, inner_bias_full = pl.pallas_call(
        functools.partial(project_kernel, attn_count, rows),
        grid=grid,
        in_specs=[SCALARS] + [ANYWHERE] * attn_count + [steps(width)],
        out_specs=[steps(3 * width), whole((16, width)), whole((1, hidden))],
        out_shape=[
            shape_of(count, 3 * width),
            shape_of(16, width, dtype=F32),
            shape_of(1, hidden, dtype=F32),
        ],
        scratch_shapes=[
            pltpu.VMEM((width, columns), BF16),
            pltpu.SemaphoreType.DMA((attn_count,)),
        ],
        compiler_params=params(),
        cost_estimate=cost(9),
        name="project",
    )(attn_offsets, *attn_pieces, tokens)
    if cube:
        inner_x, inner_y, qkv = lax.optimization_barrier((inner_x, inner_y, qkv))
        inner_far = far_swap(inner_x, inner_y)
    hidden1, compact = pl.pallas_call(
        functools.partial(attend_kernel, attn_count, seq),
        grid=grid,
        in_specs=[SCALARS] * 4
        + [ANYWHERE] * attn_count
        + [steps(width), steps(width), steps(3 * width), whole((pairs, 1, seq)), whole((16, width))],
        out_specs=[steps(width), whole((cap, columns))],
        out_shape=[shape_of(count, width, dtype=F32), shape_of(cap, columns)],
        scratch_shapes=[
            pltpu.VMEM((width, width), BF16),
            pltpu.VMEM((STEP, width), BF16),
            pltpu.SemaphoreType.DMA((attn_count,)),
        ],
        compiler_params=params(),
        cost_estimate=cost(14),
        name="attend",
    )(
        attn_offsets,
        base,
        word_counts,
        region_counts,
        *attn_pieces,
        tokens,
        cotangent,
        qkv,
        pos,
        vector_rows,
    )

    if cube:
        inner_x, inner_y, inner_far, back_x, back_y = lax.optimization_barrier(
            (inner_x, inner_y, inner_far, back_x, back_y, hidden1)
        )[:5]
        back_far = far_swap(back_x, back_y)
        inner_core = [own[1]] + [swap(v, CORE) for v in (inner_x, inner_y) + inner_far]
        inner = with_core(near_and_far(inner_weight, inner_x, inner_y, inner_far), inner_core)
    inner_count = len(inner)
    inner_offsets, inner_pieces = small_offsets, [v for v, _, _ in inner]
    in_vmem = pl.BlockSpec(memory_space=pltpu.VMEM)
    live_act, live_slope = pl.pallas_call(
        functools.partial(live_inner_kernel, inner_count),
        in_specs=[SCALARS] * 2 + [ANYWHERE] * (inner_count + 1) + [in_vmem],
        out_specs=[ANYWHERE] * 2,
        out_shape=[shape_of(cap, hidden)] * 2,
        scratch_shapes=[
            pltpu.VMEM((width, hidden), BF16),
            pltpu.VMEM((LIVE, width), BF16),
            pltpu.VMEM((LIVE, hidden), BF16),
            pltpu.VMEM((LIVE, hidden), BF16),
            pltpu.SemaphoreType.DMA((inner_count,)),
            pltpu.SemaphoreType.DMA((3,)),
        ],
        compiler_params=params(),
        cost_estimate=cost(6),
        name="live_inner",
    )(inner_offsets, blocks, *inner_pieces, compact, inner_bias_full)

    if cube:
        back_far, back_near, live_act = lax.optimization_barrier((back_far, (back_x, back_y), live_act))
        back_core = [own[2]] + [swap(v, CORE) for v in back_near + back_far]
        back = with_core(near_and_far(back_weight, *back_near, back_far), back_core)
    back_count = len(back)
    back_pieces = [v for v, _, _ in back]

    half = BLOCKS // 2
    size = hidden // BLOCKS
    block = width // BLOCKS
    keep_back, send_back, keep_inner, send_inner, d_hidden1, sums, inner_sum = pl.pallas_call(
        functools.partial(ffn_back_kernel, (inner_count, back_count)),
        in_specs=[SCALARS] * 4 + [ANYWHERE] * (inner_count + back_count + 3) + [in_vmem],
        out_specs=[ANYWHERE] * 5 + [in_vmem] * 2,
        out_shape=[
            shape_of(half, size, width),
            shape_of(half, size, width),
            shape_of(half, size, width),
            shape_of(half, size, width),
            shape_of(cap, width, dtype=F32),
            shape_of(16, width, dtype=F32),
            shape_of(1, hidden, dtype=F32),
        ],
        scratch_shapes=[
            pltpu.VMEM((hidden, width), BF16),
            pltpu.VMEM((width, hidden), BF16),
            pltpu.VMEM((cap, width), BF16),
            pltpu.VMEM((cap, width), BF16),
            pltpu.VMEM((cap, hidden), BF16),
            pltpu.VMEM((cap, hidden), BF16),
            pltpu.VMEM((cap, width), BF16),
            pltpu.VMEM((cap, hidden), BF16),
            pltpu.VMEM((cap, width), F32),
            pltpu.VMEM((width, width), F32),
            pltpu.VMEM((BLOCKS, size, width), BF16),
            pltpu.VMEM((BLOCKS, size, width), BF16),
            pltpu.VMEM((width, LIVE), BF16),
            pltpu.VMEM((cap // LIVE, width, LIVE), BF16),
            pltpu.SemaphoreType.DMA((inner_count,)),
            pltpu.SemaphoreType.DMA((back_count,)),
            pltpu.SemaphoreType.DMA((12 + 2 * hidden // width,)),
        ],
        compiler_params=params(),
        cost_estimate=cost(13),
        name="ffn_back",
    )(
        inner_offsets,
        back_offsets,
        order,
        blocks,
        *inner_pieces,
        *back_pieces,
        compact,
        live_act,
        live_slope,
        vector_rows,
    )

    if cube:
        back_total = Sum(keep_back, send_back)
        inner_total = Sum(keep_inner, send_inner, early=True)

    d_qkv, d_r1, keep_attn, send_attn = pl.pallas_call(
        functools.partial(attend_back_kernel, attn_count, seq, rows),
        in_specs=[SCALARS] * 6 + [ANYWHERE] * (attn_count + 4) + [in_vmem] * 4,
        out_specs=[ANYWHERE] * 4,
        out_shape=[
            shape_of(count, 3 * width),
            shape_of(cap, width),
            shape_of(half, block, columns),
            shape_of(half, block, columns),
        ],
        scratch_shapes=[
            pltpu.VMEM((width, width), BF16),
            pltpu.VMEM((cap, width), BF16),
            pltpu.VMEM((cap, width), BF16),
            pltpu.VMEM((cap, 128), BF16),
            pltpu.VMEM((cap, width), F32),
            pltpu.VMEM((count, 3 * width), BF16),
            pltpu.VMEM((count, width), BF16),
            pltpu.VMEM((cap, width), BF16),
            pltpu.VMEM((cap, width), BF16),
            pltpu.VMEM((TOGETHER, seq, width), F32),
            pltpu.VMEM((TOGETHER, seq, width), F32),
            pltpu.VMEM((TOGETHER, seq, width), F32),
            pltpu.VMEM((count, 3 * width), BF16),
            pltpu.VMEM((width, width), F32),
            pltpu.VMEM((BLOCKS, block, columns), BF16),
            pltpu.VMEM((16, width), F32),
            pltpu.VMEM((width, count), BF16),
            pltpu.VMEM((width, LIVE), BF16),
            pltpu.VMEM((width, count), BF16),
            pltpu.SemaphoreType.DMA((attn_count,)),
            pltpu.SemaphoreType.DMA((16 + count // STEP,)),
        ],
        compiler_params=params(),
        cost_estimate=cost(22),
        name="attend_back",
    )(
        attn_offsets,
        order,
        base,
        word_counts,
        region_counts,
        blocks,
        *attn_pieces,
        compact,
        d_hidden1,
        qkv,
        tokens,
        vector_rows,
        sums,
        inner_sum,
        pos,
    )

    def later(shift):
        return lambda i: (i + shift, 0)

    def ffn(first, x, *done):
        return pl.pallas_call(
            functools.partial(ffn_kernel, (inner_count, back_count)),
            grid=(grid[0] // 2,),
            in_specs=[SCALARS] * 2
            + [ANYWHERE] * (inner_count + back_count)
            + [pl.BlockSpec((STEP, width), later(first)), whole((1, hidden)), whole((16, width))]
            + [ANYWHERE] * len(done),
            out_specs=pl.BlockSpec((STEP, width), later(first)),
            out_shape=shape_of(count, width),
            input_output_aliases={5 + inner_count + back_count: 0} if done else {},
            scratch_shapes=[
                pltpu.VMEM((width, hidden), BF16),
                pltpu.VMEM((hidden, width), BF16),
                pltpu.VMEM((STEP, hidden), BF16),
                pltpu.SemaphoreType.DMA((inner_count,)),
                pltpu.SemaphoreType.DMA((back_count,)),
            ],
            compiler_params=params(),
            cost_estimate=cost(11),
            name="ffn",
        )(
            inner_offsets,
            back_offsets,
            *inner_pieces,
            *back_pieces,
            x,
            inner_bias_full,
            vector_rows,
            *done,
        )

    x = hidden1
    if cube:
        sent = back_total.near(d_r1)
        sent += inner_total.rep_early(*sent)
        attn_total = Sum(keep_attn, send_attn)
        sent += attn_total.near(*sent)
        x = after(hidden1, *sent)
    result = ffn(0, x)
    if cube:
        sent = back_total.far(result)
        sent += attn_total.far(*sent)
        sent += back_total.rep_first(*sent)
        sent += inner_total.near(*sent)
        sent += attn_total.rep_first(*sent)
        sent += back_total.rep_second(*sent)
        sent += inner_total.far(*sent)
        d_qkv = after(d_qkv, *sent)

    input_grad = pl.pallas_call(
        functools.partial(input_grad_kernel, attn_count, seq),
        grid=grid,
        in_specs=[SCALARS] * 2
        + [ANYWHERE] * attn_count
        + [steps(3 * width), whole((cap, width)), whole((pairs, 1, seq))],
        out_specs=steps(width),
        out_shape=shape_of(count, width, dtype=F32),
        scratch_shapes=[
            pltpu.VMEM((width, 3 * width), BF16),
            pltpu.SemaphoreType.DMA((attn_count,)),
        ],
        compiler_params=params(),
        cost_estimate=cost(9),
        name="input_grad",
    )(attn_offsets, base, *attn_pieces, d_qkv, d_r1, pos)

    if cube:
        sent = attn_total.rep_second(input_grad)
        sent += back_total.rep_third(*sent)
        x = after(hidden1, *sent)
    result = ffn(grid[0] // 2, x, result)
    if cube:
        sent = inner_total.rep_second(result)

    quarters = hidden // width
    if cube:
        attn_total.rep_third(*sent)
        inner_total.rep_third()
        back_sum, inner_sum, attn_sum = (v.done() for v in (back_total, inner_total, attn_total))
        inner_sum = jnp.concatenate([inner_sum[c * block : (c + 1) * block] for c in range(quarters)], 1)
    else:
        back_grad = jnp.concatenate([keep_back, send_back]).reshape(hidden, width)
        inner_grad = jnp.concatenate([keep_inner, send_inner]).reshape(BLOCKS, quarters, block, width)
        inner_grad = inner_grad.transpose(0, 2, 1, 3).reshape(width, hidden)
        attn_grad = jnp.concatenate([keep_attn, send_attn]).reshape(width, columns)
        back_sum, inner_sum, attn_sum = (
            lax.psum(lax.psum_scatter(g, "shard", scatter_dimension=0, tiled=True), "rep").astype(F32)
            for g in (back_grad, inner_grad, attn_grad)
        )
    sums = attn_sum[:, 4 * width :].T
    return (
        result,
        input_grad,
        attn_sum[:, : 3 * width],
        sums[0],
        sums[1],
        attn_sum[:, 3 * width : 4 * width],
        sums[2],
        sums[3],
        sums[4],
        inner_sum,
        sums[8 : 8 + quarters].reshape(-1),
        back_sum,
        sums[5],
        sums[6],
        sums[7],
    )


def solution(mesh):
    rows, both, one = P(("rep", "shard"), None), P(("rep", "shard")), P("shard")
    matrix = P("shard", None)
    in_specs = (rows, both, both, both, rows, matrix, one, one, matrix, one, one, one)
    in_specs += (matrix, one, matrix, one, one, one, rows)
    out_specs = (rows, rows, matrix, one, one, matrix, one, one, one, matrix, one, matrix)
    out_specs += (one, one, one)
    sizes = dict(mesh.shape)

    def run(*args):
        return local(*args, shards=sizes["shard"], reps=sizes["rep"])

    return jax.shard_map(
        run, mesh=mesh, in_specs=in_specs, out_specs=out_specs, check_vma=False
    )
```

```python
import functools

import jax
import jax.numpy as jnp
from jax import lax
from jax.experimental import pallas as pl
from jax.experimental.pallas import tpu as pltpu
from jax.sharding import PartitionSpec as P

HEADS = 12
HEAD_DIM = 64
WORD_SLOTS = 60
CORE, XBIT, YBIT = 1, 2, 4
BLOCKS = 8
STEP = 256
LIVE = 192
WINDOW = 80
PART = 16
TOGETHER = 2
VMEM = 60 * 2**20
F32 = jnp.float32
BF16 = jnp.bfloat16


def mm(left, right):
    return jnp.dot(left, right, preferred_element_type=F32)


def mm_nt(left, right):
    return lax.dot_general(left, right, (((1,), (1,)), ((), ())), preferred_element_type=F32)


def mm_tn(left, right):
    return lax.dot_general(left, right, (((0,), (0,)), ((), ())), preferred_element_type=F32)


def norm_parts(value):
    mean = jnp.mean(value, -1, keepdims=True)
    centred = value - mean
    scale = lax.rsqrt(jnp.mean(centred * centred, -1, keepdims=True) + 1e-05)
    return centred * scale, scale


def norm_grad(grad, normed, scale):
    return scale * (
        grad
        - jnp.mean(grad, -1, keepdims=True)
        - normed * jnp.mean(grad * normed, -1, keepdims=True)
    )


def column_sum(value):
    return jnp.sum(value, 0, keepdims=True)


def start_pieces(pieces, offsets, scratch, sems, first=0, started=False):
    copies = []
    for j, piece in enumerate(pieces):
        start = pl.multiple_of(offsets[j], 16)
        source = piece.at[:, pl.ds(first, scratch.shape[1])]
        target = scratch.at[pl.ds(start, piece.shape[0]), :]
        copies.append(pltpu.make_async_copy(source, target, sems.at[j]))
        if not started:
            copies[-1].start()
    return copies


def stacked(block):
    lane = lax.broadcasted_iota(jnp.int32, block.shape, 1)
    zero = jnp.zeros_like(block)
    return jnp.concatenate(
        [jnp.where(lane < HEAD_DIM, block, zero), jnp.where(lane >= HEAD_DIM, block, zero)], 0
    )


def unstacked(block):
    rows = block.shape[0] // 2
    lane = lax.broadcasted_iota(jnp.int32, (rows, block.shape[1]), 1)
    return jnp.where(lane < HEAD_DIM, block[:rows], block[rows:])


def probabilities(queries, keys, valid):
    scores = jnp.where(valid, mm_nt(queries, keys), -1000000000.0)
    peak = jnp.max(scores, -1, keepdims=True)
    expo = jnp.exp(scores - peak)
    return expo * (1.0 / jnp.sum(expo, -1, keepdims=True))


def valid_slots(words, regions, seq):
    slot = lax.broadcasted_iota(jnp.int32, (1, seq), 1)
    return (slot < words) | ((slot >= WORD_SLOTS) & (slot < WORD_SLOTS + regions))


def selector(pos, start, seq):
    row = lax.broadcasted_iota(jnp.int32, (WINDOW, seq), 0) + start
    return jnp.where(row == pos, 1.0, 0.0).astype(BF16)


def window_start(base):
    return pl.multiple_of(base, PART)


def project_kernel(count, shard_rows, *refs):
    offsets = refs[0]
    pieces = refs[1 : 1 + count]
    tokens, qkv, vectors, bias, weights, sems = refs[1 + count :]
    width = tokens.shape[1]
    quarters = bias.shape[1] // width

    @pl.when(pl.program_id(0) == 0)
    def _():
        for copy in start_pieces(pieces, offsets, weights, sems):
            copy.wait()
        share = weights[:, 4 * width :].astype(F32)
        vectors[...] = share.T[: vectors.shape[0]]
        parts = []
        for s in range(width // shard_rows):
            for k in range(quarters):
                part = share[s * shard_rows : (s + 1) * shard_rows, 8 + k : 9 + k]
                parts.append(jnp.broadcast_to(part, (shard_rows, 8)))
        bias[...] = jnp.concatenate(parts, 0).T[:1]

    x = tokens[...]
    for part, row in ((0, 0), (1, None), (2, 1)):
        columns = slice(part * width, (part + 1) * width)
        value = mm(x, weights[:, columns])
        if row is not None:
            value = value + vectors[row : row + 1, :]
        qkv[:, columns] = value.astype(BF16)


def attend_kernel(seq, words, regions, qkv, mixed):
    width = mixed.shape[1]
    step = pl.program_id(0)
    for k in range(STEP // seq):
        rows = slice(k * seq, (k + 1) * seq)
        pair = step * (STEP // seq) + k
        valid = valid_slots(words[pair], regions[pair], seq)
        for h in range(HEADS // 2):
            lanes = slice(h * 128, (h + 1) * 128)
            queries = stacked(qkv[rows, lanes] * HEAD_DIM ** (-0.5))
            keys = qkv[rows, width + h * 128 : width + (h + 1) * 128]
            values = qkv[rows, 2 * width + h * 128 : 2 * width + (h + 1) * 128]
            scores = jnp.where(valid, mm_nt(queries, keys), -1000000000.0)
            expo = jnp.exp(scores - jnp.max(scores, -1, keepdims=True)).astype(BF16)
            both = mm(expo, jnp.concatenate([values, jnp.ones_like(values)], 1))
            mixed[rows, lanes] = (unstacked(both[:, :128]) / unstacked(both[:, 128:])).astype(BF16)


def settle_kernel(count, seq, *refs):
    offsets, base = refs[:2]
    pieces = refs[2 : 2 + count]
    tokens, cotangent, mixed, pos, vectors, hidden, compact, proj, sems = refs[2 + count :]
    width = tokens.shape[1]
    step = pl.program_id(0)

    @pl.when(step == 0)
    def _():
        copies = start_pieces(pieces, offsets, proj, sems, 3 * width)
        compact[...] = jnp.zeros_like(compact)
        for copy in copies:
            copy.wait()

    branch = mm(mixed[...], proj[...]) + vectors[2:3, :]
    normed, scale = norm_parts(tokens[...].astype(F32) + branch)
    value = normed * vectors[3:4, :] + vectors[4:5, :]
    hidden[...] = value
    high = scale.astype(BF16)
    rest = scale - high.astype(F32)
    middle = rest.astype(BF16)
    low = (rest - middle.astype(F32)).astype(BF16)
    lane = lax.broadcasted_iota(jnp.int32, (STEP, 128), 1)
    zero = jnp.zeros((STEP, 128), BF16)
    scales = jnp.where(lane == 0, high, jnp.where(lane == 1, middle, jnp.where(lane == 2, low, zero)))
    parts = (value.astype(BF16), normed.astype(BF16), mixed[...], cotangent[...], scales)
    for k in range(STEP // seq):
        pair = step * (STEP // seq) + k
        start = window_start(base[pair])
        chosen = selector(pos[pair], start, seq)
        at = 0
        for part in parts:
            columns = slice(at, at + part.shape[1])
            at += part.shape[1]
            got = mm(chosen, part[k * seq : (k + 1) * seq]).astype(BF16)
            compact[pl.ds(start, WINDOW), columns] = got


def gelu_parts(inner):
    cumul = 0.5 + 0.5 * lax.erf(inner * 0.7071067811865476)
    return inner * cumul, cumul


def live_inner_kernel(count, *refs):
    offsets, blocks = refs[:2]
    pieces = refs[2 : 2 + count]
    compact, bias, act_out, slope_out = refs[2 + count : 6 + count]
    weights, hidden, act, slope, sems, more = refs[6 + count :]
    width = hidden.shape[1]
    copies = start_pieces(pieces, offsets, weights, sems)
    count_live = blocks[0]

    def rows_of(b):
        return pl.ds(pl.multiple_of(b * LIVE, LIVE), LIVE)

    def load(b):
        return pltpu.make_async_copy(compact.at[rows_of(b), pl.ds(0, width)], hidden, more.at[0])

    load(0).start()
    for copy in copies:
        copy.wait()

    @pl.loop(0, count_live)
    def _(b):
        load(b).wait()
        x = hidden[...]
        for c in range(weights.shape[1] // width):
            columns = slice(c * width, (c + 1) * width)
            inner = mm(x, weights[:, columns]) + bias[:, columns]
            value, cumul = gelu_parts(inner)
            density = jnp.exp(-0.5 * inner * inner) * 0.3989422804014327
            act[:, columns] = value.astype(BF16)
            slope[:, columns] = (cumul + inner * density).astype(BF16)
        outs = [
            pltpu.make_async_copy(act, act_out.at[rows_of(b)], more.at[1]),
            pltpu.make_async_copy(slope, slope_out.at[rows_of(b)], more.at[2]),
        ]
        for copy in outs:
            copy.start()

        @pl.when(b + 1 < count_live)
        def _():
            load(b + 1).start()

        for copy in outs:
            copy.wait()


def ffn_kernel(counts, *refs):
    inner_offsets, back_offsets = refs[:2]
    inner_pieces = refs[2 : 2 + counts[0]]
    back_pieces = refs[2 + counts[0] : 2 + counts[0] + counts[1]]
    hidden, bias, vectors = refs[2 + sum(counts) : 5 + sum(counts)]
    result, inner, back, act, inner_sems, back_sems = refs[-6:]
    width = hidden.shape[1]
    step = pl.program_id(0)

    @pl.when(step == 0)
    def _():
        copies = start_pieces(inner_pieces, inner_offsets, inner, inner_sems)
        start_pieces(back_pieces, back_offsets, back, back_sems)
        for copy in copies:
            copy.wait()

    x = hidden[...]
    low = x.astype(BF16)
    for c in range(inner.shape[1] // width):
        columns = slice(c * width, (c + 1) * width)
        value = mm(low, inner[:, columns]) + bias[:, columns]
        act[:, columns] = gelu_parts(value)[0].astype(BF16)

    @pl.when(step == 0)
    def _():
        for copy in start_pieces(back_pieces, back_offsets, back, back_sems, started=True):
            copy.wait()

    second = mm(act[...], back[...]) + vectors[5:6, :]
    normed, _ = norm_parts(x + second)
    result[...] = (normed * vectors[6:7, :] + vectors[7:8, :]).astype(BF16)


def rows_of(b):
    return pl.ds(pl.multiple_of(b * LIVE, LIVE), LIVE)


def load_live(count_live, pairs, sems):
    def copies(b):
        here = rows_of(b)
        return [
            pltpu.make_async_copy(source(here), target.at[here], sems.at[j])
            for j, (source, target) in enumerate(pairs)
        ]

    for copy in copies(0):
        copy.start()

    def finish():
        for copy in copies(0):
            copy.wait()

        @pl.loop(1, count_live)
        def _(b):
            later = copies(b)
            for copy in later:
                copy.start()
            for copy in later:
                copy.wait()

    return finish


def store_live(count_live, pairs, sems):
    def copies(b):
        here = rows_of(b)
        return [
            pltpu.make_async_copy(source.at[here], target.at[here], sems.at[j])
            for j, (source, target) in enumerate(pairs)
        ]

    for copy in copies(0):
        copy.start()

    def finish():
        for copy in copies(0):
            copy.wait()

        @pl.loop(1, count_live)
        def _(b):
            later = copies(b)
            for copy in later:
                copy.start()
            for copy in later:
                copy.wait()

    return finish


def ffn_back_kernel(counts, *refs):
    inner_offsets, back_offsets, order, blocks = refs[:4]
    inner_pieces = refs[4 : 4 + counts[0]]
    back_pieces = refs[4 + counts[0] : 4 + sum(counts)]
    refs = refs[4 + sum(counts) :]
    compact_hbm, act_hbm, slope_hbm, vectors = refs[:4]
    keep_back, send_back, keep_inner, send_inner, d_hidden_out, sums, inner_sum = refs[4:11]
    back, inner, hidden, cotangent, act, slope, d_second, d_inner, d_hidden = refs[11:20]
    total, out_back, out_inner, turned, ordered, inner_sems, back_sems, more = refs[20:]
    width = inner.shape[0]
    size = inner.shape[1] // BLOCKS
    quarters = inner.shape[1] // width
    rows = width // BLOCKS
    half = BLOCKS // 2
    first = slice(0, LIVE)
    count_live = blocks[0]

    def live_copies(b):
        here = rows_of(b)
        return [
            pltpu.make_async_copy(compact_hbm.at[here, pl.ds(0, width)], hidden.at[here], more.at[0]),
            pltpu.make_async_copy(
                compact_hbm.at[here, pl.ds(3 * width, width)], cotangent.at[here], more.at[1]
            ),
            pltpu.make_async_copy(act_hbm.at[here], act.at[here], more.at[2]),
            pltpu.make_async_copy(slope_hbm.at[here], slope.at[here], more.at[3]),
        ]

    now = live_copies(0)
    for copy in now:
        copy.start()
    back_copies = start_pieces(back_pieces, back_offsets, back, back_sems)
    inner_copies = start_pieces(inner_pieces, inner_offsets, inner, inner_sems)
    sums[...] = jnp.zeros_like(sums)
    inner_sum[...] = jnp.zeros_like(inner_sum)
    for copy in now:
        copy.wait()

    @pl.loop(1, count_live)
    def _(b):
        later = live_copies(b)
        for copy in later:
            copy.start()
        for copy in later:
            copy.wait()

    for copy in back_copies:
        copy.wait()

    @pl.loop(0, count_live)
    def _(b):
        here = rows_of(b)
        second = mm(act[here, :], back[...]) + vectors[5:6, :]
        normed, scale = norm_parts(hidden[here, :].astype(F32) + second)
        d_out = cotangent[here, :].astype(F32)
        sums[6:7, :] += column_sum(d_out * normed)
        sums[7:8, :] += column_sum(d_out)
        d_r2 = norm_grad(d_out * vectors[6:7, :], normed, scale)
        low = d_r2.astype(BF16)
        d_second[here, :] = low
        sums[5:6, :] += column_sum(low.astype(F32))
        d_hidden[here, :] = d_r2

    single = count_live == 1
    outs = []
    for i in range(BLOCKS):
        chunk = pl.ds(pl.multiple_of(order[i] * size, 128), size)

        @pl.when(single)
        def _():
            out_back[i] = mm_tn(act[first, chunk], d_second[first, :]).astype(BF16)

        @pl.when(jnp.logical_not(single))
        def _():
            total[:size, :] = mm_tn(act[first, chunk], d_second[first, :])

            @pl.loop(1, count_live)
            def _(b):
                here = rows_of(b)
                total[:size, :] += mm_tn(act[here, chunk], d_second[here, :])

            out_back[i] = total[:size, :].astype(BF16)

        target = keep_back.at[i] if i < half else send_back.at[i - half]
        outs.append(pltpu.make_async_copy(out_back.at[i], target, more.at[4 + i]))
        outs[-1].start()
    for copy in inner_copies:
        copy.wait()

    @pl.loop(0, count_live)
    def _(b):
        here = rows_of(b)
        grad = d_second[here, :]
        for c in range(quarters):
            columns = slice(c * width, (c + 1) * width)
            d_act = mm_nt(grad, back[columns, :])
            low = (d_act * slope[here, columns].astype(F32)).astype(BF16)
            d_inner[here, columns] = low
            inner_sum[:, columns] += column_sum(low.astype(F32))
            d_hidden[here, :] += mm_nt(low, inner[:, columns])

    def hidden_copy(b):
        return pltpu.make_async_copy(
            d_hidden.at[rows_of(b)], d_hidden_out.at[rows_of(b)], more.at[0]
        )

    hidden_copy(0).start()

    @pl.loop(0, count_live)
    def _(b):
        here = rows_of(b)
        turned[...] = hidden[here, :].T
        for i in range(BLOCKS):
            start = pl.multiple_of(order[i] * rows, 16)
            ordered[b, i * rows : (i + 1) * rows, :] = turned[pl.ds(start, rows), :]

    for c in range(quarters):
        columns = slice(c * width, (c + 1) * width)
        target = slice(c * rows, (c + 1) * rows)

        @pl.when(single)
        def _():
            value = mm(ordered[0], d_inner[first, columns]).astype(BF16)
            for i in range(BLOCKS):
                out_inner[i, target, :] = value[i * rows : (i + 1) * rows, :]

        @pl.when(jnp.logical_not(single))
        def _():
            total[...] = mm(ordered[0], d_inner[first, columns])

            @pl.loop(1, count_live)
            def _(b):
                total[...] += mm(ordered[b], d_inner[rows_of(b), columns])

            for i in range(BLOCKS):
                out_inner[i, target, :] = total[i * rows : (i + 1) * rows, :].astype(BF16)

        for j, out in enumerate((keep_inner, send_inner)):
            blocks_out = pl.ds(j * half, half)
            part = pl.ds(c * rows, rows)
            source = out_inner.at[blocks_out, part]
            outs.append(pltpu.make_async_copy(source, out.at[:, part], more.at[12 + 2 * c + j]))
            outs[-1].start()
    hidden_copy(0).wait()

    @pl.loop(1, count_live)
    def _(b):
        hidden_copy(b).start()
        hidden_copy(b).wait()

    for copy in outs:
        copy.wait()


def by_head(block):
    lane = lax.broadcasted_iota(jnp.int32, block.shape, 1) // HEAD_DIM
    zero = jnp.zeros_like(block)
    return jnp.concatenate([jnp.where(lane == h, block, zero) for h in range(HEADS)], 0)


def from_heads(block):
    rows = block.shape[0] // HEADS
    lane = lax.broadcasted_iota(jnp.int32, (rows, 128), 1)
    parts = []
    for h in range(HEADS // 2):
        lanes = slice(h * 128, (h + 1) * 128)
        left = block[2 * h * rows : (2 * h + 1) * rows, lanes]
        right = block[(2 * h + 1) * rows : (2 * h + 2) * rows, lanes]
        parts.append(jnp.where(lane < HEAD_DIM, left, right))
    return jnp.concatenate(parts, 1)


def attend_back_kernel(count, seq, shard_rows, *refs):
    offsets, order, base, words, regions, blocks = refs[:6]
    pieces = refs[6 : 6 + count]
    refs = refs[6 + count :]
    compact, d_hidden_hbm, qkv_hbm, tokens_hbm, vectors, ffn_sums, inner_sum, pos = refs[:8]
    d_qkv_out, d_r1_out, keep_out, send_out = refs[8:12]
    weights, normed_in, mixed, scales, d_hidden, qkv, tokens, d_r1, d_mixed = refs[12:21]
    d_query, d_keys, d_values, d_qkv, total, out, sums = refs[21:28]
    turned, mixed_turned, tokens_turned, sems, more = refs[28:]
    width = weights.shape[0]
    rows = width // BLOCKS
    half = BLOCKS // 2
    pairs = pos.shape[0]
    count_live = blocks[0]

    loads = [
        (lambda here: compact.at[here, pl.ds(width, width)], normed_in),
        (lambda here: compact.at[here, pl.ds(2 * width, width)], mixed),
        (lambda here: compact.at[here, pl.ds(4 * width, 128)], scales),
        (lambda here: d_hidden_hbm.at[here], d_hidden),
    ]
    loaded = load_live(count_live, loads, more)
    weight_copies = start_pieces(pieces, offsets, weights, sems, 3 * width)
    qkv_copy = pltpu.make_async_copy(qkv_hbm, qkv, more.at[4])
    tokens_copy = pltpu.make_async_copy(tokens_hbm, tokens, more.at[5])
    qkv_copy.start()
    tokens_copy.start()
    d_r1[...] = jnp.zeros_like(d_r1)
    sums[...] = ffn_sums[...]
    loaded()
    for copy in weight_copies:
        copy.wait()

    @pl.loop(0, count_live)
    def _(b):
        here = rows_of(b)
        grad = d_hidden[here, :]
        normed = normed_in[here, :].astype(F32)
        scale = jnp.sum(scales[here, :].astype(F32), -1, keepdims=True)
        sums[3:4, :] += column_sum(grad * normed)
        sums[4:5, :] += column_sum(grad)
        low = norm_grad(grad * vectors[3:4, :], normed, scale).astype(BF16)
        sums[2:3, :] += column_sum(low.astype(F32))
        d_r1[here, :] = low
        d_mixed[here, :] = mm_nt(low, weights[...]).astype(BF16)

    def in_order(source, target):
        turned[:, : source.shape[0]] = source.T
        for i in range(BLOCKS):
            start = pl.multiple_of(order[i] * rows, 16)
            target[i * rows : (i + 1) * rows, :] = turned[pl.ds(start, rows), : source.shape[0]]

    outs = []

    def spread(value, first, size):
        low = value.astype(BF16)
        for i in range(BLOCKS):
            out[i, :, first : first + size] = low[i * rows : (i + 1) * rows, :size]
        columns = pl.ds(first, size)
        for j, target in enumerate((keep_out, send_out)):
            source = out.at[pl.ds(j * half, half), :, columns]
            sem = more.at[6 + len(outs)]
            outs.append(pltpu.make_async_copy(source, target.at[:, :, columns], sem))
            outs[-1].start()

    in_order(mixed[:LIVE, :], mixed_turned)

    @pl.when(count_live == 1)
    def _():
        total[...] = mm(mixed_turned[...], d_r1[:LIVE, :])

    @pl.when(count_live > 1)
    def _():
        total[...] = mm(mixed_turned[...], d_r1[:LIVE, :])

        @pl.loop(1, count_live)
        def _(b):
            here = rows_of(b)
            in_order(mixed[here, :], mixed_turned)
            total[...] += mm(mixed_turned[...], d_r1[here, :])

    spread(total[...], 3 * width, width)
    tokens_copy.wait()
    in_order(tokens[...], tokens_turned)
    qkv_copy.wait()

    def pair_part(pair, b):
        mine = pl.ds(pl.multiple_of(pair * seq, seq), seq)
        valid = valid_slots(words[pair], regions[pair], seq)
        first = pl.multiple_of(base[pair] + b * PART, PART)
        row = lax.broadcasted_iota(jnp.int32, (PART, seq), 0) + first
        chosen = jnp.where(row == pos[pair], 1.0, 0.0).astype(BF16)
        live_query = mm(chosen, qkv[mine, :width]).astype(BF16) * HEAD_DIM ** (-0.5)
        queries = by_head(live_query)
        grad = d_mixed[pl.ds(first, PART), :]
        row = lax.broadcasted_iota(jnp.int32, grad.shape, 0) + first
        grad = by_head(jnp.where(row < base[pair + 1], grad, jnp.zeros_like(grad)))
        keys = qkv[mine, width : 2 * width]
        probs = probabilities(queries, keys, valid)
        d_probs = mm_nt(grad, qkv[mine, 2 * width :])
        inside = jnp.sum(d_probs * probs, -1, keepdims=True)
        d_scores = (probs * (d_probs - inside)).astype(BF16)
        part = (from_heads(mm(d_scores, keys)) * HEAD_DIM ** (-0.5)).astype(BF16)
        return mm_tn(chosen, part), mm_tn(d_scores, queries), mm_tn(probs.astype(BF16), grad)

    @pl.loop(0, pairs // TOGETHER)
    def _(step):
        group = [step * TOGETHER + k for k in range(TOGETHER)]
        trips = (base[group[0] + 1] - base[group[0]]) // PART
        for pair in group[1:]:
            trips = jnp.maximum(trips, (base[pair + 1] - base[pair]) // PART)
        for k, pair in enumerate(group):
            for ref, value in zip((d_query, d_keys, d_values), pair_part(pair, 0)):
                ref[k] = value

        @pl.loop(1, trips)
        def _(b):
            for k, pair in enumerate(group):
                for ref, value in zip((d_query, d_keys, d_values), pair_part(pair, b)):
                    ref[k] += value

        for k, pair in enumerate(group):
            mine = pl.ds(pl.multiple_of(pair * seq, seq), seq)
            for part, ref in enumerate((d_query, d_keys, d_values)):
                low = ref[k].astype(BF16)
                d_qkv[mine, part * width : (part + 1) * width] = low
                if part != 1:
                    row = 0 if part == 0 else 1
                    sums[row : row + 1, :] += column_sum(low.astype(F32))

    column_form = jnp.broadcast_to(inner_sum[...], (8, inner_sum.shape[1])).T
    quarters = inner_sum.shape[1] // width
    block = jnp.concatenate([sums[...], jnp.zeros((128 - sums.shape[0], width), F32)], 0).T
    lane = lax.broadcasted_iota(jnp.int32, block.shape, 1)
    for k in range(quarters):
        starts = [(s * quarters + k) * shard_rows for s in range(width // shard_rows)]
        column = jnp.concatenate([column_form[s : s + shard_rows, :1] for s in starts], 0)
        block = jnp.where(lane == 8 + k, column, block)
    total[:, :128] = block
    spread(
        jnp.concatenate(
            [total[pl.ds(pl.multiple_of(order[i] * rows, 8), rows), :128] for i in range(BLOCKS)], 0
        ),
        4 * width,
        128,
    )
    for part in range(3):
        columns = slice(part * width, (part + 1) * width)
        spread(mm(tokens_turned[...], d_qkv[:, columns]), part * width, width)

    outs += [
        pltpu.make_async_copy(d_qkv, d_qkv_out, more.at[6 + len(outs)]),
        pltpu.make_async_copy(d_r1, d_r1_out, more.at[7 + len(outs)]),
    ]
    outs[-2].start()
    outs[-1].start()
    for copy in outs:
        copy.wait()


def input_grad_kernel(count, seq, *refs):
    offsets, base = refs[:2]
    pieces = refs[2 : 2 + count]
    d_qkv, d_r1, pos, out, weights, sems = refs[2 + count :]
    step = pl.program_id(0)

    @pl.when(step == 0)
    def _():
        for copy in start_pieces(pieces, offsets, weights, sems):
            copy.wait()

    value = mm_nt(d_qkv[...], weights[...])
    for k in range(STEP // seq):
        pair = step * (STEP // seq) + k
        start = window_start(base[pair])
        chosen = selector(pos[pair], start, seq)
        rows = slice(k * seq, (k + 1) * seq)
        out[rows, :] = value[rows] + mm_tn(chosen, d_r1[pl.ds(start, WINDOW), :])


def swap(value, bit):
    return lax.ppermute(value, "shard", [(i, i ^ bit) for i in range(8)])


def after(value, *others):
    return lax.optimization_barrier((value,) + others)[0]


def far_swap(by_x, by_y):
    half = by_x.shape[0] // 2
    return swap(by_y[:half], XBIT), swap(by_x[half:], YBIT)


def near_and_far(mine, by_x, by_y, by_both):
    far = XBIT | YBIT
    half = mine.shape[0] // 2
    near = [(mine, 0, 0), (by_x, XBIT, 0), (by_y, YBIT, 0)]
    return near + [(by_both[0], far, 0), (by_both[1], far, half)]


def chip_pieces(mine, others):
    keys = (0, XBIT, YBIT, XBIT | YBIT)
    return [(v, key, 0) for v, key in zip((mine,) + tuple(others), keys)]


def with_core(pieces, others):
    return pieces + [(v, key | CORE, row) for v, (_, key, row) in zip(others, pieces)]


class Sum:
    def __init__(self, keep, send, early=False):
        self.keep, self.early = keep, early
        self.got = swap(send, CORE)
        self.extra = None
        z = lax.axis_index("rep")
        self.ends = (z == 0) | (z == 3)

    def wait(self, names, others):
        values = tuple(getattr(self, name) for name in names)
        got = lax.optimization_barrier(values + tuple(others))
        for name, value in zip(names, got):
            setattr(self, name, value)

    def chip(self, block, bottom):
        if self.early:
            half = self.mine.shape[1] // 2
            rows = slice(half, None) if bottom else slice(0, half)
            return self.mine[block, rows].astype(F32) + self.extra[block, rows].astype(F32)
        half = self.keep.shape[1] // 2
        rows = slice(half, None) if bottom else slice(0, half)
        return self.keep[block, rows].astype(F32) + self.got[block, rows].astype(F32)

    def rep_early(self, *others):
        self.wait(("keep", "got"), others)
        half = self.keep.shape[1] // 2
        a = self.keep[:, :half].astype(F32) + self.got[:, :half].astype(F32)
        b = self.keep[:, half:].astype(F32) + self.got[:, half:].astype(F32)
        sent = jnp.where(self.ends, b, a).astype(BF16)
        self.mine = jnp.where(self.ends, a, b).astype(BF16)
        self.extra = lax.ppermute(sent, "rep", PAIRS)
        return (sent,)

    def near(self, *others):
        self.wait(("mine", "extra") if self.early else ("keep", "got"), others)
        sent = self.chip(slice(1, 3), False).astype(BF16), self.chip(slice(2, 4), True).astype(BF16)
        self.got_a, self.got_b = swap(sent[0], XBIT), swap(sent[1], YBIT)
        return sent

    def far(self, *others):
        self.wait(("got_a", "got_b"), others)
        send_a = (self.chip(3, False) + self.got_a[1].astype(F32)).astype(BF16)
        send_b = (self.chip(1, True) + self.got_b[0].astype(F32)).astype(BF16)
        self.far_a, self.far_b = swap(send_a, YBIT), swap(send_b, XBIT)
        return send_a, send_b

    def halves(self):
        a = self.chip(0, False) + self.got_a[0].astype(F32) + self.far_a.astype(F32)
        b = self.chip(0, True) + self.got_b[1].astype(F32) + self.far_b.astype(F32)
        return a, b

    def rep_first(self, *others):
        self.wait(("far_a", "far_b"), others)
        a, b = self.halves()
        sent = jnp.where(self.ends, b, a).astype(BF16)
        self.total = jnp.where(self.ends, a, b).astype(BF16)
        self.across = lax.ppermute(sent, "rep", PAIRS)
        return (sent,)

    def rep_second(self, *others):
        if self.early:
            self.wait(("far_a", "far_b"), others)
            self.total = jnp.concatenate(self.halves(), 0).astype(BF16)
        else:
            self.wait(("across",), others)
            self.total = (self.total.astype(F32) + self.across.astype(F32)).astype(BF16)
        self.across = lax.ppermute(self.total, "rep", ACROSS)
        return (self.total,)

    def rep_third(self, *others):
        self.wait(("across",), others)
        self.low = (self.total.astype(F32) + self.across.astype(F32)).astype(BF16)
        self.other = lax.ppermute(self.low, "rep", PAIRS)
        return (self.low,)

    def done(self):
        top = jnp.where(self.ends, self.low, self.other)
        bottom = jnp.where(self.ends, self.other, self.low)
        return jnp.concatenate([top, bottom], 0).astype(F32)


PAIRS = [(0, 1), (1, 0), (2, 3), (3, 2)]
ACROSS = [(0, 3), (3, 0), (1, 2), (2, 1)]


def whole(shape, dtype=None):
    del dtype
    return pl.BlockSpec(shape, lambda *_: (0,) * len(shape))


def steps(width):
    return pl.BlockSpec((STEP, width), lambda i: (i, 0))


SCALARS = pl.BlockSpec(memory_space=pltpu.SMEM)
ANYWHERE = pl.BlockSpec(memory_space=pl.ANY)


def shape_of(*dims, dtype=BF16):
    return jax.ShapeDtypeStruct(dims, dtype)


def params():
    return pltpu.CompilerParams(vmem_limit_bytes=VMEM)


def cost(time):
    return pl.CostEstimate(flops=int(time * 1e8), bytes_accessed=0, transcendentals=0)


def local(
    tokens,
    word_counts,
    region_counts,
    task_labels,
    masked_slots,
    qkv_weight,
    query_bias,
    value_bias,
    out_weight,
    out_bias,
    attn_gain,
    attn_shift,
    inner_weight,
    inner_bias,
    back_weight,
    back_bias,
    ffn_gain,
    ffn_shift,
    cotangent,
    *,
    shards,
    reps,
):
    pairs = word_counts.shape[0]
    count, width = tokens.shape
    hidden = back_weight.shape[0] * shards
    seq = count // pairs
    grid = (count // STEP,)
    cap = -(-pairs * WINDOW // LIVE) * LIVE
    cube = shards == 8 and reps == 4
    rows = width // shards
    me = lax.axis_index("shard")

    slots = jnp.arange(seq, dtype=jnp.int32)[None, :]
    words = word_counts[:, None]
    in_regions = (slots >= WORD_SLOTS) & (slots < WORD_SLOTS + region_counts[:, None])
    picked = masked_slots == 1
    labels = task_labels[:, None]
    live = (
        (labels == 0) & picked & (slots >= 1) & (slots < words)
        | (labels == 1) & picked & in_regions
        | (labels == 2) & (slots == 0)
    )
    live_count = jnp.sum(live.astype(jnp.int32), 1)
    taken = (live_count + PART - 1) // PART * PART
    base = jnp.concatenate([jnp.zeros((1,), jnp.int32), jnp.cumsum(taken)])
    rank = jnp.cumsum(live.astype(jnp.int32), 1) - 1 + base[:-1, None]
    pos = jnp.where(live, rank, -1).reshape(pairs, 1, seq)
    blocks = jnp.maximum(1, (base[-1:] + LIVE - 1) // LIVE)

    vectors = jnp.stack(
        [query_bias, value_bias, out_bias, attn_gain, attn_shift, back_bias, ffn_gain, ffn_shift]
        + [inner_bias[k * rows : (k + 1) * rows] for k in range(hidden // width)],
        1,
    )
    vectors = jnp.pad(vectors, ((0, 0), (0, 128 - vectors.shape[1])))
    attn_shard = jnp.concatenate([qkv_weight, out_weight, vectors], 1)
    def offsets(size, halves):
        if not cube:
            return jnp.zeros((1,), jnp.int32)
        keys = [0, XBIT, YBIT, XBIT | YBIT] + [XBIT | YBIT] * halves
        keys = jnp.array(keys, jnp.int32) ^ me
        starts = jnp.array([0] * 4 + [size // 2] * halves, jnp.int32)
        return jnp.concatenate([keys * size + starts, (keys ^ CORE) * size + starts])

    attn_offsets, inner_offsets = offsets(rows, 1), offsets(rows, 0)
    back_offsets = offsets(back_weight.shape[0], 0)
    order = jnp.arange(BLOCKS, dtype=jnp.int32)
    if cube:
        order = jnp.array([0, 2, 6, 4, 1, 3, 7, 5], jnp.int32) ^ me
    indices = (base, pos, blocks, attn_offsets, inner_offsets, back_offsets, order)
    if cube:
        attn_x, attn_y = swap(attn_shard, XBIT), swap(attn_shard, YBIT)
        own = [swap(v, CORE) for v in (attn_shard, inner_weight, back_weight)]
        near = lax.optimization_barrier((attn_x, attn_y, inner_weight, indices, *own))
        attn_x, attn_y, inner_weight, indices, *own = near
        attn_far = far_swap(attn_x, attn_y)
        inner_x, inner_y = swap(inner_weight, XBIT), swap(inner_weight, YBIT)
        attn_core = swap(attn_x, CORE), swap(attn_y, CORE)
        attn_far, attn_core, back_weight = lax.optimization_barrier((attn_far, attn_core, back_weight))
        back_x, back_y = swap(back_weight, XBIT), swap(back_weight, YBIT)
        attn = near_and_far(attn_shard, attn_x, attn_y, attn_far)
        attn_core = (own[0],) + attn_core + tuple(swap(v, CORE) for v in attn_far)
        attn = with_core(attn, attn_core)
    else:
        attn, inner, back = (
            [(lax.all_gather(v, "shard", axis=0, tiled=True), 0, 0)]
            for v in (attn_shard, inner_weight, back_weight)
        )
    base, pos, blocks, attn_offsets, inner_offsets, back_offsets, order = indices

    columns = 4 * width + 128
    attn_count = len(attn)
    attn_pieces = [v for v, _, _ in attn]
    qkv, vector_rows, inner_bias_full = pl.pallas_call(
        functools.partial(project_kernel, attn_count, rows),
        grid=grid,
        in_specs=[SCALARS] + [ANYWHERE] * attn_count + [steps(width)],
        out_specs=[steps(3 * width), whole((16, width)), whole((1, hidden))],
        out_shape=[
            shape_of(count, 3 * width),
            shape_of(16, width, dtype=F32),
            shape_of(1, hidden, dtype=F32),
        ],
        scratch_shapes=[
            pltpu.VMEM((width, columns), BF16),
            pltpu.SemaphoreType.DMA((attn_count,)),
        ],
        compiler_params=params(),
        cost_estimate=cost(9),
        name="project",
    )(attn_offsets, *attn_pieces, tokens)
    if cube:
        inner_x, inner_y, qkv = lax.optimization_barrier((inner_x, inner_y, qkv))
        inner_far = swap(inner_y, XBIT)
        inner_core = swap(inner_x, CORE), swap(inner_y, CORE)
    mixed = pl.pallas_call(
        functools.partial(attend_kernel, seq),
        grid=grid,
        in_specs=[SCALARS] * 2 + [steps(3 * width)],
        out_specs=steps(width),
        out_shape=shape_of(count, width),
        compiler_params=params(),
        cost_estimate=cost(8),
        name="attend",
    )(word_counts, region_counts, qkv)
    if cube:
        back_x, back_y, inner_core, mixed = lax.optimization_barrier(
            (back_x, back_y, inner_core, mixed)
        )
        back_far = swap(back_x, YBIT)
        back_core = swap(back_x, CORE), swap(back_y, CORE)
    hidden1, compact = pl.pallas_call(
        functools.partial(settle_kernel, attn_count, seq),
        grid=grid,
        in_specs=[SCALARS] * 2
        + [ANYWHERE] * attn_count
        + [steps(width)] * 3
        + [whole((pairs, 1, seq)), whole((16, width))],
        out_specs=[steps(width), whole((cap, columns))],
        out_shape=[shape_of(count, width, dtype=F32), shape_of(cap, columns)],
        scratch_shapes=[
            pltpu.VMEM((width, width), BF16),
            pltpu.SemaphoreType.DMA((attn_count,)),
        ],
        compiler_params=params(),
        cost_estimate=cost(9),
        name="settle",
    )(attn_offsets, base, *attn_pieces, tokens, cotangent, mixed, pos, vector_rows)

    if cube:
        inner_far, back_far, back_core, hidden1 = lax.optimization_barrier(
            (inner_far, back_far, back_core, hidden1)
        )
        inner = chip_pieces(inner_weight, (inner_x, inner_y, inner_far))
        inner = with_core(inner, (own[1],) + inner_core + (swap(inner_far, CORE),))
    inner_count = len(inner)
    inner_pieces = [v for v, _, _ in inner]
    in_vmem = pl.BlockSpec(memory_space=pltpu.VMEM)
    live_act, live_slope = pl.pallas_call(
        functools.partial(live_inner_kernel, inner_count),
        in_specs=[SCALARS] * 2 + [ANYWHERE] * (inner_count + 1) + [in_vmem],
        out_specs=[ANYWHERE] * 2,
        out_shape=[shape_of(cap, hidden)] * 2,
        scratch_shapes=[
            pltpu.VMEM((width, hidden), BF16),
            pltpu.VMEM((LIVE, width), BF16),
            pltpu.VMEM((LIVE, hidden), BF16),
            pltpu.VMEM((LIVE, hidden), BF16),
            pltpu.SemaphoreType.DMA((inner_count,)),
            pltpu.SemaphoreType.DMA((3,)),
        ],
        compiler_params=params(),
        cost_estimate=cost(6),
        name="live_inner",
    )(inner_offsets, blocks, *inner_pieces, compact, inner_bias_full)

    if cube:
        back = chip_pieces(back_weight, (back_x, back_y, back_far))
        back = with_core(back, (own[2],) + back_core + (swap(back_far, CORE),))
    back_count = len(back)
    back_pieces = [v for v, _, _ in back]

    half = BLOCKS // 2
    size = hidden // BLOCKS
    block = width // BLOCKS
    keep_back, send_back, keep_inner, send_inner, d_hidden1, sums, inner_sum = pl.pallas_call(
        functools.partial(ffn_back_kernel, (inner_count, back_count)),
        in_specs=[SCALARS] * 4 + [ANYWHERE] * (inner_count + back_count + 3) + [in_vmem],
        out_specs=[ANYWHERE] * 5 + [in_vmem] * 2,
        out_shape=[
            shape_of(half, size, width),
            shape_of(half, size, width),
            shape_of(half, size, width),
            shape_of(half, size, width),
            shape_of(cap, width, dtype=F32),
            shape_of(16, width, dtype=F32),
            shape_of(1, hidden, dtype=F32),
        ],
        scratch_shapes=[
            pltpu.VMEM((hidden, width), BF16),
            pltpu.VMEM((width, hidden), BF16),
            pltpu.VMEM((cap, width), BF16),
            pltpu.VMEM((cap, width), BF16),
            pltpu.VMEM((cap, hidden), BF16),
            pltpu.VMEM((cap, hidden), BF16),
            pltpu.VMEM((cap, width), BF16),
            pltpu.VMEM((cap, hidden), BF16),
            pltpu.VMEM((cap, width), F32),
            pltpu.VMEM((width, width), F32),
            pltpu.VMEM((BLOCKS, size, width), BF16),
            pltpu.VMEM((BLOCKS, size, width), BF16),
            pltpu.VMEM((width, LIVE), BF16),
            pltpu.VMEM((cap // LIVE, width, LIVE), BF16),
            pltpu.SemaphoreType.DMA((inner_count,)),
            pltpu.SemaphoreType.DMA((back_count,)),
            pltpu.SemaphoreType.DMA((12 + 2 * hidden // width,)),
        ],
        compiler_params=params(),
        cost_estimate=cost(13),
        name="ffn_back",
    )(
        inner_offsets,
        back_offsets,
        order,
        blocks,
        *inner_pieces,
        *back_pieces,
        compact,
        live_act,
        live_slope,
        vector_rows,
    )

    if cube:
        back_total = Sum(keep_back, send_back)
        inner_total = Sum(keep_inner, send_inner, early=True)

    d_qkv, d_r1, keep_attn, send_attn = pl.pallas_call(
        functools.partial(attend_back_kernel, attn_count, seq, rows),
        in_specs=[SCALARS] * 6 + [ANYWHERE] * (attn_count + 4) + [in_vmem] * 4,
        out_specs=[ANYWHERE] * 4,
        out_shape=[
            shape_of(count, 3 * width),
            shape_of(cap, width),
            shape_of(half, block, columns),
            shape_of(half, block, columns),
        ],
        scratch_shapes=[
            pltpu.VMEM((width, width), BF16),
            pltpu.VMEM((cap, width), BF16),
            pltpu.VMEM((cap, width), BF16),
            pltpu.VMEM((cap, 128), BF16),
            pltpu.VMEM((cap, width), F32),
            pltpu.VMEM((count, 3 * width), BF16),
            pltpu.VMEM((count, width), BF16),
            pltpu.VMEM((cap, width), BF16),
            pltpu.VMEM((cap, width), BF16),
            pltpu.VMEM((TOGETHER, seq, width), F32),
            pltpu.VMEM((TOGETHER, seq, width), F32),
            pltpu.VMEM((TOGETHER, seq, width), F32),
            pltpu.VMEM((count, 3 * width), BF16),
            pltpu.VMEM((width, width), F32),
            pltpu.VMEM((BLOCKS, block, columns), BF16),
            pltpu.VMEM((16, width), F32),
            pltpu.VMEM((width, count), BF16),
            pltpu.VMEM((width, LIVE), BF16),
            pltpu.VMEM((width, count), BF16),
            pltpu.SemaphoreType.DMA((attn_count,)),
            pltpu.SemaphoreType.DMA((16 + count // STEP,)),
        ],
        compiler_params=params(),
        cost_estimate=cost(22),
        name="attend_back",
    )(
        attn_offsets,
        order,
        base,
        word_counts,
        region_counts,
        blocks,
        *attn_pieces,
        compact,
        d_hidden1,
        qkv,
        tokens,
        vector_rows,
        sums,
        inner_sum,
        pos,
    )

    def later(shift):
        return lambda i: (i + shift, 0)

    def ffn(first, x, *done):
        return pl.pallas_call(
            functools.partial(ffn_kernel, (inner_count, back_count)),
            grid=(grid[0] // 2,),
            in_specs=[SCALARS] * 2
            + [ANYWHERE] * (inner_count + back_count)
            + [pl.BlockSpec((STEP, width), later(first)), whole((1, hidden)), whole((16, width))]
            + [ANYWHERE] * len(done),
            out_specs=pl.BlockSpec((STEP, width), later(first)),
            out_shape=shape_of(count, width),
            input_output_aliases={5 + inner_count + back_count: 0} if done else {},
            scratch_shapes=[
                pltpu.VMEM((width, hidden), BF16),
                pltpu.VMEM((hidden, width), BF16),
                pltpu.VMEM((STEP, hidden), BF16),
                pltpu.SemaphoreType.DMA((inner_count,)),
                pltpu.SemaphoreType.DMA((back_count,)),
            ],
            compiler_params=params(),
            cost_estimate=cost(11),
            name="ffn",
        )(
            inner_offsets,
            back_offsets,
            *inner_pieces,
            *back_pieces,
            x,
            inner_bias_full,
            vector_rows,
            *done,
        )

    x = hidden1
    if cube:
        sent = back_total.near(d_r1)
        sent += inner_total.rep_early(*sent)
        attn_total = Sum(keep_attn, send_attn)
        sent += attn_total.near(*sent)
        x = after(hidden1, *sent)
    result = ffn(0, x)
    if cube:
        sent = back_total.far(result)
        sent += attn_total.far(*sent)
        sent += back_total.rep_first(*sent)
        sent += inner_total.near(*sent)
        sent += attn_total.rep_first(*sent)
        sent += back_total.rep_second(*sent)
        sent += inner_total.far(*sent)
        d_qkv = after(d_qkv, *sent)

    input_grad = pl.pallas_call(
        functools.partial(input_grad_kernel, attn_count, seq),
        grid=grid,
        in_specs=[SCALARS] * 2
        + [ANYWHERE] * attn_count
        + [steps(3 * width), whole((cap, width)), whole((pairs, 1, seq))],
        out_specs=steps(width),
        out_shape=shape_of(count, width, dtype=F32),
        scratch_shapes=[
            pltpu.VMEM((width, 3 * width), BF16),
            pltpu.SemaphoreType.DMA((attn_count,)),
        ],
        compiler_params=params(),
        cost_estimate=cost(9),
        name="input_grad",
    )(attn_offsets, base, *attn_pieces, d_qkv, d_r1, pos)

    if cube:
        sent = attn_total.rep_second(input_grad)
        sent += back_total.rep_third(*sent)
        x = after(hidden1, *sent)
    result = ffn(grid[0] // 2, x, result)
    if cube:
        sent = inner_total.rep_second(result)

    quarters = hidden // width
    if cube:
        attn_total.rep_third(*sent)
        inner_total.rep_third()
        back_sum, inner_sum, attn_sum = (v.done() for v in (back_total, inner_total, attn_total))
        inner_sum = jnp.concatenate([inner_sum[c * block : (c + 1) * block] for c in range(quarters)], 1)
    else:
        back_grad = jnp.concatenate([keep_back, send_back]).reshape(hidden, width)
        inner_grad = jnp.concatenate([keep_inner, send_inner]).reshape(BLOCKS, quarters, block, width)
        inner_grad = inner_grad.transpose(0, 2, 1, 3).reshape(width, hidden)
        attn_grad = jnp.concatenate([keep_attn, send_attn]).reshape(width, columns)
        back_sum, inner_sum, attn_sum = (
            lax.psum(lax.psum_scatter(g, "shard", scatter_dimension=0, tiled=True), "rep").astype(F32)
            for g in (back_grad, inner_grad, attn_grad)
        )
    sums = attn_sum[:, 4 * width :].T
    return (
        result,
        input_grad,
        attn_sum[:, : 3 * width],
        sums[0],
        sums[1],
        attn_sum[:, 3 * width : 4 * width],
        sums[2],
        sums[3],
        sums[4],
        inner_sum,
        sums[8 : 8 + quarters].reshape(-1),
        back_sum,
        sums[5],
        sums[6],
        sums[7],
    )


def solution(mesh):
    rows, both, one = P(("rep", "shard"), None), P(("rep", "shard")), P("shard")
    matrix = P("shard", None)
    in_specs = (rows, both, both, both, rows, matrix, one, one, matrix, one, one, one)
    in_specs += (matrix, one, matrix, one, one, one, rows)
    out_specs = (rows, rows, matrix, one, one, matrix, one, one, one, matrix, one, matrix)
    out_specs += (one, one, one)
    sizes = dict(mesh.shape)

    def run(*args):
        return local(*args, shards=sizes["shard"], reps=sizes["rep"])

    return jax.shard_map(
        run, mesh=mesh, in_specs=in_specs, out_specs=out_specs, check_vma=False
    )
```

```python
import functools

import jax
import jax.numpy as jnp
from jax import lax
from jax.experimental import pallas as pl
from jax.experimental.pallas import tpu as pltpu
from jax.sharding import PartitionSpec as P

HEADS = 12
HEAD_DIM = 64
WORD_SLOTS = 60
CORE, XBIT, YBIT = 1, 2, 4
BLOCKS = 8
STEP = 256
LIVE = 192
WINDOW = 80
PART = 16
TOGETHER = 2
VMEM = 60 * 2**20
F32 = jnp.float32
BF16 = jnp.bfloat16


def mm(left, right):
    return jnp.dot(left, right, preferred_element_type=F32)


def mm_nt(left, right):
    return lax.dot_general(left, right, (((1,), (1,)), ((), ())), preferred_element_type=F32)


def mm_tn(left, right):
    return lax.dot_general(left, right, (((0,), (0,)), ((), ())), preferred_element_type=F32)


def norm_parts(value):
    mean = jnp.mean(value, -1, keepdims=True)
    centred = value - mean
    scale = lax.rsqrt(jnp.mean(centred * centred, -1, keepdims=True) + 1e-05)
    return centred * scale, scale


def norm_grad(grad, normed, scale):
    return scale * (
        grad
        - jnp.mean(grad, -1, keepdims=True)
        - normed * jnp.mean(grad * normed, -1, keepdims=True)
    )


def column_sum(value):
    return jnp.sum(value, 0, keepdims=True)


def start_pieces(pieces, offsets, scratch, sems, first=0, started=False):
    copies = []
    for j, piece in enumerate(pieces):
        start = pl.multiple_of(offsets[j], 16)
        source = piece.at[:, pl.ds(first, scratch.shape[1])]
        target = scratch.at[pl.ds(start, piece.shape[0]), :]
        copies.append(pltpu.make_async_copy(source, target, sems.at[j]))
        if not started:
            copies[-1].start()
    return copies


def stacked(block):
    lane = lax.broadcasted_iota(jnp.int32, block.shape, 1)
    zero = jnp.zeros_like(block)
    return jnp.concatenate(
        [jnp.where(lane < HEAD_DIM, block, zero), jnp.where(lane >= HEAD_DIM, block, zero)], 0
    )


def unstacked(block):
    rows = block.shape[0] // 2
    lane = lax.broadcasted_iota(jnp.int32, (rows, block.shape[1]), 1)
    return jnp.where(lane < HEAD_DIM, block[:rows], block[rows:])


def probabilities(queries, keys, valid):
    scores = jnp.where(valid, mm_nt(queries, keys), -1000000000.0)
    peak = jnp.max(scores, -1, keepdims=True)
    expo = jnp.exp(scores - peak)
    return expo * (1.0 / jnp.sum(expo, -1, keepdims=True))


def valid_slots(words, regions, seq):
    slot = lax.broadcasted_iota(jnp.int32, (1, seq), 1)
    return (slot < words) | ((slot >= WORD_SLOTS) & (slot < WORD_SLOTS + regions))


def selector(pos, start, seq):
    row = lax.broadcasted_iota(jnp.int32, (WINDOW, seq), 0) + start
    return jnp.where(row == pos, 1.0, 0.0).astype(BF16)


def window_start(base):
    return pl.multiple_of(base, PART)


def project_kernel(count, shard_rows, *refs):
    offsets = refs[0]
    pieces = refs[1 : 1 + count]
    tokens, qkv, vectors, bias, weights, sems = refs[1 + count :]
    width = tokens.shape[1]
    quarters = bias.shape[1] // width

    @pl.when(pl.program_id(0) == 0)
    def _():
        for copy in start_pieces(pieces, offsets, weights, sems):
            copy.wait()
        share = weights[:, 4 * width :].astype(F32)
        vectors[...] = share.T[: vectors.shape[0]]
        parts = []
        for s in range(width // shard_rows):
            for k in range(quarters):
                part = share[s * shard_rows : (s + 1) * shard_rows, 8 + k : 9 + k]
                parts.append(jnp.broadcast_to(part, (shard_rows, 8)))
        bias[...] = jnp.concatenate(parts, 0).T[:1]

    x = tokens[...]
    for part, row in ((0, 0), (1, None), (2, 1)):
        columns = slice(part * width, (part + 1) * width)
        value = mm(x, weights[:, columns])
        if row is not None:
            value = value + vectors[row : row + 1, :]
        qkv[:, columns] = value.astype(BF16)


def attend_kernel(seq, words, regions, qkv, mixed):
    width = mixed.shape[1]
    step = pl.program_id(0)
    for k in range(STEP // seq):
        rows = slice(k * seq, (k + 1) * seq)
        pair = step * (STEP // seq) + k
        valid = valid_slots(words[pair], regions[pair], seq)
        for h in range(HEADS // 2):
            lanes = slice(h * 128, (h + 1) * 128)
            queries = stacked(qkv[rows, lanes] * HEAD_DIM ** (-0.5))
            keys = qkv[rows, width + h * 128 : width + (h + 1) * 128]
            values = qkv[rows, 2 * width + h * 128 : 2 * width + (h + 1) * 128]
            scores = jnp.where(valid, mm_nt(queries, keys), -1000000000.0)
            expo = jnp.exp(scores - jnp.max(scores, -1, keepdims=True)).astype(BF16)
            both = mm(expo, jnp.concatenate([values, jnp.ones_like(values)], 1))
            mixed[rows, lanes] = (unstacked(both[:, :128]) / unstacked(both[:, 128:])).astype(BF16)


def settle_kernel(count, seq, *refs):
    offsets, base = refs[:2]
    pieces = refs[2 : 2 + count]
    tokens, cotangent, mixed, pos, vectors, hidden, compact, proj, sems = refs[2 + count :]
    width = tokens.shape[1]
    step = pl.program_id(0)

    @pl.when(step == 0)
    def _():
        copies = start_pieces(pieces, offsets, proj, sems, 3 * width)
        compact[...] = jnp.zeros_like(compact)
        for copy in copies:
            copy.wait()

    branch = mm(mixed[...], proj[...]) + vectors[2:3, :]
    normed, scale = norm_parts(tokens[...].astype(F32) + branch)
    value = normed * vectors[3:4, :] + vectors[4:5, :]
    hidden[...] = value
    high = scale.astype(BF16)
    rest = scale - high.astype(F32)
    middle = rest.astype(BF16)
    low = (rest - middle.astype(F32)).astype(BF16)
    lane = lax.broadcasted_iota(jnp.int32, (STEP, 128), 1)
    zero = jnp.zeros((STEP, 128), BF16)
    scales = jnp.where(lane == 0, high, jnp.where(lane == 1, middle, jnp.where(lane == 2, low, zero)))
    parts = (value.astype(BF16), normed.astype(BF16), mixed[...], cotangent[...], scales)
    for k in range(STEP // seq):
        pair = step * (STEP // seq) + k
        start = window_start(base[pair])
        chosen = selector(pos[pair], start, seq)
        at = 0
        for part in parts:
            columns = slice(at, at + part.shape[1])
            at += part.shape[1]
            got = mm(chosen, part[k * seq : (k + 1) * seq]).astype(BF16)
            compact[pl.ds(start, WINDOW), columns] = got


def gelu_parts(inner):
    cumul = 0.5 + 0.5 * lax.erf(inner * 0.7071067811865476)
    return inner * cumul, cumul


def live_inner_kernel(count, *refs):
    offsets, blocks = refs[:2]
    pieces = refs[2 : 2 + count]
    compact, bias, act_out, slope_out = refs[2 + count : 6 + count]
    weights, hidden, act, slope, sems, more = refs[6 + count :]
    width = hidden.shape[1]
    copies = start_pieces(pieces, offsets, weights, sems)
    count_live = blocks[0]

    def rows_of(b):
        return pl.ds(pl.multiple_of(b * LIVE, LIVE), LIVE)

    def load(b):
        return pltpu.make_async_copy(compact.at[rows_of(b), pl.ds(0, width)], hidden, more.at[0])

    load(0).start()
    for copy in copies:
        copy.wait()

    @pl.loop(0, count_live)
    def _(b):
        load(b).wait()
        x = hidden[...]
        for c in range(weights.shape[1] // width):
            columns = slice(c * width, (c + 1) * width)
            inner = mm(x, weights[:, columns]) + bias[:, columns]
            value, cumul = gelu_parts(inner)
            density = jnp.exp(-0.5 * inner * inner) * 0.3989422804014327
            act[:, columns] = value.astype(BF16)
            slope[:, columns] = (cumul + inner * density).astype(BF16)
        outs = [
            pltpu.make_async_copy(act, act_out.at[rows_of(b)], more.at[1]),
            pltpu.make_async_copy(slope, slope_out.at[rows_of(b)], more.at[2]),
        ]
        for copy in outs:
            copy.start()

        @pl.when(b + 1 < count_live)
        def _():
            load(b + 1).start()

        for copy in outs:
            copy.wait()


def ffn_kernel(hidden, bias, vectors, inner, back, *rest):
    result, act = rest[-2:]
    width = hidden.shape[1]
    x = hidden[...]
    low = x.astype(BF16)
    for c in range(inner.shape[1] // width):
        columns = slice(c * width, (c + 1) * width)
        value = mm(low, inner[:, columns]) + bias[:, columns]
        act[:, columns] = gelu_parts(value)[0].astype(BF16)
    second = mm(act[...], back[...]) + vectors[5:6, :]
    normed, _ = norm_parts(x + second)
    result[...] = (normed * vectors[6:7, :] + vectors[7:8, :]).astype(BF16)


def rows_of(b):
    return pl.ds(pl.multiple_of(b * LIVE, LIVE), LIVE)


def load_live(count_live, pairs, sems):
    def copies(b):
        here = rows_of(b)
        return [
            pltpu.make_async_copy(source(here), target.at[here], sems.at[j])
            for j, (source, target) in enumerate(pairs)
        ]

    for copy in copies(0):
        copy.start()

    def finish():
        for copy in copies(0):
            copy.wait()

        @pl.loop(1, count_live)
        def _(b):
            later = copies(b)
            for copy in later:
                copy.start()
            for copy in later:
                copy.wait()

    return finish


def store_live(count_live, pairs, sems):
    def copies(b):
        here = rows_of(b)
        return [
            pltpu.make_async_copy(source.at[here], target.at[here], sems.at[j])
            for j, (source, target) in enumerate(pairs)
        ]

    for copy in copies(0):
        copy.start()

    def finish():
        for copy in copies(0):
            copy.wait()

        @pl.loop(1, count_live)
        def _(b):
            later = copies(b)
            for copy in later:
                copy.start()
            for copy in later:
                copy.wait()

    return finish


def ffn_back_kernel(counts, *refs):
    inner_offsets, back_offsets, order, blocks = refs[:4]
    inner_pieces = refs[4 : 4 + counts[0]]
    back_pieces = refs[4 + counts[0] : 4 + sum(counts)]
    refs = refs[4 + sum(counts) :]
    compact_hbm, act_hbm, slope_hbm, vectors = refs[:4]
    inner_out, back_out = refs[4:6]
    keep_back, send_back, keep_inner, send_inner, d_hidden_out, sums, inner_sum = refs[6:13]
    back, inner, hidden, cotangent, act, slope, d_second, d_inner, d_hidden = refs[13:22]
    total, out_back, out_inner, turned, ordered, inner_sems, back_sems, more = refs[22:]
    width = inner.shape[0]
    size = inner.shape[1] // BLOCKS
    quarters = inner.shape[1] // width
    rows = width // BLOCKS
    half = BLOCKS // 2
    first = slice(0, LIVE)
    count_live = blocks[0]

    def live_copies(b):
        here = rows_of(b)
        return [
            pltpu.make_async_copy(compact_hbm.at[here, pl.ds(0, width)], hidden.at[here], more.at[0]),
            pltpu.make_async_copy(
                compact_hbm.at[here, pl.ds(3 * width, width)], cotangent.at[here], more.at[1]
            ),
            pltpu.make_async_copy(act_hbm.at[here], act.at[here], more.at[2]),
            pltpu.make_async_copy(slope_hbm.at[here], slope.at[here], more.at[3]),
        ]

    now = live_copies(0)
    for copy in now:
        copy.start()
    back_copies = start_pieces(back_pieces, back_offsets, back, back_sems)
    inner_copies = start_pieces(inner_pieces, inner_offsets, inner, inner_sems)
    sums[...] = jnp.zeros_like(sums)
    inner_sum[...] = jnp.zeros_like(inner_sum)
    for copy in now:
        copy.wait()

    @pl.loop(1, count_live)
    def _(b):
        later = live_copies(b)
        for copy in later:
            copy.start()
        for copy in later:
            copy.wait()

    for copy in back_copies:
        copy.wait()
    exports = [
        pltpu.make_async_copy(back, back_out, back_sems.at[0]),
        pltpu.make_async_copy(inner, inner_out, inner_sems.at[0]),
    ]
    exports[0].start()

    @pl.loop(0, count_live)
    def _(b):
        here = rows_of(b)
        second = mm(act[here, :], back[...]) + vectors[5:6, :]
        normed, scale = norm_parts(hidden[here, :].astype(F32) + second)
        d_out = cotangent[here, :].astype(F32)
        sums[6:7, :] += column_sum(d_out * normed)
        sums[7:8, :] += column_sum(d_out)
        d_r2 = norm_grad(d_out * vectors[6:7, :], normed, scale)
        low = d_r2.astype(BF16)
        d_second[here, :] = low
        sums[5:6, :] += column_sum(low.astype(F32))
        d_hidden[here, :] = d_r2

    single = count_live == 1
    outs = []
    for i in range(BLOCKS):
        chunk = pl.ds(pl.multiple_of(order[i] * size, 128), size)

        @pl.when(single)
        def _():
            out_back[i] = mm_tn(act[first, chunk], d_second[first, :]).astype(BF16)

        @pl.when(jnp.logical_not(single))
        def _():
            total[:size, :] = mm_tn(act[first, chunk], d_second[first, :])

            @pl.loop(1, count_live)
            def _(b):
                here = rows_of(b)
                total[:size, :] += mm_tn(act[here, chunk], d_second[here, :])

            out_back[i] = total[:size, :].astype(BF16)

        target = keep_back.at[i] if i < half else send_back.at[i - half]
        outs.append(pltpu.make_async_copy(out_back.at[i], target, more.at[4 + i]))
        outs[-1].start()
    for copy in inner_copies:
        copy.wait()
    exports[1].start()

    @pl.loop(0, count_live)
    def _(b):
        here = rows_of(b)
        grad = d_second[here, :]
        for c in range(quarters):
            columns = slice(c * width, (c + 1) * width)
            d_act = mm_nt(grad, back[columns, :])
            low = (d_act * slope[here, columns].astype(F32)).astype(BF16)
            d_inner[here, columns] = low
            inner_sum[:, columns] += column_sum(low.astype(F32))
            d_hidden[here, :] += mm_nt(low, inner[:, columns])

    def hidden_copy(b):
        return pltpu.make_async_copy(
            d_hidden.at[rows_of(b)], d_hidden_out.at[rows_of(b)], more.at[0]
        )

    hidden_copy(0).start()

    @pl.loop(0, count_live)
    def _(b):
        here = rows_of(b)
        turned[...] = hidden[here, :].T
        for i in range(BLOCKS):
            start = pl.multiple_of(order[i] * rows, 16)
            ordered[b, i * rows : (i + 1) * rows, :] = turned[pl.ds(start, rows), :]

    for c in range(quarters):
        columns = slice(c * width, (c + 1) * width)
        target = slice(c * rows, (c + 1) * rows)

        @pl.when(single)
        def _():
            value = mm(ordered[0], d_inner[first, columns]).astype(BF16)
            for i in range(BLOCKS):
                out_inner[i, target, :] = value[i * rows : (i + 1) * rows, :]

        @pl.when(jnp.logical_not(single))
        def _():
            total[...] = mm(ordered[0], d_inner[first, columns])

            @pl.loop(1, count_live)
            def _(b):
                total[...] += mm(ordered[b], d_inner[rows_of(b), columns])

            for i in range(BLOCKS):
                out_inner[i, target, :] = total[i * rows : (i + 1) * rows, :].astype(BF16)

        for j, out in enumerate((keep_inner, send_inner)):
            blocks_out = pl.ds(j * half, half)
            part = pl.ds(c * rows, rows)
            source = out_inner.at[blocks_out, part]
            outs.append(pltpu.make_async_copy(source, out.at[:, part], more.at[12 + 2 * c + j]))
            outs[-1].start()
    hidden_copy(0).wait()

    @pl.loop(1, count_live)
    def _(b):
        hidden_copy(b).start()
        hidden_copy(b).wait()

    for copy in outs + exports:
        copy.wait()


def by_head(block):
    lane = lax.broadcasted_iota(jnp.int32, block.shape, 1) // HEAD_DIM
    zero = jnp.zeros_like(block)
    return jnp.concatenate([jnp.where(lane == h, block, zero) for h in range(HEADS)], 0)


def from_heads(block):
    rows = block.shape[0] // HEADS
    lane = lax.broadcasted_iota(jnp.int32, (rows, 128), 1)
    parts = []
    for h in range(HEADS // 2):
        lanes = slice(h * 128, (h + 1) * 128)
        left = block[2 * h * rows : (2 * h + 1) * rows, lanes]
        right = block[(2 * h + 1) * rows : (2 * h + 2) * rows, lanes]
        parts.append(jnp.where(lane < HEAD_DIM, left, right))
    return jnp.concatenate(parts, 1)


def attend_back_kernel(count, seq, shard_rows, *refs):
    offsets, order, base, words, regions, blocks = refs[:6]
    pieces = refs[6 : 6 + count]
    refs = refs[6 + count :]
    compact, d_hidden_hbm, qkv_hbm, tokens_hbm, vectors, ffn_sums, inner_sum, pos = refs[:8]
    d_qkv_out, d_r1_out, keep_out, send_out = refs[8:12]
    weights, normed_in, mixed, scales, d_hidden, qkv, tokens, d_r1, d_mixed = refs[12:21]
    d_query, d_keys, d_values, d_qkv, total, out, sums = refs[21:28]
    turned, mixed_turned, tokens_turned, sems, more = refs[28:]
    width = weights.shape[0]
    rows = width // BLOCKS
    half = BLOCKS // 2
    pairs = pos.shape[0]
    count_live = blocks[0]

    loads = [
        (lambda here: compact.at[here, pl.ds(width, width)], normed_in),
        (lambda here: compact.at[here, pl.ds(2 * width, width)], mixed),
        (lambda here: compact.at[here, pl.ds(4 * width, 128)], scales),
        (lambda here: d_hidden_hbm.at[here], d_hidden),
    ]
    loaded = load_live(count_live, loads, more)
    weight_copies = start_pieces(pieces, offsets, weights, sems, 3 * width)
    qkv_copy = pltpu.make_async_copy(qkv_hbm, qkv, more.at[4])
    tokens_copy = pltpu.make_async_copy(tokens_hbm, tokens, more.at[5])
    qkv_copy.start()
    tokens_copy.start()
    d_r1[...] = jnp.zeros_like(d_r1)
    sums[...] = ffn_sums[...]
    loaded()
    for copy in weight_copies:
        copy.wait()

    @pl.loop(0, count_live)
    def _(b):
        here = rows_of(b)
        grad = d_hidden[here, :]
        normed = normed_in[here, :].astype(F32)
        scale = jnp.sum(scales[here, :].astype(F32), -1, keepdims=True)
        sums[3:4, :] += column_sum(grad * normed)
        sums[4:5, :] += column_sum(grad)
        low = norm_grad(grad * vectors[3:4, :], normed, scale).astype(BF16)
        sums[2:3, :] += column_sum(low.astype(F32))
        d_r1[here, :] = low
        d_mixed[here, :] = mm_nt(low, weights[...]).astype(BF16)

    def in_order(source, target):
        turned[:, : source.shape[0]] = source.T
        for i in range(BLOCKS):
            start = pl.multiple_of(order[i] * rows, 16)
            target[i * rows : (i + 1) * rows, :] = turned[pl.ds(start, rows), : source.shape[0]]

    outs = []

    def spread(value, first, size):
        low = value.astype(BF16)
        for i in range(BLOCKS):
            out[i, :, first : first + size] = low[i * rows : (i + 1) * rows, :size]
        columns = pl.ds(first, size)
        for j, target in enumerate((keep_out, send_out)):
            source = out.at[pl.ds(j * half, half), :, columns]
            sem = more.at[6 + len(outs)]
            outs.append(pltpu.make_async_copy(source, target.at[:, :, columns], sem))
            outs[-1].start()

    in_order(mixed[:LIVE, :], mixed_turned)

    @pl.when(count_live == 1)
    def _():
        total[...] = mm(mixed_turned[...], d_r1[:LIVE, :])

    @pl.when(count_live > 1)
    def _():
        total[...] = mm(mixed_turned[...], d_r1[:LIVE, :])

        @pl.loop(1, count_live)
        def _(b):
            here = rows_of(b)
            in_order(mixed[here, :], mixed_turned)
            total[...] += mm(mixed_turned[...], d_r1[here, :])

    spread(total[...], 3 * width, width)
    tokens_copy.wait()
    in_order(tokens[...], tokens_turned)
    qkv_copy.wait()

    def pair_part(pair, b):
        mine = pl.ds(pl.multiple_of(pair * seq, seq), seq)
        valid = valid_slots(words[pair], regions[pair], seq)
        first = pl.multiple_of(base[pair] + b * PART, PART)
        row = lax.broadcasted_iota(jnp.int32, (PART, seq), 0) + first
        chosen = jnp.where(row == pos[pair], 1.0, 0.0).astype(BF16)
        live_query = mm(chosen, qkv[mine, :width]).astype(BF16) * HEAD_DIM ** (-0.5)
        queries = by_head(live_query)
        grad = d_mixed[pl.ds(first, PART), :]
        row = lax.broadcasted_iota(jnp.int32, grad.shape, 0) + first
        grad = by_head(jnp.where(row < base[pair + 1], grad, jnp.zeros_like(grad)))
        keys = qkv[mine, width : 2 * width]
        probs = probabilities(queries, keys, valid)
        d_probs = mm_nt(grad, qkv[mine, 2 * width :])
        inside = jnp.sum(d_probs * probs, -1, keepdims=True)
        d_scores = (probs * (d_probs - inside)).astype(BF16)
        part = (from_heads(mm(d_scores, keys)) * HEAD_DIM ** (-0.5)).astype(BF16)
        return mm_tn(chosen, part), mm_tn(d_scores, queries), mm_tn(probs.astype(BF16), grad)

    @pl.loop(0, pairs // TOGETHER)
    def _(step):
        group = [step * TOGETHER + k for k in range(TOGETHER)]
        trips = (base[group[0] + 1] - base[group[0]]) // PART
        for pair in group[1:]:
            trips = jnp.maximum(trips, (base[pair + 1] - base[pair]) // PART)
        for k, pair in enumerate(group):
            for ref, value in zip((d_query, d_keys, d_values), pair_part(pair, 0)):
                ref[k] = value

        @pl.loop(1, trips)
        def _(b):
            for k, pair in enumerate(group):
                for ref, value in zip((d_query, d_keys, d_values), pair_part(pair, b)):
                    ref[k] += value

        for k, pair in enumerate(group):
            mine = pl.ds(pl.multiple_of(pair * seq, seq), seq)
            for part, ref in enumerate((d_query, d_keys, d_values)):
                low = ref[k].astype(BF16)
                d_qkv[mine, part * width : (part + 1) * width] = low
                if part != 1:
                    row = 0 if part == 0 else 1
                    sums[row : row + 1, :] += column_sum(low.astype(F32))

    column_form = jnp.broadcast_to(inner_sum[...], (8, inner_sum.shape[1])).T
    quarters = inner_sum.shape[1] // width
    block = jnp.concatenate([sums[...], jnp.zeros((128 - sums.shape[0], width), F32)], 0).T
    lane = lax.broadcasted_iota(jnp.int32, block.shape, 1)
    for k in range(quarters):
        starts = [(s * quarters + k) * shard_rows for s in range(width // shard_rows)]
        column = jnp.concatenate([column_form[s : s + shard_rows, :1] for s in starts], 0)
        block = jnp.where(lane == 8 + k, column, block)
    total[:, :128] = block
    spread(
        jnp.concatenate(
            [total[pl.ds(pl.multiple_of(order[i] * rows, 8), rows), :128] for i in range(BLOCKS)], 0
        ),
        4 * width,
        128,
    )
    for part in range(3):
        columns = slice(part * width, (part + 1) * width)
        spread(mm(tokens_turned[...], d_qkv[:, columns]), part * width, width)

    outs += [
        pltpu.make_async_copy(d_qkv, d_qkv_out, more.at[6 + len(outs)]),
        pltpu.make_async_copy(d_r1, d_r1_out, more.at[7 + len(outs)]),
    ]
    outs[-2].start()
    outs[-1].start()
    for copy in outs:
        copy.wait()


def input_grad_kernel(count, seq, *refs):
    offsets, base = refs[:2]
    pieces = refs[2 : 2 + count]
    d_qkv, d_r1, pos, out, weights, sems = refs[2 + count :]
    step = pl.program_id(0)

    @pl.when(step == 0)
    def _():
        for copy in start_pieces(pieces, offsets, weights, sems):
            copy.wait()

    value = mm_nt(d_qkv[...], weights[...])
    for k in range(STEP // seq):
        pair = step * (STEP // seq) + k
        start = window_start(base[pair])
        chosen = selector(pos[pair], start, seq)
        rows = slice(k * seq, (k + 1) * seq)
        out[rows, :] = value[rows] + mm_tn(chosen, d_r1[pl.ds(start, WINDOW), :])


def swap(value, bit):
    return lax.ppermute(value, "shard", [(i, i ^ bit) for i in range(8)])


def after(value, *others):
    return lax.optimization_barrier((value,) + others)[0]


def far_swap(by_x, by_y):
    half = by_x.shape[0] // 2
    return swap(by_y[:half], XBIT), swap(by_x[half:], YBIT)


def near_and_far(mine, by_x, by_y, by_both):
    far = XBIT | YBIT
    half = mine.shape[0] // 2
    near = [(mine, 0, 0), (by_x, XBIT, 0), (by_y, YBIT, 0)]
    return near + [(by_both[0], far, 0), (by_both[1], far, half)]


def chip_pieces(mine, others):
    keys = (0, XBIT, YBIT, XBIT | YBIT)
    return [(v, key, 0) for v, key in zip((mine,) + tuple(others), keys)]


def with_core(pieces, others):
    return pieces + [(v, key | CORE, row) for v, (_, key, row) in zip(others, pieces)]


class Sum:
    def __init__(self, keep, send):
        self.keep = keep
        self.got = swap(send, CORE)
        z = lax.axis_index("rep")
        self.ends = (z == 0) | (z == 3)

    def wait(self, names, others):
        values = tuple(getattr(self, name) for name in names)
        got = lax.optimization_barrier(values + tuple(others))
        for name, value in zip(names, got):
            setattr(self, name, value)

    def chip(self, block, bottom):
        half = self.keep.shape[1] // 2
        rows = slice(half, None) if bottom else slice(0, half)
        return self.keep[block, rows].astype(F32) + self.got[block, rows].astype(F32)

    def near(self, *others):
        self.wait(("keep", "got"), others)
        sent = self.chip(slice(1, 3), False).astype(BF16), self.chip(slice(2, 4), True).astype(BF16)
        self.got_a, self.got_b = swap(sent[0], XBIT), swap(sent[1], YBIT)
        return sent

    def far(self, *others):
        self.wait(("got_a", "got_b"), others)
        send_a = (self.chip(3, False) + self.got_a[1].astype(F32)).astype(BF16)
        send_b = (self.chip(1, True) + self.got_b[0].astype(F32)).astype(BF16)
        self.far_a, self.far_b = swap(send_a, YBIT), swap(send_b, XBIT)
        return send_a, send_b

    def halves(self):
        a = self.chip(0, False) + self.got_a[0].astype(F32) + self.far_a.astype(F32)
        b = self.chip(0, True) + self.got_b[1].astype(F32) + self.far_b.astype(F32)
        return a, b

    def rep_first(self, *others):
        self.wait(("far_a", "far_b"), others)
        a, b = self.halves()
        sent = jnp.where(self.ends, b, a).astype(BF16)
        self.across = lax.ppermute(sent, "rep", PAIRS)
        return (sent,)

    def rep_second(self, *others):
        self.wait(("across",), others)
        a, b = self.halves()
        self.total = (jnp.where(self.ends, a, b) + self.across.astype(F32)).astype(BF16)
        self.across = lax.ppermute(self.total, "rep", ACROSS)
        return (self.total,)

    def rep_third(self, *others):
        self.wait(("across",), others)
        self.low = (self.total.astype(F32) + self.across.astype(F32)).astype(BF16)
        self.other = lax.ppermute(self.low, "rep", PAIRS)
        return (self.low,)

    def done(self):
        top = jnp.where(self.ends, self.low, self.other)
        bottom = jnp.where(self.ends, self.other, self.low)
        return jnp.concatenate([top, bottom], 0).astype(F32)


class EarlySum(Sum):
    def part(self, start, stop, other=False):
        half = self.keep.shape[1] // 2
        first = jnp.where(self.ends == other, half, 0)
        return sum(
            lax.dynamic_slice(v, (start, first, 0), (stop - start, half, v.shape[2])).astype(F32)
            for v in (self.keep, self.got)
        )

    def rep_early(self, *others):
        self.wait(("keep", "got"), others)
        sent = self.part(0, 4, other=True).astype(BF16)
        self.extra = lax.ppermute(sent, "rep", PAIRS)
        return (sent,)

    def near(self, *others):
        self.wait(("keep", "got", "extra"), others)
        sent = (self.part(1, 3) + self.extra[1:3].astype(F32)).astype(BF16)
        self.got_a = swap(sent, XBIT)
        return (sent,)

    def far(self, *others):
        self.wait(("got_a",), others)
        sent = self.part(3, 4)[0] + self.extra[3].astype(F32) + self.got_a[1].astype(F32)
        sent = sent.astype(BF16)
        self.far_a = swap(sent, YBIT)
        return (sent,)

    def rep_second(self, *others):
        self.wait(("far_a",), others)
        total = self.part(0, 1)[0] + self.extra[0].astype(F32) + self.got_a[0].astype(F32)
        self.total = (total + self.far_a.astype(F32)).astype(BF16)
        self.across = lax.ppermute(self.total, "rep", ACROSS)
        return (self.total,)


PAIRS = [(0, 1), (1, 0), (2, 3), (3, 2)]
ACROSS = [(0, 3), (3, 0), (1, 2), (2, 1)]


def whole(shape, dtype=None):
    del dtype
    return pl.BlockSpec(shape, lambda *_: (0,) * len(shape))


def steps(width):
    return pl.BlockSpec((STEP, width), lambda i: (i, 0))


SCALARS = pl.BlockSpec(memory_space=pltpu.SMEM)
ANYWHERE = pl.BlockSpec(memory_space=pl.ANY)


def shape_of(*dims, dtype=BF16):
    return jax.ShapeDtypeStruct(dims, dtype)


def params(limit=VMEM):
    return pltpu.CompilerParams(vmem_limit_bytes=limit)


def cost(time):
    return pl.CostEstimate(flops=int(time * 1e8), bytes_accessed=0, transcendentals=0)


def local(
    tokens,
    word_counts,
    region_counts,
    task_labels,
    masked_slots,
    qkv_weight,
    query_bias,
    value_bias,
    out_weight,
    out_bias,
    attn_gain,
    attn_shift,
    inner_weight,
    inner_bias,
    back_weight,
    back_bias,
    ffn_gain,
    ffn_shift,
    cotangent,
    *,
    shards,
    reps,
):
    pairs = word_counts.shape[0]
    count, width = tokens.shape
    hidden = back_weight.shape[0] * shards
    seq = count // pairs
    grid = (count // STEP,)
    cap = -(-pairs * WINDOW // LIVE) * LIVE
    cube = shards == 8 and reps == 4
    rows = width // shards
    me = lax.axis_index("shard")

    slots = jnp.arange(seq, dtype=jnp.int32)[None, :]
    words = word_counts[:, None]
    in_regions = (slots >= WORD_SLOTS) & (slots < WORD_SLOTS + region_counts[:, None])
    picked = masked_slots == 1
    labels = task_labels[:, None]
    live = (
        (labels == 0) & picked & (slots >= 1) & (slots < words)
        | (labels == 1) & picked & in_regions
        | (labels == 2) & (slots == 0)
    )
    live_count = jnp.sum(live.astype(jnp.int32), 1)
    taken = (live_count + PART - 1) // PART * PART
    base = jnp.concatenate([jnp.zeros((1,), jnp.int32), jnp.cumsum(taken)])
    rank = jnp.cumsum(live.astype(jnp.int32), 1) - 1 + base[:-1, None]
    pos = jnp.where(live, rank, -1).reshape(pairs, 1, seq)
    blocks = jnp.maximum(1, (base[-1:] + LIVE - 1) // LIVE)

    vectors = jnp.stack(
        [query_bias, value_bias, out_bias, attn_gain, attn_shift, back_bias, ffn_gain, ffn_shift]
        + [inner_bias[k * rows : (k + 1) * rows] for k in range(hidden // width)],
        1,
    )
    vectors = jnp.pad(vectors, ((0, 0), (0, 128 - vectors.shape[1])))
    attn_shard = jnp.concatenate([qkv_weight, out_weight, vectors], 1)
    def offsets(size, halves):
        if not cube:
            return jnp.zeros((1,), jnp.int32)
        keys = [0, XBIT, YBIT, XBIT | YBIT] + [XBIT | YBIT] * halves
        keys = jnp.array(keys, jnp.int32) ^ me
        starts = jnp.array([0] * 4 + [size // 2] * halves, jnp.int32)
        return jnp.concatenate([keys * size + starts, (keys ^ CORE) * size + starts])

    attn_offsets, inner_offsets = offsets(rows, 1), offsets(rows, 0)
    back_offsets = offsets(back_weight.shape[0], 0)
    order = jnp.arange(BLOCKS, dtype=jnp.int32)
    if cube:
        order = jnp.array([0, 2, 6, 4, 1, 3, 7, 5], jnp.int32) ^ me
    indices = (base, pos, blocks, attn_offsets, inner_offsets, back_offsets, order)
    if cube:
        attn_x, attn_y = swap(attn_shard, XBIT), swap(attn_shard, YBIT)
        own = [swap(v, CORE) for v in (attn_shard, inner_weight, back_weight)]
        near = lax.optimization_barrier((attn_x, attn_y, inner_weight, indices, *own))
        attn_x, attn_y, inner_weight, indices, *own = near
        attn_far = far_swap(attn_x, attn_y)
        inner_x, inner_y = swap(inner_weight, XBIT), swap(inner_weight, YBIT)
        attn_core = swap(attn_x, CORE), swap(attn_y, CORE)
        attn_far, attn_core, back_weight = lax.optimization_barrier((attn_far, attn_core, back_weight))
        back_x, back_y = swap(back_weight, XBIT), swap(back_weight, YBIT)
        attn = near_and_far(attn_shard, attn_x, attn_y, attn_far)
        attn_core = (own[0],) + attn_core + tuple(swap(v, CORE) for v in attn_far)
        attn = with_core(attn, attn_core)
    else:
        attn, inner, back = (
            [(lax.all_gather(v, "shard", axis=0, tiled=True), 0, 0)]
            for v in (attn_shard, inner_weight, back_weight)
        )
    base, pos, blocks, attn_offsets, inner_offsets, back_offsets, order = indices

    columns = 4 * width + 128
    attn_count = len(attn)
    attn_pieces = [v for v, _, _ in attn]
    qkv, vector_rows, inner_bias_full = pl.pallas_call(
        functools.partial(project_kernel, attn_count, rows),
        grid=grid,
        in_specs=[SCALARS] + [ANYWHERE] * attn_count + [steps(width)],
        out_specs=[steps(3 * width), whole((16, width)), whole((1, hidden))],
        out_shape=[
            shape_of(count, 3 * width),
            shape_of(16, width, dtype=F32),
            shape_of(1, hidden, dtype=F32),
        ],
        scratch_shapes=[
            pltpu.VMEM((width, columns), BF16),
            pltpu.SemaphoreType.DMA((attn_count,)),
        ],
        compiler_params=params(),
        cost_estimate=cost(9),
        name="project",
    )(attn_offsets, *attn_pieces, tokens)
    if cube:
        inner_x, inner_y, qkv = lax.optimization_barrier((inner_x, inner_y, qkv))
        inner_far = swap(inner_y, XBIT)
        inner_core = swap(inner_x, CORE), swap(inner_y, CORE)
    mixed = pl.pallas_call(
        functools.partial(attend_kernel, seq),
        grid=grid,
        in_specs=[SCALARS] * 2 + [steps(3 * width)],
        out_specs=steps(width),
        out_shape=shape_of(count, width),
        compiler_params=params(),
        cost_estimate=cost(8),
        name="attend",
    )(word_counts, region_counts, qkv)
    if cube:
        back_x, back_y, inner_core, mixed = lax.optimization_barrier(
            (back_x, back_y, inner_core, mixed)
        )
        back_far = swap(back_x, YBIT)
        back_core = swap(back_x, CORE), swap(back_y, CORE)
    hidden1, compact = pl.pallas_call(
        functools.partial(settle_kernel, attn_count, seq),
        grid=grid,
        in_specs=[SCALARS] * 2
        + [ANYWHERE] * attn_count
        + [steps(width)] * 3
        + [whole((pairs, 1, seq)), whole((16, width))],
        out_specs=[steps(width), whole((cap, columns))],
        out_shape=[shape_of(count, width, dtype=F32), shape_of(cap, columns)],
        scratch_shapes=[
            pltpu.VMEM((width, width), BF16),
            pltpu.SemaphoreType.DMA((attn_count,)),
        ],
        compiler_params=params(),
        cost_estimate=cost(9),
        name="settle",
    )(attn_offsets, base, *attn_pieces, tokens, cotangent, mixed, pos, vector_rows)

    if cube:
        inner_far, back_far, back_core, hidden1 = lax.optimization_barrier(
            (inner_far, back_far, back_core, hidden1)
        )
        inner = chip_pieces(inner_weight, (inner_x, inner_y, inner_far))
        inner = with_core(inner, (own[1],) + inner_core + (swap(inner_far, CORE),))
    inner_count = len(inner)
    inner_pieces = [v for v, _, _ in inner]
    in_vmem = pl.BlockSpec(memory_space=pltpu.VMEM)
    live_act, live_slope = pl.pallas_call(
        functools.partial(live_inner_kernel, inner_count),
        in_specs=[SCALARS] * 2 + [ANYWHERE] * (inner_count + 1) + [in_vmem],
        out_specs=[ANYWHERE] * 2,
        out_shape=[shape_of(cap, hidden)] * 2,
        scratch_shapes=[
            pltpu.VMEM((width, hidden), BF16),
            pltpu.VMEM((LIVE, width), BF16),
            pltpu.VMEM((LIVE, hidden), BF16),
            pltpu.VMEM((LIVE, hidden), BF16),
            pltpu.SemaphoreType.DMA((inner_count,)),
            pltpu.SemaphoreType.DMA((3,)),
        ],
        compiler_params=params(),
        cost_estimate=cost(6),
        name="live_inner",
    )(inner_offsets, blocks, *inner_pieces, compact, inner_bias_full)

    if cube:
        back = chip_pieces(back_weight, (back_x, back_y, back_far))
        back = with_core(back, (own[2],) + back_core + (swap(back_far, CORE),))
    back_count = len(back)
    back_pieces = [v for v, _, _ in back]

    half = BLOCKS // 2
    size = hidden // BLOCKS
    block = width // BLOCKS
    inner_full, back_full, keep_back, send_back, keep_inner, send_inner, d_hidden1, sums, inner_sum = pl.pallas_call(
        functools.partial(ffn_back_kernel, (inner_count, back_count)),
        in_specs=[SCALARS] * 4 + [ANYWHERE] * (inner_count + back_count + 3) + [in_vmem],
        out_specs=[ANYWHERE] * 7 + [in_vmem] * 2,
        out_shape=[
            shape_of(width, hidden),
            shape_of(hidden, width),
            shape_of(half, size, width),
            shape_of(half, size, width),
            shape_of(half, size, width),
            shape_of(half, size, width),
            shape_of(cap, width, dtype=F32),
            shape_of(16, width, dtype=F32),
            shape_of(1, hidden, dtype=F32),
        ],
        scratch_shapes=[
            pltpu.VMEM((hidden, width), BF16),
            pltpu.VMEM((width, hidden), BF16),
            pltpu.VMEM((cap, width), BF16),
            pltpu.VMEM((cap, width), BF16),
            pltpu.VMEM((cap, hidden), BF16),
            pltpu.VMEM((cap, hidden), BF16),
            pltpu.VMEM((cap, width), BF16),
            pltpu.VMEM((cap, hidden), BF16),
            pltpu.VMEM((cap, width), F32),
            pltpu.VMEM((width, width), F32),
            pltpu.VMEM((BLOCKS, size, width), BF16),
            pltpu.VMEM((BLOCKS, size, width), BF16),
            pltpu.VMEM((width, LIVE), BF16),
            pltpu.VMEM((cap // LIVE, width, LIVE), BF16),
            pltpu.SemaphoreType.DMA((inner_count,)),
            pltpu.SemaphoreType.DMA((back_count,)),
            pltpu.SemaphoreType.DMA((12 + 2 * hidden // width,)),
        ],
        compiler_params=params(),
        cost_estimate=cost(13),
        name="ffn_back",
    )(
        inner_offsets,
        back_offsets,
        order,
        blocks,
        *inner_pieces,
        *back_pieces,
        compact,
        live_act,
        live_slope,
        vector_rows,
    )

    if cube:
        back_total = Sum(keep_back, send_back)
        inner_total = EarlySum(keep_inner, send_inner)

    d_qkv, d_r1, keep_attn, send_attn = pl.pallas_call(
        functools.partial(attend_back_kernel, attn_count, seq, rows),
        in_specs=[SCALARS] * 6 + [ANYWHERE] * (attn_count + 4) + [in_vmem] * 4,
        out_specs=[ANYWHERE] * 4,
        out_shape=[
            shape_of(count, 3 * width),
            shape_of(cap, width),
            shape_of(half, block, columns),
            shape_of(half, block, columns),
        ],
        scratch_shapes=[
            pltpu.VMEM((width, width), BF16),
            pltpu.VMEM((cap, width), BF16),
            pltpu.VMEM((cap, width), BF16),
            pltpu.VMEM((cap, 128), BF16),
            pltpu.VMEM((cap, width), F32),
            pltpu.VMEM((count, 3 * width), BF16),
            pltpu.VMEM((count, width), BF16),
            pltpu.VMEM((cap, width), BF16),
            pltpu.VMEM((cap, width), BF16),
            pltpu.VMEM((TOGETHER, seq, width), F32),
            pltpu.VMEM((TOGETHER, seq, width), F32),
            pltpu.VMEM((TOGETHER, seq, width), F32),
            pltpu.VMEM((count, 3 * width), BF16),
            pltpu.VMEM((width, width), F32),
            pltpu.VMEM((BLOCKS, block, columns), BF16),
            pltpu.VMEM((16, width), F32),
            pltpu.VMEM((width, count), BF16),
            pltpu.VMEM((width, LIVE), BF16),
            pltpu.VMEM((width, count), BF16),
            pltpu.SemaphoreType.DMA((attn_count,)),
            pltpu.SemaphoreType.DMA((16 + count // STEP,)),
        ],
        compiler_params=params(),
        cost_estimate=cost(22),
        name="attend_back",
    )(
        attn_offsets,
        order,
        base,
        word_counts,
        region_counts,
        blocks,
        *attn_pieces,
        compact,
        d_hidden1,
        qkv,
        tokens,
        vector_rows,
        sums,
        inner_sum,
        pos,
    )

    def later(shift):
        return lambda i: (i + shift, 0)

    def ffn(first, number, x, *done):
        return pl.pallas_call(
            ffn_kernel,
            grid=(number,),
            in_specs=[pl.BlockSpec((STEP, width), later(first)), whole((1, hidden)), whole((16, width))]
            + [in_vmem] * 2
            + [ANYWHERE] * len(done),
            out_specs=pl.BlockSpec((STEP, width), later(first)),
            out_shape=shape_of(count, width),
            input_output_aliases={5: 0} if done else {},
            scratch_shapes=[pltpu.VMEM((STEP, hidden), BF16)],
            compiler_params=params(24 * 2**20),
            cost_estimate=cost(11),
            name="ffn",
        )(x, inner_bias_full, vector_rows, inner_full, back_full, *done)

    x = hidden1
    if cube:
        sent = back_total.near(d_r1)
        sent += inner_total.rep_early(*sent)
        attn_total = Sum(keep_attn, send_attn)
        sent += attn_total.near(*sent)
        x = after(hidden1, *sent)
    result = ffn(0, grid[0] - 1, x)
    if cube:
        sent = back_total.far(result)
        sent += attn_total.far(*sent)
        sent += back_total.rep_first(*sent)
        sent += inner_total.near(*sent)
        sent += attn_total.rep_first(*sent)
        sent += back_total.rep_second(*sent)
        d_qkv = after(d_qkv, *sent)

    input_grad = pl.pallas_call(
        functools.partial(input_grad_kernel, attn_count, seq),
        grid=grid,
        in_specs=[SCALARS] * 2
        + [ANYWHERE] * attn_count
        + [steps(3 * width), whole((cap, width)), whole((pairs, 1, seq))],
        out_specs=steps(width),
        out_shape=shape_of(count, width, dtype=F32),
        scratch_shapes=[
            pltpu.VMEM((width, 3 * width), BF16),
            pltpu.SemaphoreType.DMA((attn_count,)),
        ],
        compiler_params=params(24 * 2**20),
        cost_estimate=cost(9),
        name="input_grad",
    )(attn_offsets, base, *attn_pieces, d_qkv, d_r1, pos)

    if cube:
        sent = attn_total.rep_second(input_grad)
        sent += inner_total.far(*sent)
        sent += back_total.rep_third(*sent)
        x = after(hidden1, *sent)
    result = ffn(grid[0] - 1, 1, x, result)
    if cube:
        sent = inner_total.rep_second(result)

    quarters = hidden // width
    if cube:
        attn_total.rep_third(*sent)
        inner_total.rep_third()
        back_sum, inner_sum, attn_sum = (v.done() for v in (back_total, inner_total, attn_total))
        inner_sum = jnp.concatenate([inner_sum[c * block : (c + 1) * block] for c in range(quarters)], 1)
    else:
        back_grad = jnp.concatenate([keep_back, send_back]).reshape(hidden, width)
        inner_grad = jnp.concatenate([keep_inner, send_inner]).reshape(BLOCKS, quarters, block, width)
        inner_grad = inner_grad.transpose(0, 2, 1, 3).reshape(width, hidden)
        attn_grad = jnp.concatenate([keep_attn, send_attn]).reshape(width, columns)
        back_sum, inner_sum, attn_sum = (
            lax.psum(lax.psum_scatter(g, "shard", scatter_dimension=0, tiled=True), "rep").astype(F32)
            for g in (back_grad, inner_grad, attn_grad)
        )
    sums = attn_sum[:, 4 * width :].T
    return (
        result,
        input_grad,
        attn_sum[:, : 3 * width],
        sums[0],
        sums[1],
        attn_sum[:, 3 * width : 4 * width],
        sums[2],
        sums[3],
        sums[4],
        inner_sum,
        sums[8 : 8 + quarters].reshape(-1),
        back_sum,
        sums[5],
        sums[6],
        sums[7],
    )


def solution(mesh):
    rows, both, one = P(("rep", "shard"), None), P(("rep", "shard")), P("shard")
    matrix = P("shard", None)
    in_specs = (rows, both, both, both, rows, matrix, one, one, matrix, one, one, one)
    in_specs += (matrix, one, matrix, one, one, one, rows)
    out_specs = (rows, rows, matrix, one, one, matrix, one, one, one, matrix, one, matrix)
    out_specs += (one, one, one)
    sizes = dict(mesh.shape)

    def run(*args):
        return local(*args, shards=sizes["shard"], reps=sizes["rep"])

    return jax.shard_map(
        run, mesh=mesh, in_specs=in_specs, out_specs=out_specs, check_vma=False
    )
```

```python
import functools

import jax
import jax.numpy as jnp
from jax import lax
from jax.experimental import pallas as pl
from jax.experimental.pallas import tpu as pltpu
from jax.sharding import PartitionSpec as P

HEADS = 12
HEAD_DIM = 64
WORD_SLOTS = 60
CORE, XBIT, YBIT = 1, 2, 4
BLOCKS = 8
STEP = 256
LIVE = 192
WINDOW = 80
PART = 16
TOGETHER = 2
VMEM = 60 * 2**20
F32 = jnp.float32
BF16 = jnp.bfloat16


def mm(left, right):
    return jnp.dot(left, right, preferred_element_type=F32)


def mm_nt(left, right):
    return lax.dot_general(left, right, (((1,), (1,)), ((), ())), preferred_element_type=F32)


def mm_tn(left, right):
    return lax.dot_general(left, right, (((0,), (0,)), ((), ())), preferred_element_type=F32)


def norm_parts(value):
    mean = jnp.mean(value, -1, keepdims=True)
    centred = value - mean
    scale = lax.rsqrt(jnp.mean(centred * centred, -1, keepdims=True) + 1e-05)
    return centred * scale, scale


def norm_grad(grad, normed, scale):
    return scale * (
        grad
        - jnp.mean(grad, -1, keepdims=True)
        - normed * jnp.mean(grad * normed, -1, keepdims=True)
    )


def piece_at(index, size):
    return pl.ds(pl.multiple_of(index * size, 128), size)


def column_sum(value):
    return jnp.sum(value, 0, keepdims=True)


def start_pieces(pieces, offsets, scratch, sems, first=0, started=False):
    copies = []
    for j, piece in enumerate(pieces):
        start = pl.multiple_of(offsets[j], 16)
        source = piece.at[:, pl.ds(first, scratch.shape[1])]
        target = scratch.at[pl.ds(start, piece.shape[0]), :]
        copies.append(pltpu.make_async_copy(source, target, sems.at[j]))
        if not started:
            copies[-1].start()
    return copies


def stacked(block):
    lane = lax.broadcasted_iota(jnp.int32, block.shape, 1)
    zero = jnp.zeros_like(block)
    return jnp.concatenate(
        [jnp.where(lane < HEAD_DIM, block, zero), jnp.where(lane >= HEAD_DIM, block, zero)], 0
    )


def unstacked(block):
    rows = block.shape[0] // 2
    lane = lax.broadcasted_iota(jnp.int32, (rows, block.shape[1]), 1)
    return jnp.where(lane < HEAD_DIM, block[:rows], block[rows:])


def probabilities(queries, keys, valid):
    scores = jnp.where(valid, mm_nt(queries, keys), -1000000000.0)
    peak = jnp.max(scores, -1, keepdims=True)
    expo = jnp.exp(scores - peak)
    return expo * (1.0 / jnp.sum(expo, -1, keepdims=True))


def valid_slots(words, regions, seq):
    slot = lax.broadcasted_iota(jnp.int32, (1, seq), 1)
    return (slot < words) | ((slot >= WORD_SLOTS) & (slot < WORD_SLOTS + regions))


def selector(pos, start, seq):
    row = lax.broadcasted_iota(jnp.int32, (WINDOW, seq), 0) + start
    return jnp.where(row == pos, 1.0, 0.0).astype(BF16)


def window_start(base):
    return pl.multiple_of(base, PART)


def project_kernel(count, shard_rows, *refs):
    offsets = refs[0]
    pieces = refs[1 : 1 + count]
    tokens, qkv, vectors, bias, weights, sems = refs[1 + count :]
    width = tokens.shape[1]
    quarters = bias.shape[1] // width

    @pl.when(pl.program_id(0) == 0)
    def _():
        for copy in start_pieces(pieces, offsets, weights, sems):
            copy.wait()
        share = weights[:, 4 * width :].astype(F32)
        vectors[...] = share.T[: vectors.shape[0]]
        parts = []
        for s in range(width // shard_rows):
            for k in range(quarters):
                part = share[s * shard_rows : (s + 1) * shard_rows, 8 + k : 9 + k]
                parts.append(jnp.broadcast_to(part, (shard_rows, 8)))
        bias[...] = jnp.concatenate(parts, 0).T[:1]

    x = tokens[...]
    for part, row in ((0, 0), (1, None), (2, 1)):
        columns = slice(part * width, (part + 1) * width)
        value = mm(x, weights[:, columns])
        if row is not None:
            value = value + vectors[row : row + 1, :]
        qkv[:, columns] = value.astype(BF16)


def attend_kernel(seq, words, regions, qkv, mixed):
    width = mixed.shape[1]
    step = pl.program_id(0)
    for k in range(STEP // seq):
        rows = slice(k * seq, (k + 1) * seq)
        pair = step * (STEP // seq) + k
        valid = valid_slots(words[pair], regions[pair], seq)
        for h in range(HEADS // 2):
            lanes = slice(h * 128, (h + 1) * 128)
            queries = stacked(qkv[rows, lanes] * HEAD_DIM ** (-0.5))
            keys = qkv[rows, width + h * 128 : width + (h + 1) * 128]
            values = qkv[rows, 2 * width + h * 128 : 2 * width + (h + 1) * 128]
            scores = jnp.where(valid, mm_nt(queries, keys), -1000000000.0)
            expo = jnp.exp(scores - jnp.max(scores, -1, keepdims=True)).astype(BF16)
            both = mm(expo, jnp.concatenate([values, jnp.ones_like(values)], 1))
            mixed[rows, lanes] = (unstacked(both[:, :128]) / unstacked(both[:, 128:])).astype(BF16)


def settle_kernel(count, seq, *refs):
    offsets, base = refs[:2]
    pieces = refs[2 : 2 + count]
    tokens, cotangent, mixed, pos, vectors, hidden, compact, proj, sems = refs[2 + count :]
    width = tokens.shape[1]
    step = pl.program_id(0)

    @pl.when(step == 0)
    def _():
        copies = start_pieces(pieces, offsets, proj, sems, 3 * width)
        compact[...] = jnp.zeros_like(compact)
        for copy in copies:
            copy.wait()

    branch = mm(mixed[...], proj[...]) + vectors[2:3, :]
    normed, scale = norm_parts(tokens[...].astype(F32) + branch)
    value = normed * vectors[3:4, :] + vectors[4:5, :]
    hidden[...] = value
    high = scale.astype(BF16)
    rest = scale - high.astype(F32)
    middle = rest.astype(BF16)
    low = (rest - middle.astype(F32)).astype(BF16)
    lane = lax.broadcasted_iota(jnp.int32, (STEP, 128), 1)
    zero = jnp.zeros((STEP, 128), BF16)
    scales = jnp.where(lane == 0, high, jnp.where(lane == 1, middle, jnp.where(lane == 2, low, zero)))
    parts = (value.astype(BF16), normed.astype(BF16), mixed[...], cotangent[...], scales)
    for k in range(STEP // seq):
        pair = step * (STEP // seq) + k
        start = window_start(base[pair])
        chosen = selector(pos[pair], start, seq)
        at = 0
        for part in parts:
            columns = slice(at, at + part.shape[1])
            at += part.shape[1]
            got = mm(chosen, part[k * seq : (k + 1) * seq]).astype(BF16)
            compact[pl.ds(start, WINDOW), columns] = got


def gelu_parts(inner):
    cumul = 0.5 + 0.5 * lax.erf(inner * 0.7071067811865476)
    return inner * cumul, cumul


def ffn_kernel(hidden, bias, vectors, inner, back, *rest):
    result, act = rest[-2:]
    width = hidden.shape[1]
    x = hidden[...]
    low = x.astype(BF16)
    for c in range(inner.shape[1] // width):
        columns = slice(c * width, (c + 1) * width)
        value = mm(low, inner[:, columns]) + bias[:, columns]
        act[:, columns] = gelu_parts(value)[0].astype(BF16)
    second = mm(act[...], back[...]) + vectors[5:6, :]
    normed, _ = norm_parts(x + second)
    result[...] = (normed * vectors[6:7, :] + vectors[7:8, :]).astype(BF16)


def rows_of(b):
    return pl.ds(pl.multiple_of(b * LIVE, LIVE), LIVE)


def load_live(count_live, pairs, sems):
    def copies(b):
        here = rows_of(b)
        return [
            pltpu.make_async_copy(source(here), target.at[here], sems.at[j])
            for j, (source, target) in enumerate(pairs)
        ]

    for copy in copies(0):
        copy.start()

    def finish():
        for copy in copies(0):
            copy.wait()

        @pl.loop(1, count_live)
        def _(b):
            later = copies(b)
            for copy in later:
                copy.start()
            for copy in later:
                copy.wait()

    return finish


def store_live(count_live, pairs, sems):
    def copies(b):
        here = rows_of(b)
        return [
            pltpu.make_async_copy(source.at[here], target.at[here], sems.at[j])
            for j, (source, target) in enumerate(pairs)
        ]

    for copy in copies(0):
        copy.start()

    def finish():
        for copy in copies(0):
            copy.wait()

        @pl.loop(1, count_live)
        def _(b):
            later = copies(b)
            for copy in later:
                copy.start()
            for copy in later:
                copy.wait()

    return finish


def ffn_back_kernel(counts, *refs):
    inner_offsets, back_offsets, order, blocks = refs[:4]
    inner_pieces = refs[4 : 4 + counts[0]]
    back_pieces = refs[4 + counts[0] : 4 + sum(counts)]
    refs = refs[4 + sum(counts) :]
    compact_hbm, bias, vectors = refs[:3]
    inner_out, back_out = refs[3:5]
    keep_back, send_back, keep_inner, send_inner, d_hidden_out, sums, inner_sum = refs[5:12]
    back, inner, hidden, cotangent, act, slope, d_second, d_inner, d_hidden = refs[12:21]
    total, out_back, out_inner, turned, ordered, inner_sems, back_sems, more = refs[21:]
    width = inner.shape[0]
    size = inner.shape[1] // BLOCKS
    quarters = inner.shape[1] // width
    rows = width // BLOCKS
    half = BLOCKS // 2
    first = slice(0, LIVE)
    count_live = blocks[0]

    def live_copies(b):
        here = rows_of(b)
        return [
            pltpu.make_async_copy(compact_hbm.at[here, pl.ds(0, width)], hidden.at[here], more.at[0]),
            pltpu.make_async_copy(
                compact_hbm.at[here, pl.ds(3 * width, width)], cotangent.at[here], more.at[1]
            ),
        ]

    now = live_copies(0)
    for copy in now:
        copy.start()
    inner_copies = start_pieces(inner_pieces, inner_offsets, inner, inner_sems)
    back_copies = start_pieces(back_pieces, back_offsets, back, back_sems)
    sums[...] = jnp.zeros_like(sums)
    inner_sum[...] = jnp.zeros_like(inner_sum)
    for copy in now:
        copy.wait()

    @pl.loop(1, count_live)
    def _(b):
        later = live_copies(b)
        for copy in later:
            copy.start()
        for copy in later:
            copy.wait()

    for copy in inner_copies:
        copy.wait()

    @pl.loop(0, count_live)
    def _(b):
        here = rows_of(b)

        @pl.loop(0, quarters)
        def _(c):
            columns = piece_at(c, width)
            value = mm(hidden[here, :], inner[:, columns]) + bias[:, columns]
            grown, cumul = gelu_parts(value)
            density = jnp.exp(-0.5 * value * value) * 0.3989422804014327
            act[here, columns] = grown.astype(BF16)
            slope[here, columns] = (cumul + value * density).astype(BF16)

    for copy in back_copies:
        copy.wait()
    exports = [
        pltpu.make_async_copy(back, back_out, back_sems.at[0]),
        pltpu.make_async_copy(inner, inner_out, inner_sems.at[0]),
    ]
    exports[0].start()
    exports[1].start()

    @pl.loop(0, count_live)
    def _(b):
        here = rows_of(b)
        second = mm(act[here, :], back[...]) + vectors[5:6, :]
        normed, scale = norm_parts(hidden[here, :].astype(F32) + second)
        d_out = cotangent[here, :].astype(F32)
        sums[6:7, :] += column_sum(d_out * normed)
        sums[7:8, :] += column_sum(d_out)
        d_r2 = norm_grad(d_out * vectors[6:7, :], normed, scale)
        low = d_r2.astype(BF16)
        d_second[here, :] = low
        sums[5:6, :] += column_sum(low.astype(F32))
        d_hidden[here, :] = d_r2

    single = count_live == 1
    outs = []
    for i in range(BLOCKS):
        chunk = pl.ds(pl.multiple_of(order[i] * size, 128), size)

        @pl.when(single)
        def _():
            out_back[i] = mm_tn(act[first, chunk], d_second[first, :]).astype(BF16)

        @pl.when(jnp.logical_not(single))
        def _():
            total[:size, :] = mm_tn(act[first, chunk], d_second[first, :])

            @pl.loop(1, count_live)
            def _(b):
                here = rows_of(b)
                total[:size, :] += mm_tn(act[here, chunk], d_second[here, :])

            out_back[i] = total[:size, :].astype(BF16)

        target = keep_back.at[i] if i < half else send_back.at[i - half]
        outs.append(pltpu.make_async_copy(out_back.at[i], target, more.at[4 + i]))
        outs[-1].start()

    @pl.loop(0, count_live)
    def _(b):
        here = rows_of(b)
        grad = d_second[here, :]
        for c in range(quarters):
            columns = slice(c * width, (c + 1) * width)
            d_act = mm_nt(grad, back[columns, :])
            low = (d_act * slope[here, columns].astype(F32)).astype(BF16)
            d_inner[here, columns] = low
            inner_sum[:, columns] += column_sum(low.astype(F32))
            d_hidden[here, :] += mm_nt(low, inner[:, columns])

    def hidden_copy(b):
        return pltpu.make_async_copy(
            d_hidden.at[rows_of(b)], d_hidden_out.at[rows_of(b)], more.at[0]
        )

    hidden_copy(0).start()

    @pl.loop(0, count_live)
    def _(b):
        here = rows_of(b)
        turned[...] = hidden[here, :].T
        for i in range(BLOCKS):
            start = pl.multiple_of(order[i] * rows, 16)
            ordered[b, i * rows : (i + 1) * rows, :] = turned[pl.ds(start, rows), :]

    for c in range(quarters):
        columns = slice(c * width, (c + 1) * width)
        target = slice(c * rows, (c + 1) * rows)

        @pl.when(single)
        def _():
            value = mm(ordered[0], d_inner[first, columns]).astype(BF16)
            for i in range(BLOCKS):
                out_inner[i, target, :] = value[i * rows : (i + 1) * rows, :]

        @pl.when(jnp.logical_not(single))
        def _():
            total[...] = mm(ordered[0], d_inner[first, columns])

            @pl.loop(1, count_live)
            def _(b):
                total[...] += mm(ordered[b], d_inner[rows_of(b), columns])

            for i in range(BLOCKS):
                out_inner[i, target, :] = total[i * rows : (i + 1) * rows, :].astype(BF16)

        for j, out in enumerate((keep_inner, send_inner)):
            blocks_out = pl.ds(j * half, half)
            part = pl.ds(c * rows, rows)
            source = out_inner.at[blocks_out, part]
            outs.append(pltpu.make_async_copy(source, out.at[:, part], more.at[12 + 2 * c + j]))
            outs[-1].start()
    hidden_copy(0).wait()

    @pl.loop(1, count_live)
    def _(b):
        hidden_copy(b).start()
        hidden_copy(b).wait()

    for copy in outs + exports:
        copy.wait()


def by_head(block):
    lane = lax.broadcasted_iota(jnp.int32, block.shape, 1) // HEAD_DIM
    zero = jnp.zeros_like(block)
    return jnp.concatenate([jnp.where(lane == h, block, zero) for h in range(HEADS)], 0)


def from_heads(block):
    rows = block.shape[0] // HEADS
    lane = lax.broadcasted_iota(jnp.int32, (rows, 128), 1)
    parts = []
    for h in range(HEADS // 2):
        lanes = slice(h * 128, (h + 1) * 128)
        left = block[2 * h * rows : (2 * h + 1) * rows, lanes]
        right = block[(2 * h + 1) * rows : (2 * h + 2) * rows, lanes]
        parts.append(jnp.where(lane < HEAD_DIM, left, right))
    return jnp.concatenate(parts, 1)


def attend_back_kernel(count, seq, shard_rows, *refs):
    offsets, order, base, words, regions, blocks = refs[:6]
    pieces = refs[6 : 6 + count]
    refs = refs[6 + count :]
    compact, d_hidden_hbm, qkv_hbm, tokens_hbm, vectors, ffn_sums, inner_sum, pos = refs[:8]
    d_qkv_out, d_r1_out, keep_out, send_out = refs[8:12]
    weights, normed_in, mixed, scales, d_hidden, qkv, tokens, d_r1, d_mixed = refs[12:21]
    d_query, d_keys, d_values, d_qkv, total, out, sums = refs[21:28]
    turned, mixed_turned, tokens_turned, sems, more = refs[28:]
    width = weights.shape[0]
    rows = width // BLOCKS
    half = BLOCKS // 2
    pairs = pos.shape[0]
    count_live = blocks[0]

    loads = [
        (lambda here: compact.at[here, pl.ds(width, width)], normed_in),
        (lambda here: compact.at[here, pl.ds(2 * width, width)], mixed),
        (lambda here: compact.at[here, pl.ds(4 * width, 128)], scales),
        (lambda here: d_hidden_hbm.at[here], d_hidden),
    ]
    loaded = load_live(count_live, loads, more)
    weight_copies = start_pieces(pieces, offsets, weights, sems, 3 * width)
    qkv_copy = pltpu.make_async_copy(qkv_hbm, qkv, more.at[4])
    tokens_copy = pltpu.make_async_copy(tokens_hbm, tokens, more.at[5])
    qkv_copy.start()
    tokens_copy.start()
    d_r1[...] = jnp.zeros_like(d_r1)
    sums[...] = ffn_sums[...]
    loaded()
    for copy in weight_copies:
        copy.wait()

    @pl.loop(0, count_live)
    def _(b):
        here = rows_of(b)
        grad = d_hidden[here, :]
        normed = normed_in[here, :].astype(F32)
        scale = jnp.sum(scales[here, :].astype(F32), -1, keepdims=True)
        sums[3:4, :] += column_sum(grad * normed)
        sums[4:5, :] += column_sum(grad)
        low = norm_grad(grad * vectors[3:4, :], normed, scale).astype(BF16)
        sums[2:3, :] += column_sum(low.astype(F32))
        d_r1[here, :] = low
        d_mixed[here, :] = mm_nt(low, weights[...]).astype(BF16)

    def in_order(source, target):
        turned[:, : source.shape[0]] = source.T
        for i in range(BLOCKS):
            start = pl.multiple_of(order[i] * rows, 16)
            target[i * rows : (i + 1) * rows, :] = turned[pl.ds(start, rows), : source.shape[0]]

    outs = []

    def spread(value, first, size):
        low = value.astype(BF16)
        for i in range(BLOCKS):
            out[i, :, first : first + size] = low[i * rows : (i + 1) * rows, :size]
        columns = pl.ds(first, size)
        for j, target in enumerate((keep_out, send_out)):
            source = out.at[pl.ds(j * half, half), :, columns]
            sem = more.at[6 + len(outs)]
            outs.append(pltpu.make_async_copy(source, target.at[:, :, columns], sem))
            outs[-1].start()

    in_order(mixed[:LIVE, :], mixed_turned)

    @pl.when(count_live == 1)
    def _():
        total[...] = mm(mixed_turned[...], d_r1[:LIVE, :])

    @pl.when(count_live > 1)
    def _():
        total[...] = mm(mixed_turned[...], d_r1[:LIVE, :])

        @pl.loop(1, count_live)
        def _(b):
            here = rows_of(b)
            in_order(mixed[here, :], mixed_turned)
            total[...] += mm(mixed_turned[...], d_r1[here, :])

    spread(total[...], 3 * width, width)
    tokens_copy.wait()
    in_order(tokens[...], tokens_turned)
    qkv_copy.wait()

    def pair_part(pair, b):
        mine = pl.ds(pl.multiple_of(pair * seq, seq), seq)
        valid = valid_slots(words[pair], regions[pair], seq)
        first = pl.multiple_of(base[pair] + b * PART, PART)
        row = lax.broadcasted_iota(jnp.int32, (PART, seq), 0) + first
        chosen = jnp.where(row == pos[pair], 1.0, 0.0).astype(BF16)
        live_query = mm(chosen, qkv[mine, :width]).astype(BF16) * HEAD_DIM ** (-0.5)
        queries = by_head(live_query)
        grad = d_mixed[pl.ds(first, PART), :]
        row = lax.broadcasted_iota(jnp.int32, grad.shape, 0) + first
        grad = by_head(jnp.where(row < base[pair + 1], grad, jnp.zeros_like(grad)))
        keys = qkv[mine, width : 2 * width]
        probs = probabilities(queries, keys, valid)
        d_probs = mm_nt(grad, qkv[mine, 2 * width :])
        inside = jnp.sum(d_probs * probs, -1, keepdims=True)
        d_scores = (probs * (d_probs - inside)).astype(BF16)
        part = (from_heads(mm(d_scores, keys)) * HEAD_DIM ** (-0.5)).astype(BF16)
        return mm_tn(chosen, part), mm_tn(d_scores, queries), mm_tn(probs.astype(BF16), grad)

    @pl.loop(0, pairs // TOGETHER)
    def _(step):
        group = [step * TOGETHER + k for k in range(TOGETHER)]
        trips = (base[group[0] + 1] - base[group[0]]) // PART
        for pair in group[1:]:
            trips = jnp.maximum(trips, (base[pair + 1] - base[pair]) // PART)
        for k, pair in enumerate(group):
            for ref, value in zip((d_query, d_keys, d_values), pair_part(pair, 0)):
                ref[k] = value

        @pl.loop(1, trips)
        def _(b):
            for k, pair in enumerate(group):
                for ref, value in zip((d_query, d_keys, d_values), pair_part(pair, b)):
                    ref[k] += value

        for k, pair in enumerate(group):
            mine = pl.ds(pl.multiple_of(pair * seq, seq), seq)
            for part, ref in enumerate((d_query, d_keys, d_values)):
                low = ref[k].astype(BF16)
                d_qkv[mine, part * width : (part + 1) * width] = low
                if part != 1:
                    row = 0 if part == 0 else 1
                    sums[row : row + 1, :] += column_sum(low.astype(F32))

    column_form = jnp.broadcast_to(inner_sum[...], (8, inner_sum.shape[1])).T
    quarters = inner_sum.shape[1] // width
    block = jnp.concatenate([sums[...], jnp.zeros((128 - sums.shape[0], width), F32)], 0).T
    lane = lax.broadcasted_iota(jnp.int32, block.shape, 1)
    for k in range(quarters):
        starts = [(s * quarters + k) * shard_rows for s in range(width // shard_rows)]
        column = jnp.concatenate([column_form[s : s + shard_rows, :1] for s in starts], 0)
        block = jnp.where(lane == 8 + k, column, block)
    total[:, :128] = block
    spread(
        jnp.concatenate(
            [total[pl.ds(pl.multiple_of(order[i] * rows, 8), rows), :128] for i in range(BLOCKS)], 0
        ),
        4 * width,
        128,
    )
    for part in range(3):
        columns = slice(part * width, (part + 1) * width)
        spread(mm(tokens_turned[...], d_qkv[:, columns]), part * width, width)

    outs += [
        pltpu.make_async_copy(d_qkv, d_qkv_out, more.at[6 + len(outs)]),
        pltpu.make_async_copy(d_r1, d_r1_out, more.at[7 + len(outs)]),
    ]
    outs[-2].start()
    outs[-1].start()
    for copy in outs:
        copy.wait()


def input_grad_kernel(count, seq, *refs):
    offsets, base = refs[:2]
    pieces = refs[2 : 2 + count]
    d_qkv, d_r1, pos, out, weights, sems = refs[2 + count :]
    step = pl.program_id(0)

    @pl.when(step == 0)
    def _():
        for copy in start_pieces(pieces, offsets, weights, sems):
            copy.wait()

    value = mm_nt(d_qkv[...], weights[...])
    for k in range(STEP // seq):
        pair = step * (STEP // seq) + k
        start = window_start(base[pair])
        chosen = selector(pos[pair], start, seq)
        rows = slice(k * seq, (k + 1) * seq)
        out[rows, :] = value[rows] + mm_tn(chosen, d_r1[pl.ds(start, WINDOW), :])


def swap(value, bit):
    return lax.ppermute(value, "shard", [(i, i ^ bit) for i in range(8)])


def after(value, *others):
    return lax.optimization_barrier((value,) + others)[0]


def far_swap(by_x, by_y):
    half = by_x.shape[0] // 2
    return swap(by_y[:half], XBIT), swap(by_x[half:], YBIT)


def near_and_far(mine, by_x, by_y, by_both):
    far = XBIT | YBIT
    half = mine.shape[0] // 2
    near = [(mine, 0, 0), (by_x, XBIT, 0), (by_y, YBIT, 0)]
    return near + [(by_both[0], far, 0), (by_both[1], far, half)]


def chip_pieces(mine, others):
    keys = (0, XBIT, YBIT, XBIT | YBIT)
    return [(v, key, 0) for v, key in zip((mine,) + tuple(others), keys)]


def with_core(pieces, others):
    return pieces + [(v, key | CORE, row) for v, (_, key, row) in zip(others, pieces)]


class Sum:
    def __init__(self, keep, send):
        self.keep = keep
        self.got = swap(send, CORE)
        z = lax.axis_index("rep")
        self.ends = (z == 0) | (z == 3)

    def wait(self, names, others):
        values = tuple(getattr(self, name) for name in names)
        got = lax.optimization_barrier(values + tuple(others))
        for name, value in zip(names, got):
            setattr(self, name, value)

    def chip(self, block, bottom):
        half = self.keep.shape[1] // 2
        rows = slice(half, None) if bottom else slice(0, half)
        return self.keep[block, rows].astype(F32) + self.got[block, rows].astype(F32)

    def near(self, *others):
        self.wait(("keep", "got"), others)
        sent = self.chip(slice(1, 3), False).astype(BF16), self.chip(slice(2, 4), True).astype(BF16)
        self.got_a, self.got_b = swap(sent[0], XBIT), swap(sent[1], YBIT)
        return sent

    def far(self, *others):
        self.wait(("got_a", "got_b"), others)
        send_a = (self.chip(3, False) + self.got_a[1].astype(F32)).astype(BF16)
        send_b = (self.chip(1, True) + self.got_b[0].astype(F32)).astype(BF16)
        self.far_a, self.far_b = swap(send_a, YBIT), swap(send_b, XBIT)
        return send_a, send_b

    def halves(self):
        a = self.chip(0, False) + self.got_a[0].astype(F32) + self.far_a.astype(F32)
        b = self.chip(0, True) + self.got_b[1].astype(F32) + self.far_b.astype(F32)
        return a, b

    def rep_first(self, *others):
        self.wait(("far_a", "far_b"), others)
        a, b = self.halves()
        sent = jnp.where(self.ends, b, a).astype(BF16)
        self.across = lax.ppermute(sent, "rep", PAIRS)
        return (sent,)

    def rep_second(self, *others):
        self.wait(("across",), others)
        a, b = self.halves()
        self.total = (jnp.where(self.ends, a, b) + self.across.astype(F32)).astype(BF16)
        self.across = lax.ppermute(self.total, "rep", ACROSS)
        return (self.total,)

    def rep_third(self, *others):
        self.wait(("across",), others)
        self.low = (self.total.astype(F32) + self.across.astype(F32)).astype(BF16)
        self.other = lax.ppermute(self.low, "rep", PAIRS)
        return (self.low,)

    def done(self):
        top = jnp.where(self.ends, self.low, self.other)
        bottom = jnp.where(self.ends, self.other, self.low)
        return jnp.concatenate([top, bottom], 0).astype(F32)


class EarlySum(Sum):
    def part(self, start, stop, other=False):
        half = self.keep.shape[1] // 2
        first = jnp.where(self.ends == other, half, 0)
        return sum(
            lax.dynamic_slice(v, (start, first, 0), (stop - start, half, v.shape[2])).astype(F32)
            for v in (self.keep, self.got)
        )

    def rep_early(self, *others):
        self.wait(("keep", "got"), others)
        sent = self.part(0, 4, other=True).astype(BF16)
        self.extra = lax.ppermute(sent, "rep", PAIRS)
        return (sent,)

    def near(self, *others):
        self.wait(("keep", "got", "extra"), others)
        sent = (self.part(1, 3) + self.extra[1:3].astype(F32)).astype(BF16)
        self.got_a = swap(sent, XBIT)
        return (sent,)

    def far(self, *others):
        self.wait(("got_a",), others)
        sent = self.part(3, 4)[0] + self.extra[3].astype(F32) + self.got_a[1].astype(F32)
        sent = sent.astype(BF16)
        self.far_a = swap(sent, YBIT)
        return (sent,)

    def rep_second(self, *others):
        self.wait(("far_a",), others)
        total = self.part(0, 1)[0] + self.extra[0].astype(F32) + self.got_a[0].astype(F32)
        self.total = (total + self.far_a.astype(F32)).astype(BF16)
        self.across = lax.ppermute(self.total, "rep", ACROSS)
        return (self.total,)


PAIRS = [(0, 1), (1, 0), (2, 3), (3, 2)]
ACROSS = [(0, 3), (3, 0), (1, 2), (2, 1)]


def whole(shape, dtype=None):
    del dtype
    return pl.BlockSpec(shape, lambda *_: (0,) * len(shape))


def steps(width):
    return pl.BlockSpec((STEP, width), lambda i: (i, 0))


SCALARS = pl.BlockSpec(memory_space=pltpu.SMEM)
ANYWHERE = pl.BlockSpec(memory_space=pl.ANY)


def shape_of(*dims, dtype=BF16):
    return jax.ShapeDtypeStruct(dims, dtype)


def params(limit=VMEM):
    return pltpu.CompilerParams(vmem_limit_bytes=limit)


def cost(time):
    return pl.CostEstimate(flops=int(time * 1e8), bytes_accessed=0, transcendentals=0)


def local(
    tokens,
    word_counts,
    region_counts,
    task_labels,
    masked_slots,
    qkv_weight,
    query_bias,
    value_bias,
    out_weight,
    out_bias,
    attn_gain,
    attn_shift,
    inner_weight,
    inner_bias,
    back_weight,
    back_bias,
    ffn_gain,
    ffn_shift,
    cotangent,
    *,
    shards,
    reps,
):
    pairs = word_counts.shape[0]
    count, width = tokens.shape
    hidden = back_weight.shape[0] * shards
    seq = count // pairs
    grid = (count // STEP,)
    cap = -(-pairs * WINDOW // LIVE) * LIVE
    cube = shards == 8 and reps == 4
    rows = width // shards
    me = lax.axis_index("shard")

    slots = jnp.arange(seq, dtype=jnp.int32)[None, :]
    words = word_counts[:, None]
    in_regions = (slots >= WORD_SLOTS) & (slots < WORD_SLOTS + region_counts[:, None])
    picked = masked_slots == 1
    labels = task_labels[:, None]
    live = (
        (labels == 0) & picked & (slots >= 1) & (slots < words)
        | (labels == 1) & picked & in_regions
        | (labels == 2) & (slots == 0)
    )
    live_count = jnp.sum(live.astype(jnp.int32), 1)
    taken = (live_count + PART - 1) // PART * PART
    base = jnp.concatenate([jnp.zeros((1,), jnp.int32), jnp.cumsum(taken)])
    rank = jnp.cumsum(live.astype(jnp.int32), 1) - 1 + base[:-1, None]
    pos = jnp.where(live, rank, -1).reshape(pairs, 1, seq)
    blocks = jnp.maximum(1, (base[-1:] + LIVE - 1) // LIVE)

    vectors = jnp.stack(
        [query_bias, value_bias, out_bias, attn_gain, attn_shift, back_bias, ffn_gain, ffn_shift]
        + [inner_bias[k * rows : (k + 1) * rows] for k in range(hidden // width)],
        1,
    )
    vectors = jnp.pad(vectors, ((0, 0), (0, 128 - vectors.shape[1])))
    attn_shard = jnp.concatenate([qkv_weight, out_weight, vectors], 1)
    def offsets(size, halves):
        if not cube:
            return jnp.zeros((1,), jnp.int32)
        keys = [0, XBIT, YBIT, XBIT | YBIT] + [XBIT | YBIT] * halves
        keys = jnp.array(keys, jnp.int32) ^ me
        starts = jnp.array([0] * 4 + [size // 2] * halves, jnp.int32)
        return jnp.concatenate([keys * size + starts, (keys ^ CORE) * size + starts])

    attn_offsets, inner_offsets = offsets(rows, 1), offsets(rows, 0)
    back_offsets = offsets(back_weight.shape[0], 0)
    order = jnp.arange(BLOCKS, dtype=jnp.int32)
    if cube:
        order = jnp.array([0, 2, 6, 4, 1, 3, 7, 5], jnp.int32) ^ me
    indices = (base, pos, blocks, attn_offsets, inner_offsets, back_offsets, order)
    if cube:
        attn_x, attn_y = swap(attn_shard, XBIT), swap(attn_shard, YBIT)
        own = [swap(v, CORE) for v in (attn_shard, inner_weight, back_weight)]
        near = lax.optimization_barrier((attn_x, attn_y, inner_weight, indices, *own))
        attn_x, attn_y, inner_weight, indices, *own = near
        attn_far = far_swap(attn_x, attn_y)
        inner_x, inner_y = swap(inner_weight, XBIT), swap(inner_weight, YBIT)
        attn_core = swap(attn_x, CORE), swap(attn_y, CORE)
        attn_far, attn_core, back_weight = lax.optimization_barrier((attn_far, attn_core, back_weight))
        back_x, back_y = swap(back_weight, XBIT), swap(back_weight, YBIT)
        attn = near_and_far(attn_shard, attn_x, attn_y, attn_far)
        attn_core = (own[0],) + attn_core + tuple(swap(v, CORE) for v in attn_far)
        attn = with_core(attn, attn_core)
    else:
        attn, inner, back = (
            [(lax.all_gather(v, "shard", axis=0, tiled=True), 0, 0)]
            for v in (attn_shard, inner_weight, back_weight)
        )
    base, pos, blocks, attn_offsets, inner_offsets, back_offsets, order = indices

    columns = 4 * width + 128
    attn_count = len(attn)
    attn_pieces = [v for v, _, _ in attn]
    qkv, vector_rows, inner_bias_full = pl.pallas_call(
        functools.partial(project_kernel, attn_count, rows),
        grid=grid,
        in_specs=[SCALARS] + [ANYWHERE] * attn_count + [steps(width)],
        out_specs=[steps(3 * width), whole((16, width)), whole((1, hidden))],
        out_shape=[
            shape_of(count, 3 * width),
            shape_of(16, width, dtype=F32),
            shape_of(1, hidden, dtype=F32),
        ],
        scratch_shapes=[
            pltpu.VMEM((width, columns), BF16),
            pltpu.SemaphoreType.DMA((attn_count,)),
        ],
        compiler_params=params(24 * 2**20),
        cost_estimate=cost(9),
        name="project",
    )(attn_offsets, *attn_pieces, tokens)
    if cube:
        inner_x, inner_y, qkv = lax.optimization_barrier((inner_x, inner_y, qkv))
        inner_far = swap(inner_y, XBIT)
        inner_core = swap(inner_x, CORE), swap(inner_y, CORE)
    mixed = pl.pallas_call(
        functools.partial(attend_kernel, seq),
        grid=grid,
        in_specs=[SCALARS] * 2 + [steps(3 * width)],
        out_specs=steps(width),
        out_shape=shape_of(count, width),
        compiler_params=params(24 * 2**20),
        cost_estimate=cost(8),
        name="attend",
    )(word_counts, region_counts, qkv)
    if cube:
        back_x, back_y, inner_core, mixed = lax.optimization_barrier(
            (back_x, back_y, inner_core, mixed)
        )
        back_far = swap(back_x, YBIT)
        back_core = swap(back_x, CORE), swap(back_y, CORE)
    hidden1, compact = pl.pallas_call(
        functools.partial(settle_kernel, attn_count, seq),
        grid=grid,
        in_specs=[SCALARS] * 2
        + [ANYWHERE] * attn_count
        + [steps(width)] * 3
        + [whole((pairs, 1, seq)), whole((16, width))],
        out_specs=[steps(width), whole((cap, columns))],
        out_shape=[shape_of(count, width, dtype=F32), shape_of(cap, columns)],
        scratch_shapes=[
            pltpu.VMEM((width, width), BF16),
            pltpu.SemaphoreType.DMA((attn_count,)),
        ],
        compiler_params=params(30 * 2**20),
        cost_estimate=cost(9),
        name="settle",
    )(attn_offsets, base, *attn_pieces, tokens, cotangent, mixed, pos, vector_rows)

    if cube:
        inner_far, back_far, back_core, hidden1 = lax.optimization_barrier(
            (inner_far, back_far, back_core, hidden1)
        )
        inner = chip_pieces(inner_weight, (inner_x, inner_y, inner_far))
        inner = with_core(inner, (own[1],) + inner_core + (swap(inner_far, CORE),))
    inner_count = len(inner)
    inner_pieces = [v for v, _, _ in inner]
    in_vmem = pl.BlockSpec(memory_space=pltpu.VMEM)
    if cube:
        back = chip_pieces(back_weight, (back_x, back_y, back_far))
        back = with_core(back, (own[2],) + back_core + (swap(back_far, CORE),))
    back_count = len(back)
    back_pieces = [v for v, _, _ in back]

    half = BLOCKS // 2
    size = hidden // BLOCKS
    block = width // BLOCKS
    inner_full, back_full, keep_back, send_back, keep_inner, send_inner, d_hidden1, sums, inner_sum = pl.pallas_call(
        functools.partial(ffn_back_kernel, (inner_count, back_count)),
        in_specs=[SCALARS] * 4 + [ANYWHERE] * (inner_count + back_count + 1) + [in_vmem] * 2,
        out_specs=[ANYWHERE] * 7 + [in_vmem] * 2,
        out_shape=[
            shape_of(width, hidden),
            shape_of(hidden, width),
            shape_of(half, size, width),
            shape_of(half, size, width),
            shape_of(half, size, width),
            shape_of(half, size, width),
            shape_of(cap, width, dtype=F32),
            shape_of(16, width, dtype=F32),
            shape_of(1, hidden, dtype=F32),
        ],
        scratch_shapes=[
            pltpu.VMEM((hidden, width), BF16),
            pltpu.VMEM((width, hidden), BF16),
            pltpu.VMEM((cap, width), BF16),
            pltpu.VMEM((cap, width), BF16),
            pltpu.VMEM((cap, hidden), BF16),
            pltpu.VMEM((cap, hidden), BF16),
            pltpu.VMEM((cap, width), BF16),
            pltpu.VMEM((cap, hidden), BF16),
            pltpu.VMEM((cap, width), F32),
            pltpu.VMEM((width, width), F32),
            pltpu.VMEM((BLOCKS, size, width), BF16),
            pltpu.VMEM((BLOCKS, size, width), BF16),
            pltpu.VMEM((width, LIVE), BF16),
            pltpu.VMEM((cap // LIVE, width, LIVE), BF16),
            pltpu.SemaphoreType.DMA((inner_count,)),
            pltpu.SemaphoreType.DMA((back_count,)),
            pltpu.SemaphoreType.DMA((12 + 2 * hidden // width,)),
        ],
        compiler_params=params(),
        cost_estimate=cost(13),
        name="ffn_back",
    )(
        inner_offsets,
        back_offsets,
        order,
        blocks,
        *inner_pieces,
        *back_pieces,
        compact,
        inner_bias_full,
        vector_rows,
    )

    if cube:
        back_total = Sum(keep_back, send_back)
        inner_total = EarlySum(keep_inner, send_inner)

    d_qkv, d_r1, keep_attn, send_attn = pl.pallas_call(
        functools.partial(attend_back_kernel, attn_count, seq, rows),
        in_specs=[SCALARS] * 6 + [ANYWHERE] * (attn_count + 4) + [in_vmem] * 4,
        out_specs=[ANYWHERE] * 4,
        out_shape=[
            shape_of(count, 3 * width),
            shape_of(cap, width),
            shape_of(half, block, columns),
            shape_of(half, block, columns),
        ],
        scratch_shapes=[
            pltpu.VMEM((width, width), BF16),
            pltpu.VMEM((cap, width), BF16),
            pltpu.VMEM((cap, width), BF16),
            pltpu.VMEM((cap, 128), BF16),
            pltpu.VMEM((cap, width), F32),
            pltpu.VMEM((count, 3 * width), BF16),
            pltpu.VMEM((count, width), BF16),
            pltpu.VMEM((cap, width), BF16),
            pltpu.VMEM((cap, width), BF16),
            pltpu.VMEM((TOGETHER, seq, width), F32),
            pltpu.VMEM((TOGETHER, seq, width), F32),
            pltpu.VMEM((TOGETHER, seq, width), F32),
            pltpu.VMEM((count, 3 * width), BF16),
            pltpu.VMEM((width, width), F32),
            pltpu.VMEM((BLOCKS, block, columns), BF16),
            pltpu.VMEM((16, width), F32),
            pltpu.VMEM((width, count), BF16),
            pltpu.VMEM((width, LIVE), BF16),
            pltpu.VMEM((width, count), BF16),
            pltpu.SemaphoreType.DMA((attn_count,)),
            pltpu.SemaphoreType.DMA((16 + count // STEP,)),
        ],
        compiler_params=params(),
        cost_estimate=cost(22),
        name="attend_back",
    )(
        attn_offsets,
        order,
        base,
        word_counts,
        region_counts,
        blocks,
        *attn_pieces,
        compact,
        d_hidden1,
        qkv,
        tokens,
        vector_rows,
        sums,
        inner_sum,
        pos,
    )

    def later(shift):
        return lambda i: (i + shift, 0)

    def ffn(first, number, x, *done):
        return pl.pallas_call(
            ffn_kernel,
            grid=(number,),
            in_specs=[pl.BlockSpec((STEP, width), later(first)), whole((1, hidden)), whole((16, width))]
            + [in_vmem] * 2
            + [ANYWHERE] * len(done),
            out_specs=pl.BlockSpec((STEP, width), later(first)),
            out_shape=shape_of(count, width),
            input_output_aliases={5: 0} if done else {},
            scratch_shapes=[pltpu.VMEM((STEP, hidden), BF16)],
            compiler_params=params(24 * 2**20),
            cost_estimate=cost(11),
            name="ffn",
        )(x, inner_bias_full, vector_rows, inner_full, back_full, *done)

    x = hidden1
    if cube:
        sent = back_total.near(d_r1)
        sent += inner_total.rep_early(*sent)
        attn_total = Sum(keep_attn, send_attn)
        sent += attn_total.near(*sent)
        x = after(hidden1, *sent)
    result = ffn(0, grid[0] - 1, x)
    if cube:
        sent = back_total.far(result)
        sent += attn_total.far(*sent)
        sent += back_total.rep_first(*sent)
        sent += inner_total.near(*sent)
        sent += attn_total.rep_first(*sent)
        sent += back_total.rep_second(*sent)
        d_qkv = after(d_qkv, *sent)

    input_grad = pl.pallas_call(
        functools.partial(input_grad_kernel, attn_count, seq),
        grid=grid,
        in_specs=[SCALARS] * 2
        + [ANYWHERE] * attn_count
        + [steps(3 * width), whole((cap, width)), whole((pairs, 1, seq))],
        out_specs=steps(width),
        out_shape=shape_of(count, width, dtype=F32),
        scratch_shapes=[
            pltpu.VMEM((width, 3 * width), BF16),
            pltpu.SemaphoreType.DMA((attn_count,)),
        ],
        compiler_params=params(24 * 2**20),
        cost_estimate=cost(9),
        name="input_grad",
    )(attn_offsets, base, *attn_pieces, d_qkv, d_r1, pos)

    if cube:
        sent = attn_total.rep_second(input_grad)
        sent += inner_total.far(*sent)
        sent += back_total.rep_third(*sent)
        x = after(hidden1, *sent)
    result = ffn(grid[0] - 1, 1, x, result)
    if cube:
        sent = inner_total.rep_second(result)

    quarters = hidden // width
    if cube:
        attn_total.rep_third(*sent)
        inner_total.rep_third()
        back_sum, inner_sum, attn_sum = (v.done() for v in (back_total, inner_total, attn_total))
        inner_sum = jnp.concatenate([inner_sum[c * block : (c + 1) * block] for c in range(quarters)], 1)
    else:
        back_grad = jnp.concatenate([keep_back, send_back]).reshape(hidden, width)
        inner_grad = jnp.concatenate([keep_inner, send_inner]).reshape(BLOCKS, quarters, block, width)
        inner_grad = inner_grad.transpose(0, 2, 1, 3).reshape(width, hidden)
        attn_grad = jnp.concatenate([keep_attn, send_attn]).reshape(width, columns)
        back_sum, inner_sum, attn_sum = (
            lax.psum(lax.psum_scatter(g, "shard", scatter_dimension=0, tiled=True), "rep").astype(F32)
            for g in (back_grad, inner_grad, attn_grad)
        )
    sums = attn_sum[:, 4 * width :].T
    return (
        result,
        input_grad,
        attn_sum[:, : 3 * width],
        sums[0],
        sums[1],
        attn_sum[:, 3 * width : 4 * width],
        sums[2],
        sums[3],
        sums[4],
        inner_sum,
        sums[8 : 8 + quarters].reshape(-1),
        back_sum,
        sums[5],
        sums[6],
        sums[7],
    )


def solution(mesh):
    rows, both, one = P(("rep", "shard"), None), P(("rep", "shard")), P("shard")
    matrix = P("shard", None)
    in_specs = (rows, both, both, both, rows, matrix, one, one, matrix, one, one, one)
    in_specs += (matrix, one, matrix, one, one, one, rows)
    out_specs = (rows, rows, matrix, one, one, matrix, one, one, one, matrix, one, matrix)
    out_specs += (one, one, one)
    sizes = dict(mesh.shape)

    def run(*args):
        return local(*args, shards=sizes["shard"], reps=sizes["rep"])

    return jax.shard_map(
        run, mesh=mesh, in_specs=in_specs, out_specs=out_specs, check_vma=False
    )
```

```python
import functools

import jax
import jax.numpy as jnp
from jax import lax
from jax.experimental import pallas as pl
from jax.experimental.pallas import tpu as pltpu
from jax.sharding import PartitionSpec as P

HEADS = 12
HEAD_DIM = 64
WORD_SLOTS = 60
CORE, XBIT, YBIT = 1, 2, 4
BLOCKS = 8
STEP = 256
LIVE = 192
WINDOW = 80
PART = 16
TOGETHER = 2
VMEM = 60 * 2**20
F32 = jnp.float32
BF16 = jnp.bfloat16


def mm(left, right):
    return jnp.dot(left, right, preferred_element_type=F32)


def mm_nt(left, right):
    return lax.dot_general(left, right, (((1,), (1,)), ((), ())), preferred_element_type=F32)


def mm_tn(left, right):
    return lax.dot_general(left, right, (((0,), (0,)), ((), ())), preferred_element_type=F32)


def norm_parts(value):
    mean = jnp.mean(value, -1, keepdims=True)
    centred = value - mean
    scale = lax.rsqrt(jnp.mean(centred * centred, -1, keepdims=True) + 1e-05)
    return centred * scale, scale


def norm_grad(grad, normed, scale):
    return scale * (
        grad
        - jnp.mean(grad, -1, keepdims=True)
        - normed * jnp.mean(grad * normed, -1, keepdims=True)
    )


def piece_at(index, size):
    return pl.ds(pl.multiple_of(index * size, 128), size)


def column_sum(value):
    return jnp.sum(value, 0, keepdims=True)


def start_pieces(pieces, offsets, scratch, sems, first=0, started=False):
    copies = []
    for j, piece in enumerate(pieces):
        start = pl.multiple_of(offsets[j], 16)
        source = piece.at[:, pl.ds(first, scratch.shape[1])]
        target = scratch.at[pl.ds(start, piece.shape[0]), :]
        copies.append(pltpu.make_async_copy(source, target, sems.at[j]))
        if not started:
            copies[-1].start()
    return copies


def stacked(block):
    lane = lax.broadcasted_iota(jnp.int32, block.shape, 1)
    zero = jnp.zeros_like(block)
    return jnp.concatenate(
        [jnp.where(lane < HEAD_DIM, block, zero), jnp.where(lane >= HEAD_DIM, block, zero)], 0
    )


def unstacked(block):
    rows = block.shape[0] // 2
    lane = lax.broadcasted_iota(jnp.int32, (rows, block.shape[1]), 1)
    return jnp.where(lane < HEAD_DIM, block[:rows], block[rows:])


def probabilities(queries, keys, valid):
    scores = jnp.where(valid, mm_nt(queries, keys), -1000000000.0)
    peak = jnp.max(scores, -1, keepdims=True)
    expo = jnp.exp(scores - peak)
    return expo * (1.0 / jnp.sum(expo, -1, keepdims=True))


def valid_slots(words, regions, seq):
    slot = lax.broadcasted_iota(jnp.int32, (1, seq), 1)
    return (slot < words) | ((slot >= WORD_SLOTS) & (slot < WORD_SLOTS + regions))


def selector(pos, start, seq):
    row = lax.broadcasted_iota(jnp.int32, (WINDOW, seq), 0) + start
    return jnp.where(row == pos, 1.0, 0.0).astype(BF16)


def window_start(base):
    return pl.multiple_of(base, PART)


def project_kernel(count, shard_rows, *refs):
    offsets = refs[0]
    pieces = refs[1 : 1 + count]
    tokens, qkv, vectors, bias, weights, sems = refs[1 + count :]
    width = tokens.shape[1]
    quarters = bias.shape[1] // width

    @pl.when(pl.program_id(0) == 0)
    def _():
        for copy in start_pieces(pieces, offsets, weights, sems):
            copy.wait()
        share = weights[:, 4 * width :].astype(F32)
        vectors[...] = share.T[: vectors.shape[0]]
        parts = []
        for s in range(width // shard_rows):
            for k in range(quarters):
                part = share[s * shard_rows : (s + 1) * shard_rows, 8 + k : 9 + k]
                parts.append(jnp.broadcast_to(part, (shard_rows, 8)))
        bias[...] = jnp.concatenate(parts, 0).T[:1]

    x = tokens[...]
    for part, row in ((0, 0), (1, None), (2, 1)):
        columns = slice(part * width, (part + 1) * width)
        value = mm(x, weights[:, columns])
        if row is not None:
            value = value + vectors[row : row + 1, :]
        qkv[:, columns] = value.astype(BF16)


def attend_kernel(seq, words, regions, qkv, mixed):
    width = mixed.shape[1]
    step = pl.program_id(0)
    for k in range(STEP // seq):
        rows = slice(k * seq, (k + 1) * seq)
        pair = step * (STEP // seq) + k
        valid = valid_slots(words[pair], regions[pair], seq)
        for h in range(HEADS // 2):
            lanes = slice(h * 128, (h + 1) * 128)
            queries = stacked(qkv[rows, lanes] * HEAD_DIM ** (-0.5))
            keys = qkv[rows, width + h * 128 : width + (h + 1) * 128]
            values = qkv[rows, 2 * width + h * 128 : 2 * width + (h + 1) * 128]
            scores = jnp.where(valid, mm_nt(queries, keys), -1000000000.0)
            expo = jnp.exp(scores - jnp.max(scores, -1, keepdims=True)).astype(BF16)
            both = mm(expo, jnp.concatenate([values, jnp.ones_like(values)], 1))
            mixed[rows, lanes] = (unstacked(both[:, :128]) / unstacked(both[:, 128:])).astype(BF16)


def settle_kernel(count, seq, *refs):
    offsets, base = refs[:2]
    pieces = refs[2 : 2 + count]
    tokens, cotangent, mixed, pos, vectors, hidden, compact, proj, sems = refs[2 + count :]
    width = tokens.shape[1]
    step = pl.program_id(0)

    @pl.when(step == 0)
    def _():
        copies = start_pieces(pieces, offsets, proj, sems, 3 * width)
        compact[...] = jnp.zeros_like(compact)
        for copy in copies:
            copy.wait()

    branch = mm(mixed[...], proj[...]) + vectors[2:3, :]
    normed, scale = norm_parts(tokens[...].astype(F32) + branch)
    value = normed * vectors[3:4, :] + vectors[4:5, :]
    hidden[...] = value
    high = scale.astype(BF16)
    rest = scale - high.astype(F32)
    middle = rest.astype(BF16)
    low = (rest - middle.astype(F32)).astype(BF16)
    lane = lax.broadcasted_iota(jnp.int32, (STEP, 128), 1)
    zero = jnp.zeros((STEP, 128), BF16)
    scales = jnp.where(lane == 0, high, jnp.where(lane == 1, middle, jnp.where(lane == 2, low, zero)))
    parts = (value.astype(BF16), normed.astype(BF16), mixed[...], cotangent[...], scales)
    for k in range(STEP // seq):
        pair = step * (STEP // seq) + k
        start = window_start(base[pair])
        chosen = selector(pos[pair], start, seq)
        at = 0
        for part in parts:
            columns = slice(at, at + part.shape[1])
            at += part.shape[1]
            got = mm(chosen, part[k * seq : (k + 1) * seq]).astype(BF16)
            compact[pl.ds(start, WINDOW), columns] = got


def gelu_parts(inner):
    cumul = 0.5 + 0.5 * lax.erf(inner * 0.7071067811865476)
    return inner * cumul, cumul


def ffn_kernel(hidden, bias, vectors, inner, back, *rest):
    result, act = rest[-2:]
    width = hidden.shape[1]
    x = hidden[...]
    low = x.astype(BF16)
    for c in range(inner.shape[1] // width):
        columns = slice(c * width, (c + 1) * width)
        value = mm(low, inner[:, columns]) + bias[:, columns]
        act[:, columns] = gelu_parts(value)[0].astype(BF16)
    second = mm(act[...], back[...]) + vectors[5:6, :]
    normed, _ = norm_parts(x + second)
    result[...] = (normed * vectors[6:7, :] + vectors[7:8, :]).astype(BF16)


def rows_of(b):
    return pl.ds(pl.multiple_of(b * LIVE, LIVE), LIVE)


def load_live(count_live, pairs, sems):
    def copies(b):
        here = rows_of(b)
        return [
            pltpu.make_async_copy(source(here), target.at[here], sems.at[j])
            for j, (source, target) in enumerate(pairs)
        ]

    for copy in copies(0):
        copy.start()

    def finish():
        for copy in copies(0):
            copy.wait()

        @pl.loop(1, count_live)
        def _(b):
            later = copies(b)
            for copy in later:
                copy.start()
            for copy in later:
                copy.wait()

    return finish


def store_live(count_live, pairs, sems):
    def copies(b):
        here = rows_of(b)
        return [
            pltpu.make_async_copy(source.at[here], target.at[here], sems.at[j])
            for j, (source, target) in enumerate(pairs)
        ]

    for copy in copies(0):
        copy.start()

    def finish():
        for copy in copies(0):
            copy.wait()

        @pl.loop(1, count_live)
        def _(b):
            later = copies(b)
            for copy in later:
                copy.start()
            for copy in later:
                copy.wait()

    return finish


def ffn_back_kernel(counts, *refs):
    inner_offsets, back_offsets, order, blocks = refs[:4]
    inner_pieces = refs[4 : 4 + counts[0]]
    back_pieces = refs[4 + counts[0] : 4 + sum(counts)]
    refs = refs[4 + sum(counts) :]
    compact_hbm, bias, vectors = refs[:3]
    inner_out, back_out = refs[3:5]
    keep_back, send_back, keep_inner, send_inner, d_hidden_out, sums, inner_sum = refs[5:12]
    back, inner, hidden, cotangent, act, slope, d_second, d_inner, d_hidden = refs[12:21]
    total, out_back, out_inner, turned, ordered, inner_sems, back_sems, more = refs[21:]
    width = inner.shape[0]
    size = inner.shape[1] // BLOCKS
    quarters = inner.shape[1] // width
    rows = width // BLOCKS
    half = BLOCKS // 2
    first = slice(0, LIVE)
    count_live = blocks[0]

    def live_copies(b):
        here = rows_of(b)
        return [
            pltpu.make_async_copy(compact_hbm.at[here, pl.ds(0, width)], hidden.at[here], more.at[0]),
            pltpu.make_async_copy(
                compact_hbm.at[here, pl.ds(3 * width, width)], cotangent.at[here], more.at[1]
            ),
        ]

    now = live_copies(0)
    for copy in now:
        copy.start()
    inner_copies = start_pieces(inner_pieces, inner_offsets, inner, inner_sems)
    back_copies = start_pieces(back_pieces, back_offsets, back, back_sems)
    sums[...] = jnp.zeros_like(sums)
    inner_sum[...] = jnp.zeros_like(inner_sum)
    for copy in now:
        copy.wait()

    @pl.loop(1, count_live)
    def _(b):
        later = live_copies(b)
        for copy in later:
            copy.start()
        for copy in later:
            copy.wait()

    for copy in inner_copies:
        copy.wait()

    @pl.loop(0, count_live)
    def _(b):
        here = rows_of(b)

        @pl.loop(0, quarters)
        def _(c):
            columns = piece_at(c, width)
            value = mm(hidden[here, :], inner[:, columns]) + bias[:, columns]
            grown, cumul = gelu_parts(value)
            density = jnp.exp(-0.5 * value * value) * 0.3989422804014327
            act[here, columns] = grown.astype(BF16)
            slope[here, columns] = (cumul + value * density).astype(BF16)

    for copy in back_copies:
        copy.wait()
    exports = [
        pltpu.make_async_copy(back, back_out, back_sems.at[0]),
        pltpu.make_async_copy(inner, inner_out, inner_sems.at[0]),
    ]
    exports[0].start()
    exports[1].start()

    @pl.loop(0, count_live)
    def _(b):
        here = rows_of(b)
        second = mm(act[here, :], back[...]) + vectors[5:6, :]
        normed, scale = norm_parts(hidden[here, :].astype(F32) + second)
        d_out = cotangent[here, :].astype(F32)
        sums[6:7, :] += column_sum(d_out * normed)
        sums[7:8, :] += column_sum(d_out)
        d_r2 = norm_grad(d_out * vectors[6:7, :], normed, scale)
        low = d_r2.astype(BF16)
        d_second[here, :] = low
        sums[5:6, :] += column_sum(low.astype(F32))
        d_hidden[here, :] = d_r2

    single = count_live == 1
    outs = []
    for i in range(BLOCKS):
        chunk = pl.ds(pl.multiple_of(order[i] * size, 128), size)

        @pl.when(single)
        def _():
            out_back[i] = mm_tn(act[first, chunk], d_second[first, :]).astype(BF16)

        @pl.when(jnp.logical_not(single))
        def _():
            total[:size, :] = mm_tn(act[first, chunk], d_second[first, :])

            @pl.loop(1, count_live)
            def _(b):
                here = rows_of(b)
                total[:size, :] += mm_tn(act[here, chunk], d_second[here, :])

            out_back[i] = total[:size, :].astype(BF16)

        target = keep_back.at[i] if i < half else send_back.at[i - half]
        outs.append(pltpu.make_async_copy(out_back.at[i], target, more.at[4 + i]))
        outs[-1].start()

    @pl.loop(0, count_live)
    def _(b):
        here = rows_of(b)
        grad = d_second[here, :]
        for c in range(quarters):
            columns = slice(c * width, (c + 1) * width)
            d_act = mm_nt(grad, back[columns, :])
            low = (d_act * slope[here, columns].astype(F32)).astype(BF16)
            d_inner[here, columns] = low
            inner_sum[:, columns] += column_sum(low.astype(F32))
            d_hidden[here, :] += mm_nt(low, inner[:, columns])

    def hidden_copy(b):
        return pltpu.make_async_copy(
            d_hidden.at[rows_of(b)], d_hidden_out.at[rows_of(b)], more.at[0]
        )

    hidden_copy(0).start()

    @pl.loop(0, count_live)
    def _(b):
        here = rows_of(b)
        turned[...] = hidden[here, :].T
        for i in range(BLOCKS):
            start = pl.multiple_of(order[i] * rows, 16)
            ordered[b, i * rows : (i + 1) * rows, :] = turned[pl.ds(start, rows), :]

    for c in range(quarters):
        columns = slice(c * width, (c + 1) * width)
        target = slice(c * rows, (c + 1) * rows)

        @pl.when(single)
        def _():
            value = mm(ordered[0], d_inner[first, columns]).astype(BF16)
            for i in range(BLOCKS):
                out_inner[i, target, :] = value[i * rows : (i + 1) * rows, :]

        @pl.when(jnp.logical_not(single))
        def _():
            total[...] = mm(ordered[0], d_inner[first, columns])

            @pl.loop(1, count_live)
            def _(b):
                total[...] += mm(ordered[b], d_inner[rows_of(b), columns])

            for i in range(BLOCKS):
                out_inner[i, target, :] = total[i * rows : (i + 1) * rows, :].astype(BF16)

        for j, out in enumerate((keep_inner, send_inner)):
            blocks_out = pl.ds(j * half, half)
            part = pl.ds(c * rows, rows)
            source = out_inner.at[blocks_out, part]
            outs.append(pltpu.make_async_copy(source, out.at[:, part], more.at[12 + 2 * c + j]))
            outs[-1].start()
    hidden_copy(0).wait()

    @pl.loop(1, count_live)
    def _(b):
        hidden_copy(b).start()
        hidden_copy(b).wait()

    for copy in outs + exports:
        copy.wait()


def by_head(block):
    lane = lax.broadcasted_iota(jnp.int32, block.shape, 1) // HEAD_DIM
    zero = jnp.zeros_like(block)
    return jnp.concatenate([jnp.where(lane == h, block, zero) for h in range(HEADS)], 0)


def from_heads(block):
    rows = block.shape[0] // HEADS
    lane = lax.broadcasted_iota(jnp.int32, (rows, 128), 1)
    parts = []
    for h in range(HEADS // 2):
        lanes = slice(h * 128, (h + 1) * 128)
        left = block[2 * h * rows : (2 * h + 1) * rows, lanes]
        right = block[(2 * h + 1) * rows : (2 * h + 2) * rows, lanes]
        parts.append(jnp.where(lane < HEAD_DIM, left, right))
    return jnp.concatenate(parts, 1)


def attend_back_kernel(count, seq, shard_rows, *refs):
    offsets, order, base, words, regions, blocks = refs[:6]
    pieces = refs[6 : 6 + count]
    refs = refs[6 + count :]
    compact, d_hidden_hbm, qkv_hbm, tokens_hbm, vectors, ffn_sums, inner_sum, pos = refs[:8]
    d_qkv_out, d_r1_out, keep_out, send_out = refs[8:12]
    weights, normed_in, mixed, scales, d_hidden, qkv, tokens, d_r1, d_mixed = refs[12:21]
    d_query, d_keys, d_values, d_qkv, total, out, sums = refs[21:28]
    turned, mixed_turned, tokens_turned, sems, more = refs[28:]
    width = weights.shape[0]
    rows = width // BLOCKS
    half = BLOCKS // 2
    pairs = pos.shape[0]
    count_live = blocks[0]

    loads = [
        (lambda here: compact.at[here, pl.ds(width, width)], normed_in),
        (lambda here: compact.at[here, pl.ds(2 * width, width)], mixed),
        (lambda here: compact.at[here, pl.ds(4 * width, 128)], scales),
        (lambda here: d_hidden_hbm.at[here], d_hidden),
    ]
    loaded = load_live(count_live, loads, more)
    weight_copies = start_pieces(pieces, offsets, weights, sems, 3 * width)
    qkv_copy = pltpu.make_async_copy(qkv_hbm, qkv, more.at[4])
    tokens_copy = pltpu.make_async_copy(tokens_hbm, tokens, more.at[5])
    qkv_copy.start()
    tokens_copy.start()
    d_r1[...] = jnp.zeros_like(d_r1)
    sums[...] = ffn_sums[...]
    loaded()
    for copy in weight_copies:
        copy.wait()

    @pl.loop(0, count_live)
    def _(b):
        here = rows_of(b)
        grad = d_hidden[here, :]
        normed = normed_in[here, :].astype(F32)
        scale = jnp.sum(scales[here, :].astype(F32), -1, keepdims=True)
        sums[3:4, :] += column_sum(grad * normed)
        sums[4:5, :] += column_sum(grad)
        low = norm_grad(grad * vectors[3:4, :], normed, scale).astype(BF16)
        sums[2:3, :] += column_sum(low.astype(F32))
        d_r1[here, :] = low
        d_mixed[here, :] = mm_nt(low, weights[...]).astype(BF16)

    def in_order(source, target):
        turned[:, : source.shape[0]] = source.T
        for i in range(BLOCKS):
            start = pl.multiple_of(order[i] * rows, 16)
            target[i * rows : (i + 1) * rows, :] = turned[pl.ds(start, rows), : source.shape[0]]

    outs = []

    def spread(value, first, size):
        low = value.astype(BF16)
        for i in range(BLOCKS):
            out[i, :, first : first + size] = low[i * rows : (i + 1) * rows, :size]
        columns = pl.ds(first, size)
        for j, target in enumerate((keep_out, send_out)):
            source = out.at[pl.ds(j * half, half), :, columns]
            sem = more.at[6 + len(outs)]
            outs.append(pltpu.make_async_copy(source, target.at[:, :, columns], sem))
            outs[-1].start()

    in_order(mixed[:LIVE, :], mixed_turned)

    @pl.when(count_live == 1)
    def _():
        total[...] = mm(mixed_turned[...], d_r1[:LIVE, :])

    @pl.when(count_live > 1)
    def _():
        total[...] = mm(mixed_turned[...], d_r1[:LIVE, :])

        @pl.loop(1, count_live)
        def _(b):
            here = rows_of(b)
            in_order(mixed[here, :], mixed_turned)
            total[...] += mm(mixed_turned[...], d_r1[here, :])

    spread(total[...], 3 * width, width)
    tokens_copy.wait()
    in_order(tokens[...], tokens_turned)
    qkv_copy.wait()

    def pair_part(pair, b):
        mine = pl.ds(pl.multiple_of(pair * seq, seq), seq)
        valid = valid_slots(words[pair], regions[pair], seq)
        first = pl.multiple_of(base[pair] + b * PART, PART)
        row = lax.broadcasted_iota(jnp.int32, (PART, seq), 0) + first
        chosen = jnp.where(row == pos[pair], 1.0, 0.0).astype(BF16)
        live_query = mm(chosen, qkv[mine, :width]).astype(BF16) * HEAD_DIM ** (-0.5)
        queries = by_head(live_query)
        grad = d_mixed[pl.ds(first, PART), :]
        row = lax.broadcasted_iota(jnp.int32, grad.shape, 0) + first
        grad = by_head(jnp.where(row < base[pair + 1], grad, jnp.zeros_like(grad)))
        keys = qkv[mine, width : 2 * width]
        probs = probabilities(queries, keys, valid)
        d_probs = mm_nt(grad, qkv[mine, 2 * width :])
        inside = jnp.sum(d_probs * probs, -1, keepdims=True)
        d_scores = (probs * (d_probs - inside)).astype(BF16)
        part = (from_heads(mm(d_scores, keys)) * HEAD_DIM ** (-0.5)).astype(BF16)
        return mm_tn(chosen, part), mm_tn(d_scores, queries), mm_tn(probs.astype(BF16), grad)

    @pl.loop(0, pairs // TOGETHER)
    def _(step):
        group = [step * TOGETHER + k for k in range(TOGETHER)]
        trips = (base[group[0] + 1] - base[group[0]]) // PART
        for pair in group[1:]:
            trips = jnp.maximum(trips, (base[pair + 1] - base[pair]) // PART)
        for k, pair in enumerate(group):
            for ref, value in zip((d_query, d_keys, d_values), pair_part(pair, 0)):
                ref[k] = value

        @pl.loop(1, trips)
        def _(b):
            for k, pair in enumerate(group):
                for ref, value in zip((d_query, d_keys, d_values), pair_part(pair, b)):
                    ref[k] += value

        for k, pair in enumerate(group):
            mine = pl.ds(pl.multiple_of(pair * seq, seq), seq)
            for part, ref in enumerate((d_query, d_keys, d_values)):
                low = ref[k].astype(BF16)
                d_qkv[mine, part * width : (part + 1) * width] = low
                if part != 1:
                    row = 0 if part == 0 else 1
                    sums[row : row + 1, :] += column_sum(low.astype(F32))

    column_form = jnp.broadcast_to(inner_sum[...], (8, inner_sum.shape[1])).T
    quarters = inner_sum.shape[1] // width
    block = jnp.concatenate([sums[...], jnp.zeros((128 - sums.shape[0], width), F32)], 0).T
    lane = lax.broadcasted_iota(jnp.int32, block.shape, 1)
    for k in range(quarters):
        starts = [(s * quarters + k) * shard_rows for s in range(width // shard_rows)]
        column = jnp.concatenate([column_form[s : s + shard_rows, :1] for s in starts], 0)
        block = jnp.where(lane == 8 + k, column, block)
    total[:, :128] = block
    spread(
        jnp.concatenate(
            [total[pl.ds(pl.multiple_of(order[i] * rows, 8), rows), :128] for i in range(BLOCKS)], 0
        ),
        4 * width,
        128,
    )
    for part in range(3):
        columns = slice(part * width, (part + 1) * width)
        spread(mm(tokens_turned[...], d_qkv[:, columns]), part * width, width)

    outs += [
        pltpu.make_async_copy(d_qkv, d_qkv_out, more.at[6 + len(outs)]),
        pltpu.make_async_copy(d_r1, d_r1_out, more.at[7 + len(outs)]),
    ]
    outs[-2].start()
    outs[-1].start()
    for copy in outs:
        copy.wait()


def input_grad_kernel(count, seq, *refs):
    offsets, base = refs[:2]
    pieces = refs[2 : 2 + count]
    d_qkv, d_r1, pos, out, weights, sems = refs[2 + count :]
    step = pl.program_id(0)

    @pl.when(step == 0)
    def _():
        for copy in start_pieces(pieces, offsets, weights, sems):
            copy.wait()

    value = mm_nt(d_qkv[...], weights[...])
    for k in range(STEP // seq):
        pair = step * (STEP // seq) + k
        start = window_start(base[pair])
        chosen = selector(pos[pair], start, seq)
        rows = slice(k * seq, (k + 1) * seq)
        out[rows, :] = value[rows] + mm_tn(chosen, d_r1[pl.ds(start, WINDOW), :])


def swap(value, bit):
    return lax.ppermute(value, "shard", [(i, i ^ bit) for i in range(8)])


def after(value, *others):
    return lax.optimization_barrier((value,) + others)[0]


def far_swap(by_x, by_y):
    half = by_x.shape[0] // 2
    return swap(by_y[:half], XBIT), swap(by_x[half:], YBIT)


def near_and_far(mine, by_x, by_y, by_both):
    far = XBIT | YBIT
    half = mine.shape[0] // 2
    near = [(mine, 0, 0), (by_x, XBIT, 0), (by_y, YBIT, 0)]
    return near + [(by_both[0], far, 0), (by_both[1], far, half)]


def chip_pieces(mine, others):
    keys = (0, XBIT, YBIT, XBIT | YBIT)
    return [(v, key, 0) for v, key in zip((mine,) + tuple(others), keys)]


def with_core(pieces, others):
    return pieces + [(v, key | CORE, row) for v, (_, key, row) in zip(others, pieces)]


class Sum:
    def __init__(self, keep, send):
        self.keep = keep
        self.got = swap(send, CORE)
        z = lax.axis_index("rep")
        self.ends = (z == 0) | (z == 3)

    def wait(self, names, others):
        values = tuple(getattr(self, name) for name in names)
        got = lax.optimization_barrier(values + tuple(others))
        for name, value in zip(names, got):
            setattr(self, name, value)

    def chip(self, block, bottom):
        half = self.keep.shape[1] // 2
        rows = slice(half, None) if bottom else slice(0, half)
        return self.keep[block, rows].astype(F32) + self.got[block, rows].astype(F32)

    def near(self, *others):
        self.wait(("keep", "got"), others)
        sent = self.chip(slice(1, 3), False).astype(BF16), self.chip(slice(2, 4), True).astype(BF16)
        self.got_a, self.got_b = swap(sent[0], XBIT), swap(sent[1], YBIT)
        return sent

    def far(self, *others):
        self.wait(("got_a", "got_b"), others)
        send_a = (self.chip(3, False) + self.got_a[1].astype(F32)).astype(BF16)
        send_b = (self.chip(1, True) + self.got_b[0].astype(F32)).astype(BF16)
        self.far_a, self.far_b = swap(send_a, YBIT), swap(send_b, XBIT)
        return send_a, send_b

    def halves(self):
        a = self.chip(0, False) + self.got_a[0].astype(F32) + self.far_a.astype(F32)
        b = self.chip(0, True) + self.got_b[1].astype(F32) + self.far_b.astype(F32)
        return a, b

    def rep_first(self, *others):
        self.wait(("far_a", "far_b"), others)
        a, b = self.halves()
        sent = jnp.where(self.ends, b, a).astype(BF16)
        self.across = lax.ppermute(sent, "rep", PAIRS)
        return (sent,)

    def rep_second(self, *others):
        self.wait(("across",), others)
        a, b = self.halves()
        self.total = (jnp.where(self.ends, a, b) + self.across.astype(F32)).astype(BF16)
        self.across = lax.ppermute(self.total, "rep", ACROSS)
        return (self.total,)

    def rep_third(self, *others):
        self.wait(("across",), others)
        self.low = (self.total.astype(F32) + self.across.astype(F32)).astype(BF16)
        self.other = lax.ppermute(self.low, "rep", PAIRS)
        return (self.low,)

    def done(self):
        top = jnp.where(self.ends, self.low, self.other)
        bottom = jnp.where(self.ends, self.other, self.low)
        return jnp.concatenate([top, bottom], 0).astype(F32)


class EarlySum(Sum):
    def part(self, start, stop, other=False):
        half = self.keep.shape[1] // 2
        first = jnp.where(self.ends == other, half, 0)
        return sum(
            lax.dynamic_slice(v, (start, first, 0), (stop - start, half, v.shape[2])).astype(F32)
            for v in (self.keep, self.got)
        )

    def rep_early(self, *others):
        self.wait(("keep", "got"), others)
        sent = self.part(0, 4, other=True).astype(BF16)
        self.extra = lax.ppermute(sent, "rep", PAIRS)
        return (sent,)

    def near(self, *others):
        self.wait(("keep", "got", "extra"), others)
        sent = (self.part(1, 3) + self.extra[1:3].astype(F32)).astype(BF16)
        self.got_a = swap(sent, XBIT)
        return (sent,)

    def far(self, *others):
        self.wait(("got_a",), others)
        sent = self.part(3, 4)[0] + self.extra[3].astype(F32) + self.got_a[1].astype(F32)
        sent = sent.astype(BF16)
        self.far_a = swap(sent, YBIT)
        return (sent,)

    def rep_second(self, *others):
        self.wait(("far_a",), others)
        total = self.part(0, 1)[0] + self.extra[0].astype(F32) + self.got_a[0].astype(F32)
        self.total = (total + self.far_a.astype(F32)).astype(BF16)
        self.across = lax.ppermute(self.total, "rep", ACROSS)
        return (self.total,)


PAIRS = [(0, 1), (1, 0), (2, 3), (3, 2)]
ACROSS = [(0, 3), (3, 0), (1, 2), (2, 1)]


def whole(shape, dtype=None):
    del dtype
    return pl.BlockSpec(shape, lambda *_: (0,) * len(shape))


def steps(width):
    return pl.BlockSpec((STEP, width), lambda i: (i, 0))


SCALARS = pl.BlockSpec(memory_space=pltpu.SMEM)
ANYWHERE = pl.BlockSpec(memory_space=pl.ANY)


def shape_of(*dims, dtype=BF16):
    return jax.ShapeDtypeStruct(dims, dtype)


def params(limit=VMEM):
    return pltpu.CompilerParams(vmem_limit_bytes=limit)


def cost(time):
    return pl.CostEstimate(flops=int(time * 1e8), bytes_accessed=0, transcendentals=0)


def local(
    tokens,
    word_counts,
    region_counts,
    task_labels,
    masked_slots,
    qkv_weight,
    query_bias,
    value_bias,
    out_weight,
    out_bias,
    attn_gain,
    attn_shift,
    inner_weight,
    inner_bias,
    back_weight,
    back_bias,
    ffn_gain,
    ffn_shift,
    cotangent,
    *,
    shards,
    reps,
):
    pairs = word_counts.shape[0]
    count, width = tokens.shape
    hidden = back_weight.shape[0] * shards
    seq = count // pairs
    grid = (count // STEP,)
    cap = -(-pairs * WINDOW // LIVE) * LIVE
    cube = shards == 8 and reps == 4
    rows = width // shards
    me = lax.axis_index("shard")

    slots = jnp.arange(seq, dtype=jnp.int32)[None, :]
    words = word_counts[:, None]
    in_regions = (slots >= WORD_SLOTS) & (slots < WORD_SLOTS + region_counts[:, None])
    picked = masked_slots == 1
    labels = task_labels[:, None]
    live = (
        (labels == 0) & picked & (slots >= 1) & (slots < words)
        | (labels == 1) & picked & in_regions
        | (labels == 2) & (slots == 0)
    )
    live_count = jnp.sum(live.astype(jnp.int32), 1)
    taken = (live_count + PART - 1) // PART * PART
    base = jnp.concatenate([jnp.zeros((1,), jnp.int32), jnp.cumsum(taken)])
    rank = jnp.cumsum(live.astype(jnp.int32), 1) - 1 + base[:-1, None]
    pos = jnp.where(live, rank, -1).reshape(pairs, 1, seq)
    blocks = jnp.maximum(1, (base[-1:] + LIVE - 1) // LIVE)

    vectors = jnp.stack(
        [query_bias, value_bias, out_bias, attn_gain, attn_shift, back_bias, ffn_gain, ffn_shift]
        + [inner_bias[k * rows : (k + 1) * rows] for k in range(hidden // width)],
        1,
    )
    vectors = jnp.pad(vectors, ((0, 0), (0, 128 - vectors.shape[1])))
    attn_shard = jnp.concatenate([qkv_weight, out_weight, vectors], 1)
    def offsets(size, halves):
        if not cube:
            return jnp.zeros((1,), jnp.int32)
        keys = [0, XBIT, YBIT, XBIT | YBIT] + [XBIT | YBIT] * halves
        keys = jnp.array(keys, jnp.int32) ^ me
        starts = jnp.array([0] * 4 + [size // 2] * halves, jnp.int32)
        return jnp.concatenate([keys * size + starts, (keys ^ CORE) * size + starts])

    attn_offsets, inner_offsets = offsets(rows, 1), offsets(rows, 0)
    back_offsets = offsets(back_weight.shape[0], 0)
    order = jnp.arange(BLOCKS, dtype=jnp.int32)
    if cube:
        order = jnp.array([0, 2, 6, 4, 1, 3, 7, 5], jnp.int32) ^ me
    indices = (base, pos, blocks, attn_offsets, inner_offsets, back_offsets, order)
    if cube:
        attn_x, attn_y = swap(attn_shard, XBIT), swap(attn_shard, YBIT)
        own = [swap(v, CORE) for v in (attn_shard, inner_weight, back_weight)]
        near = lax.optimization_barrier((attn_x, attn_y, inner_weight, indices, *own))
        attn_x, attn_y, inner_weight, indices, *own = near
        attn_far = far_swap(attn_x, attn_y)
        inner_x, inner_y = swap(inner_weight, XBIT), swap(inner_weight, YBIT)
        attn_core = swap(attn_x, CORE), swap(attn_y, CORE)
        attn_far, attn_core, back_weight = lax.optimization_barrier((attn_far, attn_core, back_weight))
        back_x, back_y = swap(back_weight, XBIT), swap(back_weight, YBIT)
        attn = near_and_far(attn_shard, attn_x, attn_y, attn_far)
        attn_core = (own[0],) + attn_core + tuple(swap(v, CORE) for v in attn_far)
        attn = with_core(attn, attn_core)
    else:
        attn, inner, back = (
            [(lax.all_gather(v, "shard", axis=0, tiled=True), 0, 0)]
            for v in (attn_shard, inner_weight, back_weight)
        )
    base, pos, blocks, attn_offsets, inner_offsets, back_offsets, order = indices

    columns = 4 * width + 128
    attn_count = len(attn)
    attn_pieces = [v for v, _, _ in attn]
    qkv, vector_rows, inner_bias_full = pl.pallas_call(
        functools.partial(project_kernel, attn_count, rows),
        grid=grid,
        in_specs=[SCALARS] + [ANYWHERE] * attn_count + [steps(width)],
        out_specs=[steps(3 * width), whole((16, width)), whole((1, hidden))],
        out_shape=[
            shape_of(count, 3 * width),
            shape_of(16, width, dtype=F32),
            shape_of(1, hidden, dtype=F32),
        ],
        scratch_shapes=[
            pltpu.VMEM((width, columns), BF16),
            pltpu.SemaphoreType.DMA((attn_count,)),
        ],
        compiler_params=params(24 * 2**20),
        cost_estimate=cost(9),
        name="project",
    )(attn_offsets, *attn_pieces, tokens)
    if cube:
        inner_x, inner_y, qkv = lax.optimization_barrier((inner_x, inner_y, qkv))
        inner_far = swap(inner_y, XBIT)
        inner_core = swap(inner_x, CORE), swap(inner_y, CORE)
    mixed = pl.pallas_call(
        functools.partial(attend_kernel, seq),
        grid=grid,
        in_specs=[SCALARS] * 2 + [steps(3 * width)],
        out_specs=steps(width),
        out_shape=shape_of(count, width),
        compiler_params=params(24 * 2**20),
        cost_estimate=cost(8),
        name="attend",
    )(word_counts, region_counts, qkv)
    if cube:
        back_x, back_y, inner_core, mixed = lax.optimization_barrier(
            (back_x, back_y, inner_core, mixed)
        )
        back_far = swap(back_x, YBIT)
        back_core = swap(back_x, CORE), swap(back_y, CORE)
    hidden1, compact = pl.pallas_call(
        functools.partial(settle_kernel, attn_count, seq),
        grid=grid,
        in_specs=[SCALARS] * 2
        + [ANYWHERE] * attn_count
        + [steps(width)] * 3
        + [whole((pairs, 1, seq)), whole((16, width))],
        out_specs=[steps(width), whole((cap, columns))],
        out_shape=[shape_of(count, width, dtype=F32), shape_of(cap, columns)],
        scratch_shapes=[
            pltpu.VMEM((width, width), BF16),
            pltpu.SemaphoreType.DMA((attn_count,)),
        ],
        compiler_params=params(30 * 2**20),
        cost_estimate=cost(9),
        name="settle",
    )(attn_offsets, base, *attn_pieces, tokens, cotangent, mixed, pos, vector_rows)

    if cube:
        inner_far, back_far, back_core, hidden1 = lax.optimization_barrier(
            (inner_far, back_far, back_core, hidden1)
        )
        inner = chip_pieces(inner_weight, (inner_x, inner_y, inner_far))
        inner = with_core(inner, (own[1],) + inner_core + (swap(inner_far, CORE),))
    inner_count = len(inner)
    inner_pieces = [v for v, _, _ in inner]
    in_vmem = pl.BlockSpec(memory_space=pltpu.VMEM)
    if cube:
        back = chip_pieces(back_weight, (back_x, back_y, back_far))
        back = with_core(back, (own[2],) + back_core + (swap(back_far, CORE),))
    back_count = len(back)
    back_pieces = [v for v, _, _ in back]

    half = BLOCKS // 2
    size = hidden // BLOCKS
    block = width // BLOCKS
    inner_full, back_full, keep_back, send_back, keep_inner, send_inner, d_hidden1, sums, inner_sum = pl.pallas_call(
        functools.partial(ffn_back_kernel, (inner_count, back_count)),
        in_specs=[SCALARS] * 4 + [ANYWHERE] * (inner_count + back_count + 1) + [in_vmem] * 2,
        out_specs=[ANYWHERE] * 7 + [in_vmem] * 2,
        out_shape=[
            shape_of(width, hidden),
            shape_of(hidden, width),
            shape_of(half, size, width),
            shape_of(half, size, width),
            shape_of(half, size, width),
            shape_of(half, size, width),
            shape_of(cap, width, dtype=F32),
            shape_of(16, width, dtype=F32),
            shape_of(1, hidden, dtype=F32),
        ],
        scratch_shapes=[
            pltpu.VMEM((hidden, width), BF16),
            pltpu.VMEM((width, hidden), BF16),
            pltpu.VMEM((cap, width), BF16),
            pltpu.VMEM((cap, width), BF16),
            pltpu.VMEM((cap, hidden), BF16),
            pltpu.VMEM((cap, hidden), BF16),
            pltpu.VMEM((cap, width), BF16),
            pltpu.VMEM((cap, hidden), BF16),
            pltpu.VMEM((cap, width), F32),
            pltpu.VMEM((width, width), F32),
            pltpu.VMEM((BLOCKS, size, width), BF16),
            pltpu.VMEM((BLOCKS, size, width), BF16),
            pltpu.VMEM((width, LIVE), BF16),
            pltpu.VMEM((cap // LIVE, width, LIVE), BF16),
            pltpu.SemaphoreType.DMA((inner_count,)),
            pltpu.SemaphoreType.DMA((back_count,)),
            pltpu.SemaphoreType.DMA((12 + 2 * hidden // width,)),
        ],
        compiler_params=params(),
        cost_estimate=cost(13),
        name="ffn_back",
    )(
        inner_offsets,
        back_offsets,
        order,
        blocks,
        *inner_pieces,
        *back_pieces,
        compact,
        inner_bias_full,
        vector_rows,
    )

    if cube:
        back_total = Sum(keep_back, send_back)
        inner_total = EarlySum(keep_inner, send_inner)

    d_qkv, d_r1, keep_attn, send_attn = pl.pallas_call(
        functools.partial(attend_back_kernel, attn_count, seq, rows),
        in_specs=[SCALARS] * 6 + [ANYWHERE] * (attn_count + 4) + [in_vmem] * 4,
        out_specs=[ANYWHERE] * 4,
        out_shape=[
            shape_of(count, 3 * width),
            shape_of(cap, width),
            shape_of(half, block, columns),
            shape_of(half, block, columns),
        ],
        scratch_shapes=[
            pltpu.VMEM((width, width), BF16),
            pltpu.VMEM((cap, width), BF16),
            pltpu.VMEM((cap, width), BF16),
            pltpu.VMEM((cap, 128), BF16),
            pltpu.VMEM((cap, width), F32),
            pltpu.VMEM((count, 3 * width), BF16),
            pltpu.VMEM((count, width), BF16),
            pltpu.VMEM((cap, width), BF16),
            pltpu.VMEM((cap, width), BF16),
            pltpu.VMEM((TOGETHER, seq, width), F32),
            pltpu.VMEM((TOGETHER, seq, width), F32),
            pltpu.VMEM((TOGETHER, seq, width), F32),
            pltpu.VMEM((count, 3 * width), BF16),
            pltpu.VMEM((width, width), F32),
            pltpu.VMEM((BLOCKS, block, columns), BF16),
            pltpu.VMEM((16, width), F32),
            pltpu.VMEM((width, count), BF16),
            pltpu.VMEM((width, LIVE), BF16),
            pltpu.VMEM((width, count), BF16),
            pltpu.SemaphoreType.DMA((attn_count,)),
            pltpu.SemaphoreType.DMA((16 + count // STEP,)),
        ],
        compiler_params=params(),
        cost_estimate=cost(22),
        name="attend_back",
    )(
        attn_offsets,
        order,
        base,
        word_counts,
        region_counts,
        blocks,
        *attn_pieces,
        compact,
        d_hidden1,
        qkv,
        tokens,
        vector_rows,
        sums,
        inner_sum,
        pos,
    )

    def later(shift):
        return lambda i: (i + shift, 0)

    def ffn(first, number, x, *done):
        return pl.pallas_call(
            ffn_kernel,
            grid=(number,),
            in_specs=[pl.BlockSpec((STEP, width), later(first)), whole((1, hidden)), whole((16, width))]
            + [in_vmem] * 2
            + [ANYWHERE] * len(done),
            out_specs=pl.BlockSpec((STEP, width), later(first)),
            out_shape=shape_of(count, width),
            input_output_aliases={5: 0} if done else {},
            scratch_shapes=[pltpu.VMEM((STEP, hidden), BF16)],
            compiler_params=params(24 * 2**20),
            cost_estimate=cost(11),
            name="ffn",
        )(x, inner_bias_full, vector_rows, inner_full, back_full, *done)

    x = hidden1
    if cube:
        sent = back_total.near(d_r1)
        sent += inner_total.rep_early(*sent)
        attn_total = Sum(keep_attn, send_attn)
        sent += attn_total.near(*sent)
        x = after(hidden1, *sent)
    result = ffn(0, grid[0] - 2, x)
    if cube:
        sent = back_total.far(result)
        sent += attn_total.far(*sent)
        sent += back_total.rep_first(*sent)
        sent += inner_total.near(*sent)
        sent += attn_total.rep_first(*sent)
        sent += back_total.rep_second(*sent)
        d_qkv = after(d_qkv, *sent)

    input_grad = pl.pallas_call(
        functools.partial(input_grad_kernel, attn_count, seq),
        grid=grid,
        in_specs=[SCALARS] * 2
        + [ANYWHERE] * attn_count
        + [steps(3 * width), whole((cap, width)), whole((pairs, 1, seq))],
        out_specs=steps(width),
        out_shape=shape_of(count, width, dtype=F32),
        scratch_shapes=[
            pltpu.VMEM((width, 3 * width), BF16),
            pltpu.SemaphoreType.DMA((attn_count,)),
        ],
        compiler_params=params(24 * 2**20),
        cost_estimate=cost(9),
        name="input_grad",
    )(attn_offsets, base, *attn_pieces, d_qkv, d_r1, pos)

    if cube:
        sent = attn_total.rep_second(input_grad)
        sent += inner_total.far(*sent)
        sent += back_total.rep_third(*sent)
        x = after(hidden1, *sent)
    result = ffn(grid[0] - 2, 2, x, result)
    if cube:
        sent = inner_total.rep_second(result)

    quarters = hidden // width
    if cube:
        attn_total.rep_third(*sent)
        inner_total.rep_third()
        back_sum, inner_sum, attn_sum = (v.done() for v in (back_total, inner_total, attn_total))
        inner_sum = jnp.concatenate([inner_sum[c * block : (c + 1) * block] for c in range(quarters)], 1)
    else:
        back_grad = jnp.concatenate([keep_back, send_back]).reshape(hidden, width)
        inner_grad = jnp.concatenate([keep_inner, send_inner]).reshape(BLOCKS, quarters, block, width)
        inner_grad = inner_grad.transpose(0, 2, 1, 3).reshape(width, hidden)
        attn_grad = jnp.concatenate([keep_attn, send_attn]).reshape(width, columns)
        back_sum, inner_sum, attn_sum = (
            lax.psum(lax.psum_scatter(g, "shard", scatter_dimension=0, tiled=True), "rep").astype(F32)
            for g in (back_grad, inner_grad, attn_grad)
        )
    sums = attn_sum[:, 4 * width :].T
    return (
        result,
        input_grad,
        attn_sum[:, : 3 * width],
        sums[0],
        sums[1],
        attn_sum[:, 3 * width : 4 * width],
        sums[2],
        sums[3],
        sums[4],
        inner_sum,
        sums[8 : 8 + quarters].reshape(-1),
        back_sum,
        sums[5],
        sums[6],
        sums[7],
    )


def solution(mesh):
    rows, both, one = P(("rep", "shard"), None), P(("rep", "shard")), P("shard")
    matrix = P("shard", None)
    in_specs = (rows, both, both, both, rows, matrix, one, one, matrix, one, one, one)
    in_specs += (matrix, one, matrix, one, one, one, rows)
    out_specs = (rows, rows, matrix, one, one, matrix, one, one, one, matrix, one, matrix)
    out_specs += (one, one, one)
    sizes = dict(mesh.shape)

    def run(*args):
        return local(*args, shards=sizes["shard"], reps=sizes["rep"])

    return jax.shard_map(
        run, mesh=mesh, in_specs=in_specs, out_specs=out_specs, check_vma=False
    )
```
